32 devices in a mesh: dp: 8 (over z, x), row: 2 (over y), col: 2 (over core).
Axes of the slice: x: 2, y: 2, z: 4, core: 2. Of those that a mesh axis runs over, the one named last changes fastest.
Arguments:
- tokens_in: bfloat16 [37824, 768], P('dp', ('row', 'col')), may hold values from -8 to 8
- out_grad: bfloat16 [37824, 768], P('dp', ('row', 'col')), may hold values from -6 to 6
- qkv_weight: float32 [768, 2304], P('row', 'col'), may hold values from -0.21875 to 0.21875
- proj_weight: float32 [768, 768], P('col', 'row'), may hold values from -0.875 to 0.875
- expand_weight: float32 [768, 3072], P('row', 'col'), may hold values from -0.21875 to 0.21875
- contract_weight: float32 [3072, 768], P('col', 'row'), may hold values from -0.15625 to 0.15625
- norm_params: float32 [4, 768], P(None, ('row', 'col')), may hold values from -1 to 1.7
- qkv_first: float32 [768, 2304], P('row', 'col'), may hold values from -64 to 64
- qkv_second: float32 [768, 2304], P('row', 'col'), may hold values from 5.6736 to 90.7776
- proj_first: float32 [768, 768], P('col', 'row'), may hold values from -24 to 24
- proj_second: float32 [768, 768], P('col', 'row'), may hold values from 0.56736 to 9.07776
- expand_first: float32 [768, 3072], P('row', 'col'), may hold values from -64 to 64
- expand_second: float32 [768, 3072], P('row', 'col'), may hold values from 4.16064 to 66.57024
- contract_first: float32 [3072, 768], P('col', 'row'), may hold values from -96 to 96
- contract_second: float32 [3072, 768], P('col', 'row'), may hold values from 9.456 to 151.296
- norm_first: float32 [4, 768], P(None, ('row', 'col')), may hold values from -112 to 112
- norm_second: float32 [4, 768], P(None, ('row', 'col')), may hold values from 15.1296 to 242.0736
Outputs:
- output_tokens: float32 [37824, 768], P('dp', ('row', 'col'))
- input_grad: float32 [37824, 768], P('dp', ('row', 'col'))
- qkv_new: float32 [768, 2304], P('row', 'col')
- qkv_first_new: float32 [768, 2304], P('row', 'col')
- qkv_second_new: float32 [768, 2304], P('row', 'col')
- proj_new: float32 [768, 768], P('col', 'row')
- proj_first_new: float32 [768, 768], P('col', 'row')
- proj_second_new: float32 [768, 768], P('col', 'row')
- expand_new: float32 [768, 3072], P('row', 'col')
- expand_first_new: float32 [768, 3072], P('row', 'col')
- expand_second_new: float32 [768, 3072], P('row', 'col')
- contract_new: float32 [3072, 768], P('col', 'row')
- contract_first_new: float32 [3072, 768], P('col', 'row')
- contract_second_new: float32 [3072, 768], P('col', 'row')
- norm_new: float32 [4, 768], P(None, ('row', 'col'))
- norm_first_new: float32 [4, 768], P(None, ('row', 'col'))
- norm_second_new: float32 [4, 768], P(None, ('row', 'col'))
The draws below stay inside these ranges and needn't reach their ends.
All inputs are finite; a program needn't handle non-finite values.
Results may differ from the reference program's by a relative error of at most 0.012.
Values may be sent and summed in bfloat16 or wider, within the bound.
No kernel may reach another device: no remote copies, remote signals or barrier semaphores. Data moves between devices by JAX's collectives and lax.ppermute only.
A program may use at most 256 MiB of HBM per device.

```python
import math
import jax
import jax.numpy as jnp
from jax import lax

D = 768
HEADS = 12
HEAD_DIM = 64
FF = 3072
SEQ = 197
IMG_DEV = 24
STEP = 10
TOKENS = 37824
N_DP = 8


def draw_tokens_in(key, part):
    key = jax.random.fold_in(key, 11)
    column = jnp.arange(D, dtype=jnp.float32) / (D - 1)
    noise = jnp.clip(jax.random.normal(key, (TOKENS, D), jnp.float32), -4.0, 4.0)
    feature_scale = 0.6 * 3.0 ** column
    return (noise * feature_scale).astype(jnp.bfloat16)


def draw_norm_params(key, part):
    key = jax.random.fold_in(key, 23)
    noise = jnp.clip(jax.random.normal(key, (4, D), jnp.float32), -3.0, 3.0)
    gains = 1.0 + 0.2 * noise
    shifts = 0.3 * noise
    row_index = jnp.arange(4)[:, None]
    return jnp.where(row_index % 2 == 0, gains, shifts).astype(jnp.float32)


def shard_levels(own_key, shape, split, low, top_value):
    level = 1.0
    for axis_at, blocks in split:
        heights = jax.random.uniform(jax.random.fold_in(jax.random.fold_in(own_key, 6), axis_at), (blocks,), jnp.float32, low / len(split), top_value / len(split))
        level = level * jnp.repeat(jnp.exp(heights), shape[axis_at] // blocks).reshape((-1,) + (1,) * (len(shape) - 1 - axis_at))
    return level


def gaussian(own_key, extent, scale, most, shards=(), held_as=jnp.bfloat16):
    entries = jax.random.normal(own_key, extent, jnp.float32) * scale
    if len(shards) > 0:
        entries = shard_levels(own_key, extent, shards, -0.22, 0.18) * entries
    return jnp.clip(entries, min=-most, max=most).astype(held_as)


def setup_inputs(seed: int = 0) -> dict:
    seeds = jax.random.split(jax.random.key(seed), 18)
    tokens_in = draw_tokens_in(jax.random.fold_in(seeds[17], 71), 0)
    out_grad = gaussian(seeds[1], (TOKENS, D), 1.0, 6.0, ((0, 8), (1, 4)))
    qkv_weight = gaussian(seeds[2], (D, 3 * D), D ** -0.5, 0.21875, ((0, 2), (1, 2)), jnp.float32)
    proj_weight = gaussian(seeds[3], (D, D), (D // 16) ** -0.5, 0.875, ((0, 2), (1, 2)), jnp.float32)
    expand_weight = gaussian(seeds[4], (D, FF), D ** -0.5, 0.21875, ((0, 2), (1, 2)), jnp.float32)
    contract_weight = gaussian(seeds[5], (FF, D), (FF // 2) ** -0.5, 0.15625, ((0, 2), (1, 2)), jnp.float32)
    norm_params = draw_norm_params(jax.random.fold_in(seeds[17], 71), 0)
    qkv_first = gaussian(seeds[7], (D, 3 * D), (0.061 * TOKENS ** 0.5), 64.0, ((0, 2), (1, 2)), jnp.float32)
    qkv_second = jnp.clip(jnp.exp(math.log(90.7776) - 2.7725887 * jax.random.uniform(seeds[8], (D, 3 * D), jnp.float32) ** shard_levels(seeds[8], (D, 3 * D), ((0, 2), (1, 2)), -0.2, 0.2)), 5.6736, 90.7776)
    proj_first = gaussian(seeds[9], (D, D), (0.0192 * TOKENS ** 0.5), 24.0, ((0, 2), (1, 2)), jnp.float32)
    proj_second = jnp.clip(jnp.exp(math.log(9.07776) - 2.7725887 * jax.random.uniform(seeds[10], (D, D), jnp.float32) ** shard_levels(seeds[10], (D, D), ((0, 2), (1, 2)), -0.2, 0.2)), 0.56736, 9.07776)
    expand_first = gaussian(seeds[11], (D, FF), (0.052 * TOKENS ** 0.5), 64.0, ((0, 2), (1, 2)), jnp.float32)
    expand_second = jnp.clip(jnp.exp(math.log(66.57024) - 2.7725887 * jax.random.uniform(seeds[12], (D, FF), jnp.float32) ** shard_levels(seeds[12], (D, FF), ((0, 2), (1, 2)), -0.2, 0.2)), 4.16064, 66.57024)
    contract_first = gaussian(seeds[13], (FF, D), (0.0785 * TOKENS ** 0.5), 96.0, ((0, 2), (1, 2)), jnp.float32)
    contract_second = jnp.clip(jnp.exp(math.log(151.296) - 2.7725887 * jax.random.uniform(seeds[14], (FF, D), jnp.float32) ** shard_levels(seeds[14], (FF, D), ((0, 2), (1, 2)), -0.2, 0.2)), 9.456, 151.296)
    norm_first = gaussian(seeds[15], (4, D), (0.0993 * TOKENS ** 0.5), 112.0, ((1, 4),), jnp.float32)
    norm_second = jnp.clip(jnp.exp(math.log(242.0736) - 2.7725887 * jax.random.uniform(seeds[16], (4, D), jnp.float32) ** shard_levels(seeds[16], (4, D), ((1, 4),), -0.2, 0.2)), 15.1296, 242.0736)
    return {"tokens_in": tokens_in, "out_grad": out_grad, "qkv_weight": qkv_weight, "proj_weight": proj_weight, "expand_weight": expand_weight, "contract_weight": contract_weight, "norm_params": norm_params, "qkv_first": qkv_first, "qkv_second": qkv_second, "proj_first": proj_first, "proj_second": proj_second, "expand_first": expand_first, "expand_second": expand_second, "contract_first": contract_first, "contract_second": contract_second, "norm_first": norm_first, "norm_second": norm_second}


norm_epsilon = 1e-06
beta_first = 0.9
beta_second = 0.999
adam_epsilon = 1e-08
rate_matrix = 0.1
rate_norm = 0.5
decay_matrix = 0.05

@jax.custom_vjp
def low(v):
    return lax.optimization_barrier(v.astype(jnp.bfloat16)).astype(jnp.float32)

@jax.custom_vjp
def low_back(v):
    return v

def low_keep(v):
    return (low(v), None)

def low_pass(kept, grad):
    return (grad,)

def back_keep(v):
    return (v, None)

def back_low(kept, grad):
    return (low(grad),)
low.defvjp(low_keep, low_pass)
low_back.defvjp(back_keep, back_low)

def multiply(left, right):
    return jnp.dot(left, right, precision=lax.Precision.HIGHEST, preferred_element_type=jnp.float32)

def layer_norm(values, gain_row, shift_row):
    center = lax.optimization_barrier(jnp.mean(values, axis=-1, keepdims=True))
    spread = lax.optimization_barrier(jnp.mean(values * values, axis=-1, keepdims=True)) - center * center
    return (values - center) * lax.rsqrt(spread + norm_epsilon) * gain_row + shift_row

def attend_image(image_rows):
    queries = image_rows[:, :, 0]
    key_rows = image_rows[:, :, 1]
    value_rows = image_rows[:, :, 2]
    raw_scores = jnp.einsum('qhd,khd->hqk', queries, key_rows, precision=lax.Precision.HIGHEST)
    scores = low_back(raw_scores * HEAD_DIM ** (-0.5))
    attn_probs = jax.nn.softmax(scores, axis=-1)
    mixed_out = jnp.einsum('hqk,khd->qhd', low(attn_probs), value_rows, precision=lax.Precision.HIGHEST)
    return low_back(low(mixed_out))

def block_forward(resid, qkv_weight, proj_weight, expand_weight, contract_weight, norm_params):
    tokens = resid.shape[0]
    images = tokens // SEQ
    h_one = low(layer_norm(resid, norm_params[0], norm_params[1]))
    mixed_qkv = low_back(low(multiply(h_one, low(qkv_weight))))
    grouped = mixed_qkv.reshape(images, SEQ, HEADS, 3, HEAD_DIM)
    attended = lax.map(jax.checkpoint(attend_image), grouped).reshape(tokens, D)
    branch = low_back(multiply(attended, low(proj_weight)))
    middle = resid + branch
    h_two = low(layer_norm(middle, norm_params[2], norm_params[3]))
    hidden_pre = low_back(multiply(h_two, low(expand_weight)))
    hidden = low(jax.nn.gelu(hidden_pre, approximate=False))
    feed = low_back(multiply(hidden, low(contract_weight)))
    return middle + feed

def adamw_update(weight, gradient, first_old, second_old, rate_value, decay_value):
    first_new = beta_first * first_old + (1.0 - beta_first) * gradient
    second_new = beta_second * second_old + (1.0 - beta_second) * (gradient * gradient)
    first_hat = first_new / (1.0 - beta_first ** STEP)
    second_hat = second_new / (1.0 - beta_second ** STEP)
    moved = weight - rate_value * (first_hat / (jnp.sqrt(second_hat) + adam_epsilon) + decay_value * weight)
    return (moved, first_new, second_new)

def reference(tokens_in, out_grad, qkv_weight, proj_weight, expand_weight, contract_weight, norm_params, qkv_first, qkv_second, proj_first, proj_second, expand_first, expand_second, contract_first, contract_second, norm_first, norm_second):
    params = (qkv_weight, proj_weight, expand_weight, contract_weight, norm_params)
    inputs = tokens_in.astype(jnp.float32).reshape(N_DP, IMG_DEV * SEQ, D)
    cotangents = out_grad.astype(jnp.float32).reshape(N_DP, IMG_DEV * SEQ, D)

    def group_step(totals, group_pair):
        outputs, pullback = jax.vjp(block_forward, group_pair[0], params[0], params[1], params[2], params[3], params[4])
        gradients = pullback(group_pair[1])
        summed = tuple((old_total + new_part for old_total, new_part in zip(totals, gradients[1:])))
        return (summed, (outputs, gradients[0]))
    starting = tuple((jnp.zeros(each_param.shape, jnp.float32) for each_param in params))
    summed, (outputs, input_grads) = lax.scan(group_step, starting, (inputs, cotangents))
    qkv_new, qkv_first_new, qkv_second_new = adamw_update(qkv_weight, summed[0], qkv_first, qkv_second, rate_matrix, decay_matrix)
    proj_new, proj_first_new, proj_second_new = adamw_update(proj_weight, summed[1], proj_first, proj_second, rate_matrix, decay_matrix)
    expand_new, expand_first_new, expand_second_new = adamw_update(expand_weight, summed[2], expand_first, expand_second, rate_matrix, decay_matrix)
    contract_new, contract_first_new, contract_second_new = adamw_update(contract_weight, summed[3], contract_first, contract_second, rate_matrix, decay_matrix)
    norm_new, norm_first_new, norm_second_new = adamw_update(norm_params, summed[4], norm_first, norm_second, rate_norm, 0.0)
    output_tokens = outputs.reshape(N_DP * IMG_DEV * SEQ, D)
    input_grad = input_grads.reshape(N_DP * IMG_DEV * SEQ, D)
    return (output_tokens, input_grad, qkv_new, qkv_first_new, qkv_second_new, proj_new, proj_first_new, proj_second_new, expand_new, expand_first_new, expand_second_new, contract_new, contract_first_new, contract_second_new, norm_new, norm_first_new, norm_second_new)
```

```python
import jax
import jax.numpy as jnp
from jax import lax
from jax.experimental import pallas as pl
from jax.experimental.pallas import tpu as pltpu
from jax.sharding import PartitionSpec as P

HEAD_DIM = 64
SEQ = 197
QROWS = 208
KROWS = 256
STEP = 10

norm_epsilon = 1e-06
beta_first = 0.9
beta_second = 0.999
adam_epsilon = 1e-08
rate_matrix = 0.1
rate_norm = 0.5
decay_matrix = 0.05

GROUP = ("row", "col")
bf16 = jnp.bfloat16
f32 = jnp.float32


def dot(left, right, dims=((1,), (0,))):
    return lax.dot_general(left, right, (dims, ((), ())), preferred_element_type=f32)


def swap_halves(block):
    return jnp.concatenate([block[:, HEAD_DIM:], block[:, :HEAD_DIM]], axis=1)


def attend_forward_kernel(mixed_ref, out_ref, probs_ref, wide, gathered):
    tokens = mixed_ref.shape[0]
    images = tokens // SEQ
    wide[tokens - tokens % 8 :, :] = jnp.zeros((wide.shape[0] - tokens + tokens % 8, 384), f32)
    wide[0:tokens, :] = mixed_ref[...].astype(f32)
    low_lane = lax.broadcasted_iota(jnp.int32, (1, 128), 1) < HEAD_DIM
    key_lane = lax.broadcasted_iota(jnp.int32, (1, KROWS), 1) < SEQ
    for image in range(images):
        start = image * SEQ
        block_a = wide[start : start + KROWS, 0:128]
        block_b = wide[start : start + KROWS, 128:256]
        block_c = wide[start : start + KROWS, 256:384]
        scale = HEAD_DIM ** (-0.5)
        query_0 = jnp.where(low_lane, block_a[:QROWS] * scale, 0.0).astype(bf16)
        query_1 = jnp.where(low_lane, 0.0, block_b[:QROWS] * scale).astype(bf16)
        keys_0 = swap_halves(block_a).astype(bf16)
        keys_1 = swap_halves(block_c).astype(bf16)
        outs = []
        for which, (query, keys, values) in enumerate(
            ((query_0, keys_0, block_b), (query_1, keys_1, block_c))
        ):
            scores = jnp.where(key_lane, dot(query, keys, ((1,), (1,))), -1e30)
            exponent = jnp.exp(scores - jnp.max(scores, axis=1, keepdims=True))
            total = jnp.sum(exponent, axis=1, keepdims=True)
            probs = (exponent * (1.0 / total)).astype(bf16)
            probs_ref[0, image * 2 + which] = probs
            outs.append(dot(probs, values.astype(bf16)))
        gathered[start : start + QROWS, :] = jnp.where(low_lane, outs[0], outs[1])
    out_ref[...] = gathered[0:tokens, :].astype(bf16)


def attend_forward(mixed):
    tokens, width = mixed.shape
    images = tokens // SEQ
    pairs = width // 384
    padded = -(-((images - 1) * SEQ + KROWS) // 16) * 16
    return pl.pallas_call(
        attend_forward_kernel,
        grid=(pairs,),
        in_specs=[pl.BlockSpec((tokens, 384), lambda i: (0, i))],
        out_specs=[
            pl.BlockSpec((tokens, 128), lambda i: (0, i)),
            pl.BlockSpec((1, 2 * images, QROWS, KROWS), lambda i: (i, 0, 0, 0)),
        ],
        out_shape=[
            jax.ShapeDtypeStruct((tokens, pairs * 128), bf16),
            jax.ShapeDtypeStruct((pairs, 2 * images, QROWS, KROWS), bf16),
        ],
        scratch_shapes=[pltpu.VMEM((padded, 384), f32), pltpu.VMEM((padded, 128), f32)],
        compiler_params=pltpu.CompilerParams(vmem_limit_bytes=40 * 2**20),
        cost_estimate=pl.CostEstimate(
            flops=pairs * images * 4 * 2 * QROWS * KROWS * 128,
            bytes_accessed=tokens * width * 3,
            transcendentals=pairs * images * 2 * QROWS * KROWS,
        ),
        name="attend_forward",
    )(mixed)


def attend_backward_kernel(mixed_ref, probs_ref, grad_ref, out_ref, wide, grad_wide, gathered):
    tokens = mixed_ref.shape[0]
    images = tokens // SEQ
    wide[tokens - tokens % 8 :, :] = jnp.zeros((wide.shape[0] - tokens + tokens % 8, 384), f32)
    wide[0:tokens, :] = mixed_ref[...].astype(f32)
    grad_wide[0:tokens, :] = grad_ref[...].astype(f32)
    low_lane = lax.broadcasted_iota(jnp.int32, (1, 128), 1) < HEAD_DIM
    query_row = lax.broadcasted_iota(jnp.int32, (QROWS, 128), 0) < SEQ
    scale = HEAD_DIM ** (-0.5)
    for image in range(images):
        start = image * SEQ
        block_a = wide[start : start + KROWS, 0:128]
        block_b = wide[start : start + KROWS, 128:256]
        block_c = wide[start : start + KROWS, 256:384]
        grad = jnp.where(query_row, grad_wide[start : start + QROWS, :], 0.0)
        grad_low = grad.astype(bf16)
        swapped_a = (swap_halves(block_a) * scale).astype(bf16)
        swapped_b = (swap_halves(block_b) * scale).astype(bf16)
        swapped_c = (swap_halves(block_c) * scale).astype(bf16)
        probs_0 = probs_ref[0, 2 * image]
        probs_1 = probs_ref[0, 2 * image + 1]
        grad_v0 = dot(probs_0, grad_low, ((0,), (0,)))
        grad_v1 = dot(probs_1, grad_low, ((0,), (0,)))
        score_grads = []
        for probs, part, values in (
            (probs_0, jnp.where(low_lane, grad, 0.0), block_b),
            (probs_1, jnp.where(low_lane, 0.0, grad), block_c),
        ):
            grad_probs = dot(part.astype(bf16), values.astype(bf16), ((1,), (1,)))
            wide_probs = probs.astype(f32)
            inner = jnp.sum(wide_probs * grad_probs, axis=1, keepdims=True)
            score_grads.append((wide_probs * (grad_probs - inner)).astype(bf16))
        score_0, score_1 = score_grads
        grad_q0 = dot(score_0, swapped_a)
        grad_k0 = dot(score_0, swapped_a[:QROWS], ((0,), (0,)))
        grad_q1 = dot(score_1, swapped_c)
        grad_k1 = dot(score_1, swapped_b[:QROWS], ((0,), (0,)))
        rows = slice(start, start + QROWS)
        gathered[rows, 0:128] = jnp.where(low_lane, grad_q0, grad_k0[:QROWS])
        gathered[rows, 128:256] = jnp.where(low_lane, grad_v0[:QROWS], grad_q1)
        gathered[rows, 256:384] = jnp.where(low_lane, grad_k1[:QROWS], grad_v1[:QROWS])
    out_ref[...] = gathered[0:tokens, :].astype(bf16)


def attend_backward(mixed, probs, grad_attended):
    tokens, width = mixed.shape
    images = tokens // SEQ
    pairs = width // 384
    padded = -(-((images - 1) * SEQ + KROWS) // 16) * 16
    return pl.pallas_call(
        attend_backward_kernel,
        grid=(pairs,),
        in_specs=[
            pl.BlockSpec((tokens, 384), lambda i: (0, i)),
            pl.BlockSpec((1, 2 * images, QROWS, KROWS), lambda i: (i, 0, 0, 0)),
            pl.BlockSpec((tokens, 128), lambda i: (0, i)),
        ],
        out_specs=pl.BlockSpec((tokens, 384), lambda i: (0, i)),
        out_shape=jax.ShapeDtypeStruct((tokens, width), bf16),
        scratch_shapes=[
            pltpu.VMEM((padded, 384), f32),
            pltpu.VMEM((padded, 128), f32),
            pltpu.VMEM((padded, 384), f32),
        ],
        compiler_params=pltpu.CompilerParams(vmem_limit_bytes=40 * 2**20),
        cost_estimate=pl.CostEstimate(
            flops=pairs * images * 8 * 2 * QROWS * KROWS * 128,
            bytes_accessed=tokens * width * 4,
            transcendentals=0,
        ),
        name="attend_backward",
    )(mixed, probs, grad_attended)


def gelu_and_slope(value):
    size = jnp.abs(value)
    density = jnp.exp(value * value * -0.5)
    t = 1.0 / (1.0 + (0.3275911 * 0.5**0.5) * size)
    series = t * (
        0.254829592
        + t * (-0.284496736 + t * (1.421413741 + t * (-1.453152027 + t * 1.061405429)))
    )
    tail = 0.5 * series * density
    phi = jnp.where(value >= 0, 1.0 - tail, tail)
    return (value * phi, phi + value * density * 0.3989422804014327)


def norm_forward(values, gain_row, shift_row):
    center = jnp.mean(values, axis=1, keepdims=True)
    spread = jnp.mean(values * values, axis=1, keepdims=True) - center * center
    scaled = lax.rsqrt(spread + norm_epsilon)
    normed = (values - center) * scaled
    return ((normed * gain_row + shift_row).astype(bf16), normed, scaled)


def norm_backward(grad_normed, normed, scaled, gain_row):
    local_grad = grad_normed * gain_row
    first = jnp.mean(local_grad, axis=1, keepdims=True)
    second = jnp.mean(local_grad * normed, axis=1, keepdims=True)
    grad_values = scaled * (local_grad - first - normed * second)
    return (grad_values, jnp.sum(grad_normed * normed, axis=0), jnp.sum(grad_normed, axis=0))


def adamw_update(weight, gradient, first_old, second_old, rate_value, decay_value):
    first_new = beta_first * first_old + (1.0 - beta_first) * gradient
    second_new = beta_second * second_old + (1.0 - beta_second) * (gradient * gradient)
    first_hat = first_new / (1.0 - beta_first**STEP)
    second_hat = second_new / (1.0 - beta_second**STEP)
    moved = weight - rate_value * (
        first_hat / (jnp.sqrt(second_hat) + adam_epsilon) + decay_value * weight
    )
    return (moved, first_new, second_new)


def local(
    tokens_in,
    out_grad,
    qkv_weight,
    proj_weight,
    expand_weight,
    contract_weight,
    norm_params,
    qkv_first,
    qkv_second,
    proj_first,
    proj_second,
    expand_first,
    expand_second,
    contract_first,
    contract_second,
    norm_first,
    norm_second,
):
    row = lax.axis_index("row")
    col = lax.axis_index("col")
    me = 2 * row + col
    tokens = tokens_in.shape[0] // 4
    part = tokens_in.shape[1]

    def swap(array, distance):
        if distance == 0:
            return array
        return lax.ppermute(array, GROUP, [(i, i ^ distance) for i in range(4)])

    def swap_row(array):
        return swap(array, 2)

    def swap_col(array):
        return swap(array, 1)

    def in_order(first, second):
        return jnp.where(col == 0, jnp.concatenate([first, second], -1), jnp.concatenate([second, first], -1))

    def join_features(parts):
        return jnp.concatenate([in_order(parts[0], parts[1]), in_order(parts[2], parts[3])], -1)

    def tokens_together(array):
        blocks = [
            lax.dynamic_slice(array, ((me ^ d) * tokens, 0), (tokens, part)) for d in range(4)
        ]
        return join_features([swap(block, d) for d, block in enumerate(blocks)])

    def split_features(array):
        quarters = [array[..., i * part : (i + 1) * part] for i in range(4)]
        own = [jnp.where(col == 0, quarters[2 * i], quarters[2 * i + 1]) for i in range(2)]
        other = [jnp.where(col == 0, quarters[2 * i + 1], quarters[2 * i]) for i in range(2)]
        return [own[0], other[0], own[1], other[1]]

    def features_together(array):
        pieces = split_features(array)
        result = jnp.zeros((4 * tokens, part), f32)
        for d in range(4):
            received = swap(pieces[d].astype(bf16), d).astype(f32)
            result = lax.dynamic_update_slice(result, received, ((me ^ d) * tokens, 0))
        return result

    def gather_row_col(weight):
        mine = weight.astype(bf16)
        stacked = jnp.concatenate([mine, swap_row(mine)], axis=0)
        return jnp.concatenate([stacked, swap_col(stacked)], axis=1)

    def gather_col_row(weight):
        mine = weight.astype(bf16)
        stacked = jnp.concatenate([mine, swap_row(mine)], axis=1)
        return jnp.concatenate([stacked, swap_col(stacked)], axis=0)

    def reduce_row_col(left, right):
        half = right.shape[1] // 2
        rows = left.shape[1] // 2
        away = dot(left, right[:, half:], ((0,), (0,))).astype(bf16)
        kept = dot(left, right[:, :half], ((0,), (0,)))
        total = kept + swap_col(away).astype(f32)
        return total[:rows] + swap_row(total[rows:].astype(bf16)).astype(f32)

    def reduce_col_row(left, right):
        half = left.shape[1] // 2
        columns = right.shape[1] // 2
        away = dot(left[:, half:], right, ((0,), (0,))).astype(bf16)
        kept = dot(left[:, :half], right, ((0,), (0,)))
        total = kept + swap_col(away).astype(f32)
        return total[:, :columns] + swap_row(total[:, columns:].astype(bf16)).astype(f32)

    resid_low = tokens_together(tokens_in)
    params = join_features([swap(norm_params, d) for d in range(4)])
    qkv_low = gather_row_col(qkv_weight)
    proj_low = gather_col_row(proj_weight)
    expand_low = gather_row_col(expand_weight)
    contract_low = gather_col_row(contract_weight)
    grad_low = tokens_together(out_grad)

    resid = resid_low.astype(f32)
    h_one, normed_one, scaled_one = norm_forward(resid, params[0], params[1])
    mixed = dot(h_one, qkv_low).astype(bf16)
    attended, probs = attend_forward(mixed)
    middle = resid + dot(attended, proj_low)
    h_two, normed_two, scaled_two = norm_forward(middle, params[2], params[3])
    gelu_value, gelu_slope = gelu_and_slope(dot(h_two, expand_low))
    hidden = gelu_value.astype(bf16)
    gelu_slope = gelu_slope.astype(bf16)
    output_tokens = features_together(middle + dot(hidden, contract_low))

    contract_grad = reduce_col_row(hidden, grad_low)
    grad_pre = (dot(grad_low, contract_low, ((1,), (1,))) * gelu_slope.astype(f32)).astype(bf16)
    expand_grad = reduce_row_col(h_two, grad_pre)
    grad_two = dot(grad_pre, expand_low, ((1,), (1,)))
    middle_part, gain_two, shift_two = norm_backward(grad_two, normed_two, scaled_two, params[2])
    grad_middle = grad_low.astype(f32) + middle_part
    grad_branch = grad_middle.astype(bf16)
    proj_grad = reduce_col_row(attended, grad_branch)
    grad_attended = dot(grad_branch, proj_low, ((1,), (1,))).astype(bf16)
    grad_mixed = attend_backward(mixed, probs, grad_attended)
    qkv_grad = reduce_row_col(h_one, grad_mixed)
    grad_one = dot(grad_mixed, qkv_low, ((1,), (1,)))
    input_part, gain_one, shift_one = norm_backward(grad_one, normed_one, scaled_one, params[0])
    input_grad = features_together(grad_middle + input_part)

    def over_dp(gradient, after):
        gradient = gradient.astype(bf16)
        if after is not None:
            gradient, after = lax.optimization_barrier((gradient, after))
        return lax.psum(gradient, "dp")

    contract_sum = over_dp(contract_grad, None)
    expand_sum = over_dp(expand_grad, contract_sum)
    proj_sum = over_dp(proj_grad, expand_sum)
    qkv_sum = over_dp(qkv_grad, proj_sum)
    norm_parts = jnp.stack(
        split_features(jnp.stack((gain_one, shift_one, gain_two, shift_two)))
    )
    norm_mine = norm_parts[0] + sum(swap(norm_parts[d], d) for d in range(1, 4))
    norm_sum = lax.psum(norm_mine, "dp")

    results = (output_tokens, input_grad)
    for weight, gradient, first, second in (
        (qkv_weight, qkv_sum, qkv_first, qkv_second),
        (proj_weight, proj_sum, proj_first, proj_second),
        (expand_weight, expand_sum, expand_first, expand_second),
        (contract_weight, contract_sum, contract_first, contract_second),
    ):
        results += adamw_update(
            weight, gradient.astype(f32), first, second, rate_matrix, decay_matrix
        )
    return results + adamw_update(norm_params, norm_sum, norm_first, norm_second, rate_norm, 0.0)


def solution(mesh):
    tokens = P("dp", ("row", "col"))
    one = P("row", "col")
    two = P("col", "row")
    norm = P(None, ("row", "col"))
    in_specs = (tokens, tokens, one, two, one, two, norm)
    in_specs += (one, one, two, two, one, one, two, two, norm, norm)
    out_specs = (tokens, tokens) + (one,) * 3 + (two,) * 3 + (one,) * 3 + (two,) * 3 + (norm,) * 3
    return jax.shard_map(local, mesh=mesh, in_specs=in_specs, out_specs=out_specs, check_vma=False)
```

```python
import jax
import jax.numpy as jnp
from jax import lax
from jax.experimental import pallas as pl
from jax.experimental.pallas import tpu as pltpu
from jax.sharding import PartitionSpec as P

HEAD_DIM = 64
SEQ = 197
QROWS = 208
KROWS = 256
STEP = 10
ROWS = 400
CHUNK = 512

norm_epsilon = 1e-06
beta_first = 0.9
beta_second = 0.999
adam_epsilon = 1e-08
rate_matrix = 0.1
rate_norm = 0.5
decay_matrix = 0.05

GROUP = ("row", "col")
bf16 = jnp.bfloat16
f32 = jnp.float32


def dot(left, right, dims=((1,), (0,))):
    return lax.dot_general(left, right, (dims, ((), ())), preferred_element_type=f32)


def swap_halves(block):
    return jnp.concatenate([block[:, HEAD_DIM:], block[:, :HEAD_DIM]], axis=1)


def attend_forward_kernel(mixed_ref, out_ref, probs_ref, wide, gathered):
    rows = mixed_ref.shape[0]
    images = rows // SEQ
    tokens = images * SEQ
    wide[rows:, :] = jnp.zeros((wide.shape[0] - rows, 384), f32)
    wide[0:rows, :] = mixed_ref[...].astype(f32)
    low_lane = lax.broadcasted_iota(jnp.int32, (1, 128), 1) < HEAD_DIM
    key_lane = lax.broadcasted_iota(jnp.int32, (1, KROWS), 1) < SEQ
    for image in range(images):
        start = image * SEQ
        block_a = wide[start : start + KROWS, 0:128]
        block_b = wide[start : start + KROWS, 128:256]
        block_c = wide[start : start + KROWS, 256:384]
        scale = HEAD_DIM ** (-0.5)
        query_0 = jnp.where(low_lane, block_a[:QROWS] * scale, 0.0).astype(bf16)
        query_1 = jnp.where(low_lane, 0.0, block_b[:QROWS] * scale).astype(bf16)
        keys_0 = swap_halves(block_a).astype(bf16)
        keys_1 = swap_halves(block_c).astype(bf16)
        outs = []
        for which, (query, keys, values) in enumerate(
            ((query_0, keys_0, block_b), (query_1, keys_1, block_c))
        ):
            scores = jnp.where(key_lane, dot(query, keys, ((1,), (1,))), -1e30)
            exponent = jnp.exp(scores - jnp.max(scores, axis=1, keepdims=True))
            total = jnp.sum(exponent, axis=1, keepdims=True)
            probs = (exponent * (1.0 / total)).astype(bf16)
            probs_ref[0, image * 2 + which] = probs
            outs.append(dot(probs, values.astype(bf16)))
        gathered[start : start + QROWS, :] = jnp.where(low_lane, outs[0], outs[1])
    gathered[tokens:, :] = jnp.zeros((gathered.shape[0] - tokens, 128), f32)
    out_ref[...] = gathered[0:rows, :].astype(bf16)


def attend_forward(mixed):
    tokens, width = mixed.shape
    images = tokens // SEQ
    pairs = width // 384
    padded = -(-((images - 1) * SEQ + KROWS) // 16) * 16
    return pl.pallas_call(
        attend_forward_kernel,
        grid=(pairs,),
        in_specs=[pl.BlockSpec((tokens, 384), lambda i: (0, i))],
        out_specs=[
            pl.BlockSpec((tokens, 128), lambda i: (0, i)),
            pl.BlockSpec((1, 2 * images, QROWS, KROWS), lambda i: (i, 0, 0, 0)),
        ],
        out_shape=[
            jax.ShapeDtypeStruct((tokens, pairs * 128), bf16),
            jax.ShapeDtypeStruct((pairs, 2 * images, QROWS, KROWS), bf16),
        ],
        scratch_shapes=[pltpu.VMEM((padded, 384), f32), pltpu.VMEM((padded, 128), f32)],
        compiler_params=pltpu.CompilerParams(vmem_limit_bytes=40 * 2**20),
        cost_estimate=pl.CostEstimate(
            flops=pairs * images * 4 * 2 * QROWS * KROWS * 128,
            bytes_accessed=tokens * width * 3,
            transcendentals=pairs * images * 2 * QROWS * KROWS,
        ),
        name="attend_forward",
    )(mixed)


def attend_backward_kernel(mixed_ref, probs_ref, grad_ref, out_ref, wide, grad_wide, gathered):
    token_rows = mixed_ref.shape[0]
    images = token_rows // SEQ
    tokens = images * SEQ
    wide[token_rows:, :] = jnp.zeros((wide.shape[0] - token_rows, 384), f32)
    wide[0:token_rows, :] = mixed_ref[...].astype(f32)
    grad_wide[0:token_rows, :] = grad_ref[...].astype(f32)
    low_lane = lax.broadcasted_iota(jnp.int32, (1, 128), 1) < HEAD_DIM
    query_row = lax.broadcasted_iota(jnp.int32, (QROWS, 128), 0) < SEQ
    scale = HEAD_DIM ** (-0.5)
    for image in range(images):
        start = image * SEQ
        block_a = wide[start : start + KROWS, 0:128]
        block_b = wide[start : start + KROWS, 128:256]
        block_c = wide[start : start + KROWS, 256:384]
        grad = jnp.where(query_row, grad_wide[start : start + QROWS, :], 0.0)
        grad_low = grad.astype(bf16)
        swapped_a = (swap_halves(block_a) * scale).astype(bf16)
        swapped_b = (swap_halves(block_b) * scale).astype(bf16)
        swapped_c = (swap_halves(block_c) * scale).astype(bf16)
        probs_0 = probs_ref[0, 2 * image]
        probs_1 = probs_ref[0, 2 * image + 1]
        grad_v0 = dot(probs_0, grad_low, ((0,), (0,)))
        grad_v1 = dot(probs_1, grad_low, ((0,), (0,)))
        score_grads = []
        for probs, part, values in (
            (probs_0, jnp.where(low_lane, grad, 0.0), block_b),
            (probs_1, jnp.where(low_lane, 0.0, grad), block_c),
        ):
            grad_probs = dot(part.astype(bf16), values.astype(bf16), ((1,), (1,)))
            wide_probs = probs.astype(f32)
            inner = jnp.sum(wide_probs * grad_probs, axis=1, keepdims=True)
            score_grads.append((wide_probs * (grad_probs - inner)).astype(bf16))
        score_0, score_1 = score_grads
        grad_q0 = dot(score_0, swapped_a)
        grad_k0 = dot(score_0, swapped_a[:QROWS], ((0,), (0,)))
        grad_q1 = dot(score_1, swapped_c)
        grad_k1 = dot(score_1, swapped_b[:QROWS], ((0,), (0,)))
        rows = slice(start, start + QROWS)
        gathered[rows, 0:128] = jnp.where(low_lane, grad_q0, grad_k0[:QROWS])
        gathered[rows, 128:256] = jnp.where(low_lane, grad_v0[:QROWS], grad_q1)
        gathered[rows, 256:384] = jnp.where(low_lane, grad_k1[:QROWS], grad_v1[:QROWS])
    gathered[tokens:, :] = jnp.zeros((gathered.shape[0] - tokens, 384), f32)
    out_ref[...] = gathered[0:token_rows, :].astype(bf16)


def attend_backward(mixed, probs, grad_attended):
    tokens, width = mixed.shape
    images = tokens // SEQ
    pairs = width // 384
    padded = -(-((images - 1) * SEQ + KROWS) // 16) * 16
    return pl.pallas_call(
        attend_backward_kernel,
        grid=(pairs,),
        in_specs=[
            pl.BlockSpec((tokens, 384), lambda i: (0, i)),
            pl.BlockSpec((1, 2 * images, QROWS, KROWS), lambda i: (i, 0, 0, 0)),
            pl.BlockSpec((tokens, 128), lambda i: (0, i)),
        ],
        out_specs=pl.BlockSpec((tokens, 384), lambda i: (0, i)),
        out_shape=jax.ShapeDtypeStruct((tokens, width), bf16),
        scratch_shapes=[
            pltpu.VMEM((padded, 384), f32),
            pltpu.VMEM((padded, 128), f32),
            pltpu.VMEM((padded, 384), f32),
        ],
        compiler_params=pltpu.CompilerParams(vmem_limit_bytes=40 * 2**20),
        cost_estimate=pl.CostEstimate(
            flops=pairs * images * 8 * 2 * QROWS * KROWS * 128,
            bytes_accessed=tokens * width * 4,
            transcendentals=0,
        ),
        name="attend_backward",
    )(mixed, probs, grad_attended)


def gelu_and_slope(value):
    size = jnp.abs(value)
    density = jnp.exp(value * value * -0.5)
    t = 1.0 / (1.0 + (0.3275911 * 0.5**0.5) * size)
    series = t * (
        0.254829592
        + t * (-0.284496736 + t * (1.421413741 + t * (-1.453152027 + t * 1.061405429)))
    )
    tail = 0.5 * series * density
    phi = jnp.where(value >= 0, 1.0 - tail, tail)
    return (value * phi, phi + value * density * 0.3989422804014327)


def adamw_update(weight, gradient, first_old, second_old, rate_value, decay_value):
    first_new = beta_first * first_old + (1.0 - beta_first) * gradient
    second_new = beta_second * second_old + (1.0 - beta_second) * (gradient * gradient)
    first_hat = first_new / (1.0 - beta_first**STEP)
    second_hat = second_new / (1.0 - beta_second**STEP)
    moved = weight - rate_value * (
        first_hat / (jnp.sqrt(second_hat) + adam_epsilon) + decay_value * weight
    )
    return (moved, first_new, second_new)


def norm_rows(values):
    center = jnp.mean(values, axis=1, keepdims=True)
    spread = jnp.mean(values * values, axis=1, keepdims=True) - center * center
    scaled = lax.rsqrt(spread + norm_epsilon)
    return ((values - center) * scaled, scaled)


def norm_backward(grad_normed, normed, scaled, gain_row):
    local_grad = grad_normed * gain_row
    first = jnp.mean(local_grad, axis=1, keepdims=True)
    second = jnp.mean(local_grad * normed, axis=1, keepdims=True)
    return scaled * (local_grad - first - normed * second)


def square(refs, rows, columns):
    return jnp.concatenate(
        [
            jnp.concatenate([refs[0][rows, columns], refs[2][rows, columns]], axis=1),
            jnp.concatenate([refs[1][rows, columns], refs[3][rows, columns]], axis=1),
        ],
        axis=0,
    )


def in_order(col, first, second):
    return jnp.where(
        col == 0,
        jnp.concatenate([first, second], axis=-1),
        jnp.concatenate([second, first], axis=-1),
    )


def split_features(col, array):
    part = array.shape[-1] // 4
    quarters = [array[..., i * part : (i + 1) * part] for i in range(4)]
    own = [jnp.where(col == 0, quarters[2 * i], quarters[2 * i + 1]) for i in range(2)]
    other = [jnp.where(col == 0, quarters[2 * i + 1], quarters[2 * i]) for i in range(2)]
    return [own[0], other[0], own[1], other[1]]


def row_block(rows, width):
    return pl.BlockSpec((rows, width), lambda i, *_: (i, 0))


def resident(array):
    zeros = (0,) * array.ndim
    return pl.BlockSpec(array.shape, lambda i, *_: zeros)


def row_call(kernel, place, tokens, by_row, whole, by_row_out, whole_out, flops, exps, name):
    steps = -(-tokens // ROWS)
    out_specs = [row_block(ROWS, shape.shape[1]) for shape in by_row_out]
    out_specs += [resident(shape) for shape in whole_out]
    size = sum(a.size * a.dtype.itemsize for a in [*by_row, *whole, *by_row_out, *whole_out])
    return pl.pallas_call(
        kernel,
        grid_spec=pltpu.PrefetchScalarGridSpec(
            num_scalar_prefetch=1,
            grid=(steps,),
            in_specs=[row_block(ROWS, a.shape[1]) for a in by_row] + [resident(a) for a in whole],
            out_specs=out_specs,
        ),
        out_shape=[*by_row_out, *whole_out],
        compiler_params=pltpu.CompilerParams(vmem_limit_bytes=54 * 2**20),
        cost_estimate=pl.CostEstimate(flops=flops, bytes_accessed=size, transcendentals=exps),
        name=name,
    )(place, *by_row, *whole)


def qkv_kernel(tokens, place, *refs):
    parts, params, weights = refs[:4], refs[4], refs[5:9]
    resid_ref, h_ref, mixed_ref = refs[9:]
    col = place[0]
    row = lax.broadcasted_iota(jnp.int32, (ROWS, 1), 0) + pl.program_id(0) * ROWS
    half = [in_order(col, parts[2 * i][...].astype(f32), parts[2 * i + 1][...].astype(f32)) for i in range(2)]
    resid = jnp.where(row < tokens, jnp.concatenate(half, axis=1), 0.0)
    resid_ref[...] = resid.astype(bf16)
    normed, _ = norm_rows(resid)
    h = (normed * params[0:1, :] + params[1:2, :]).astype(bf16)
    h_ref[...] = h
    width = weights[0].shape[1]
    for side in range(2):
        for start in range(0, width, 384):
            columns = slice(start, start + 384)
            block = jnp.concatenate(
                [weights[2 * side][:, columns], weights[2 * side + 1][:, columns]], axis=0
            )
            at = side * width + start
            mixed_ref[:, at : at + 384] = dot(h, block).astype(bf16)


def qkv_forward(place, parts, params, weights):
    tokens = parts[0].shape[0]
    padded = -(-tokens // ROWS) * ROWS
    width, mixed_width = 4 * parts[0].shape[1], 2 * weights[0].shape[1]
    return row_call(
        lambda *refs: qkv_kernel(tokens, *refs),
        place,
        tokens,
        parts,
        [params, *weights],
        [jax.ShapeDtypeStruct((padded, w), bf16) for w in (width, width, mixed_width)],
        [],
        2 * padded * width * mixed_width,
        0,
        "norm_qkv",
    )


def block_kernel(place, *refs):
    resid_ref, attended_ref, grad_ref, params = refs[:4]
    proj, expand, contract = refs[4:8], refs[8:12], refs[12:16]
    out_parts = refs[16:20]
    h_ref, hidden_ref, pre_ref, middle_ref, branch_ref, attended_grad_ref, sums_ref = refs[20:]
    col = place[0]
    whole = slice(None)
    proj_low = square([proj[0], proj[2], proj[1], proj[3]], whole, whole)
    middle = resid_ref[...].astype(f32) + dot(attended_ref[...], proj_low)
    normed, scaled = norm_rows(middle)
    h = (normed * params[2:3, :] + params[3:4, :]).astype(bf16)
    h_ref[...] = h
    grad = grad_ref[...]
    half = expand[0].shape[1]
    output = middle
    grad_two = jnp.zeros_like(middle)
    for side in range(2):
        for start in range(0, half, CHUNK):
            chunk = slice(start, start + CHUNK)
            expand_low = jnp.concatenate(
                [expand[2 * side][:, chunk], expand[2 * side + 1][:, chunk]], axis=0
            )
            contract_low = jnp.concatenate(
                [contract[2 * side][chunk, :], contract[2 * side + 1][chunk, :]], axis=1
            )
            value, slope = gelu_and_slope(dot(h, expand_low))
            hidden = value.astype(bf16)
            grad_pre = (dot(grad, contract_low, ((1,), (1,))) * slope).astype(bf16)
            at = side * half + start
            hidden_ref[:, at : at + CHUNK] = hidden
            pre_ref[:, at : at + CHUNK] = grad_pre
            output = output + dot(hidden, contract_low)
            grad_two = grad_two + dot(grad_pre, expand_low, ((1,), (1,)))
    for part_ref, part in zip(out_parts, split_features(col, output)):
        part_ref[...] = part.astype(bf16)
    grad_middle = grad.astype(f32) + norm_backward(grad_two, normed, scaled, params[2:3, :])
    middle_ref[...] = grad_middle
    branch = grad_middle.astype(bf16)
    branch_ref[...] = branch
    attended_grad_ref[...] = dot(branch, proj_low, ((1,), (1,))).astype(bf16)

    @pl.when(pl.program_id(0) == 0)
    def _():
        sums_ref[...] = jnp.zeros_like(sums_ref)

    sums_ref[0:1, :] += jnp.sum(grad_two * normed, axis=0, keepdims=True)
    sums_ref[1:2, :] += jnp.sum(grad_two, axis=0, keepdims=True)


def block_middle(place, tokens, resid, attended, grad, params, proj, expand, contract):
    padded, width = resid.shape
    ff = 2 * expand[0].shape[1]
    part = jax.ShapeDtypeStruct((tokens, width // 4), bf16)
    narrow = jax.ShapeDtypeStruct((padded, width), bf16)
    broad = jax.ShapeDtypeStruct((padded, ff), bf16)
    return row_call(
        block_kernel,
        place,
        padded,
        [resid, attended, grad],
        [params, *proj, *expand, *contract],
        [part] * 4
        + [narrow, broad, broad, jax.ShapeDtypeStruct((padded, width), f32), narrow, narrow],
        [jax.ShapeDtypeStruct((2, width), f32)],
        2 * padded * width * (4 * ff + 2 * width),
        padded * ff,
        "block_middle",
    )


def input_kernel(place, *refs):
    mixed_ref, middle_ref, resid_ref, params = refs[:4]
    weights = refs[4:8]
    out_parts, sums_ref = refs[8:12], refs[12]
    col = place[0]
    width = weights[0].shape[1]
    grad_one = None
    for side in range(2):
        weight = jnp.concatenate([weights[2 * side][...], weights[2 * side + 1][...]], axis=0)
        piece = dot(mixed_ref[:, side * width : (side + 1) * width], weight, ((1,), (1,)))
        grad_one = piece if grad_one is None else grad_one + piece
    normed, scaled = norm_rows(resid_ref[...].astype(f32))
    result = middle_ref[...] + norm_backward(grad_one, normed, scaled, params[0:1, :])
    for part_ref, part in zip(out_parts, split_features(col, result)):
        part_ref[...] = part.astype(bf16)

    @pl.when(pl.program_id(0) == 0)
    def _():
        sums_ref[...] = jnp.zeros_like(sums_ref)

    sums_ref[0:1, :] += jnp.sum(grad_one * normed, axis=0, keepdims=True)
    sums_ref[1:2, :] += jnp.sum(grad_one, axis=0, keepdims=True)


def input_backward(place, tokens, grad_mixed, grad_middle, resid, params, weights):
    padded, width = resid.shape
    part = jax.ShapeDtypeStruct((tokens, width // 4), bf16)
    return row_call(
        input_kernel,
        place,
        padded,
        [grad_mixed, grad_middle, resid],
        [params, *weights],
        [part] * 4,
        [jax.ShapeDtypeStruct((2, width), f32)],
        2 * padded * width * grad_mixed.shape[1],
        0,
        "qkv_backward",
    )


def tokens_kernel(place, *refs):
    parts, out_ref = refs[:4], refs[4]
    tokens = parts[0].shape[0]
    for block in range(4):
        for distance in range(4):

            @pl.when((place[1] ^ block) == distance)
            def _():
                rows = slice(block * tokens, (block + 1) * tokens)
                out_ref[rows, :] = parts[distance][...].astype(f32)


def tokens_apart(place, parts):
    tokens, part = parts[0].shape
    return pl.pallas_call(
        tokens_kernel,
        in_specs=[pl.BlockSpec(memory_space=pltpu.SMEM)]
        + [pl.BlockSpec(memory_space=pltpu.VMEM)] * 4,
        out_specs=pl.BlockSpec(memory_space=pltpu.VMEM),
        out_shape=jax.ShapeDtypeStruct((4 * tokens, part), f32),
        compiler_params=pltpu.CompilerParams(vmem_limit_bytes=40 * 2**20),
        cost_estimate=pl.CostEstimate(
            flops=0, bytes_accessed=4 * tokens * part * 6, transcendentals=0
        ),
        name="tokens_apart",
    )(place, *parts)


def adamw_kernel(place, weight, first, second, here, there, weight_out, first_out, second_out):
    x = place[2]
    mine = jnp.where(pl.program_id(0) // 4 == x, here[0].astype(f32), there[0].astype(f32))
    results = adamw_update(
        weight[...], mine, first[...], second[...], rate_matrix, decay_matrix
    )
    weight_out[...], first_out[...], second_out[...] = results


def adamw_pieces(place, weight, first, second, here, there):
    rows, width = weight.shape
    piece = pl.BlockSpec((rows // 8, width), lambda i, place: (i, 0))
    part = pl.BlockSpec((1, rows // 8, width), lambda i, place: ((i % 4) ^ place[3], 0, 0))
    return pl.pallas_call(
        adamw_kernel,
        grid_spec=pltpu.PrefetchScalarGridSpec(
            num_scalar_prefetch=1,
            grid=(8,),
            in_specs=[piece, piece, piece, part, part],
            out_specs=[piece] * 3,
        ),
        out_shape=[jax.ShapeDtypeStruct((rows, width), f32)] * 3,
        compiler_params=pltpu.CompilerParams(vmem_limit_bytes=40 * 2**20),
        cost_estimate=pl.CostEstimate(
            flops=20 * rows * width, bytes_accessed=28 * rows * width, transcendentals=0
        ),
        name="adamw_pieces",
    )(place, weight, first, second, here, there)


def local(
    tokens_in,
    out_grad,
    qkv_weight,
    proj_weight,
    expand_weight,
    contract_weight,
    norm_params,
    qkv_first,
    qkv_second,
    proj_first,
    proj_second,
    expand_first,
    expand_second,
    contract_first,
    contract_second,
    norm_first,
    norm_second,
):
    row = lax.axis_index("row")
    col = lax.axis_index("col")
    dp = lax.axis_index("dp")
    n_dp = lax.axis_size("dp")
    me = 2 * row + col
    place = jnp.stack([col, me, dp % 2, dp // 2]).astype(jnp.int32)
    tokens = tokens_in.shape[0] // 4
    part = tokens_in.shape[1]
    padded = -(-tokens // ROWS) * ROWS

    def swap(array, distance):
        if distance == 0:
            return array
        return lax.ppermute(array, GROUP, [(i, i ^ distance) for i in range(4)])

    def swap_dp(array, distance):
        return lax.ppermute(array, "dp", [(i, i ^ distance) for i in range(n_dp)])

    def swap_row(array):
        return swap(array, 2)

    def swap_col(array):
        return swap(array, 1)

    def token_blocks(array):
        return [lax.dynamic_slice(array, ((me ^ d) * tokens, 0), (tokens, part)) for d in range(4)]

    def swap_all(blocks):
        return [swap(block, d) for d, block in enumerate(blocks)]

    def row_partner(mine, weight):
        rows = weight.shape[0] // n_dp
        piece = lax.dynamic_slice(weight, (dp * rows, 0), (rows, weight.shape[1]))
        return lax.all_gather(swap_row(piece.astype(bf16)), "dp", axis=0, tiled=True)

    def reduce_row_col(left, right):
        half = right.shape[1] // 2
        rows = left.shape[1] // 2
        away = dot(left, right[:, half:], ((0,), (0,))).astype(bf16)
        kept = dot(left, right[:, :half], ((0,), (0,)))
        total = kept + swap_col(away).astype(f32)
        return total[:rows], swap_row(total[rows:].astype(bf16))

    def reduce_col_row(left, right):
        half = left.shape[1] // 2
        columns = right.shape[1] // 2
        away = dot(left[:, half:], right, ((0,), (0,))).astype(bf16)
        kept = dot(left[:, :half], right, ((0,), (0,)))
        total = kept + swap_col(away).astype(f32)
        return total[:, :columns], swap_row(total[:, columns:].astype(bf16))

    resid_parts = swap_all(token_blocks(tokens_in))
    params = [swap(norm_params, d) for d in range(4)]
    params = jnp.concatenate(
        [in_order(col, params[0], params[1]), in_order(col, params[2], params[3])], axis=1
    )
    qkv_mine = qkv_weight.astype(bf16)
    qkv_row = row_partner(qkv_mine, qkv_weight)
    qkv_low = [qkv_mine, qkv_row, swap_col(qkv_mine), swap_col(qkv_row)]
    proj_mine = proj_weight.astype(bf16)
    proj_row = row_partner(proj_mine, proj_weight)
    proj_low = [proj_mine, proj_row, swap_col(proj_mine), swap_col(proj_row)]
    expand_mine = expand_weight.astype(bf16)
    expand_row = row_partner(expand_mine, expand_weight)
    expand_low = [expand_mine, expand_row, swap_col(expand_mine), swap_col(expand_row)]

    resid_parts, contract_low, grad_blocks = lax.optimization_barrier(
        (resid_parts, contract_weight.astype(bf16), token_blocks(out_grad))
    )
    contract_mine = contract_low
    contract_row = swap_row(contract_mine)
    contract_low = [contract_mine, contract_row, swap_col(contract_mine), swap_col(contract_row)]
    grad_parts = swap_all(grad_blocks)
    grad_low = jnp.concatenate(
        [in_order(col, grad_parts[0], grad_parts[1]), in_order(col, grad_parts[2], grad_parts[3])],
        axis=1,
    )
    grad_low = jnp.pad(grad_low, ((0, padded - tokens), (0, 0)))

    resid, h_one, mixed = qkv_forward(place, resid_parts, params, qkv_low)
    attended, probs = attend_forward(mixed)
    outs = block_middle(
        place, tokens, resid, attended, grad_low, params, proj_low, expand_low, contract_low
    )
    output_parts = outs[:4]
    h_two, hidden, grad_pre, grad_middle, grad_branch, grad_attended, sums_two = outs[4:]
    contract_grad = reduce_col_row(hidden, grad_low)
    expand_grad = reduce_row_col(h_two, grad_pre)
    proj_grad = reduce_col_row(attended, grad_branch)
    grad_mixed = attend_backward(mixed, probs, grad_attended)
    qkv_grad = reduce_row_col(h_one, grad_mixed)
    outs = input_backward(place, tokens, grad_mixed, grad_middle, resid, params, qkv_low)
    input_parts, sums_one = outs[:4], outs[4]

    qkv_grad, output_parts, input_parts = lax.optimization_barrier(
        (qkv_grad, output_parts, input_parts)
    )

    def over_dp(kept, received):
        gradient = (kept + received.astype(f32)).astype(bf16)
        if n_dp != 8:
            return lax.psum(gradient, "dp").astype(f32)
        rows = gradient.shape[0] // 2
        x, z = dp % 2, dp // 2
        away = lax.dynamic_slice_in_dim(gradient, (1 - x) * rows, rows)
        total = lax.dynamic_slice_in_dim(gradient, x * rows, rows).astype(f32)
        total = (total + swap_dp(away, 1).astype(f32)).astype(bf16)
        pieces = [lax.dynamic_slice_in_dim(total, (z ^ d) * (rows // 4), rows // 4) for d in range(4)]
        mine = pieces[0].astype(f32)
        for d in range(1, 4):
            mine = mine + swap_dp(pieces[d], 2 * d).astype(f32)
        mine = mine.astype(bf16)
        here = jnp.stack([mine] + [swap_dp(mine, 2 * d) for d in range(1, 4)])
        return here, swap_dp(here, 1)

    contract_sum = over_dp(*contract_grad)
    expand_sum = over_dp(*expand_grad)
    proj_sum = over_dp(*proj_grad)
    qkv_sum = over_dp(*qkv_grad)
    norm_parts = split_features(col, jnp.concatenate([sums_one, sums_two], axis=0))
    norm_sum = norm_parts[0] + sum(swap(norm_parts[d], d) for d in range(1, 4))
    if n_dp == 8:
        for d in (1, 2, 4):
            norm_sum = norm_sum + swap_dp(norm_sum, d)
    else:
        norm_sum = lax.psum(norm_sum, "dp")

    results = (
        tokens_apart(place, swap_all(output_parts)),
        tokens_apart(place, swap_all(input_parts)),
    )
    for weight, gradient, first, second in (
        (qkv_weight, qkv_sum, qkv_first, qkv_second),
        (proj_weight, proj_sum, proj_first, proj_second),
        (expand_weight, expand_sum, expand_first, expand_second),
        (contract_weight, contract_sum, contract_first, contract_second),
    ):
        if n_dp == 8:
            results += tuple(adamw_pieces(place, weight, first, second, *gradient))
        else:
            results += adamw_update(weight, gradient, first, second, rate_matrix, decay_matrix)
    return results + adamw_update(norm_params, norm_sum, norm_first, norm_second, rate_norm, 0.0)


def solution(mesh):
    tokens = P("dp", ("row", "col"))
    one = P("row", "col")
    two = P("col", "row")
    norm = P(None, ("row", "col"))
    in_specs = (tokens, tokens, one, two, one, two, norm)
    in_specs += (one, one, two, two, one, one, two, two, norm, norm)
    out_specs = (tokens, tokens) + (one,) * 3 + (two,) * 3 + (one,) * 3 + (two,) * 3 + (norm,) * 3
    return jax.shard_map(local, mesh=mesh, in_specs=in_specs, out_specs=out_specs, check_vma=False)
```

```python
import jax
import jax.numpy as jnp
from jax import lax
from jax.experimental import pallas as pl
from jax.experimental.pallas import tpu as pltpu
from jax.sharding import PartitionSpec as P

HEAD_DIM = 64
SEQ = 197
QROWS = 208
KROWS = 256
STEP = 10
ROWS = 1200
BLOCK = 240
STEPS = 6
GROUPED = 2

norm_epsilon = 1e-06
beta_first = 0.9
beta_second = 0.999
adam_epsilon = 1e-08
rate_matrix = 0.1
rate_norm = 0.5
decay_matrix = 0.05

GROUP = ("row", "col")
bf16 = jnp.bfloat16
f32 = jnp.float32


def dot(left, right, dims=((1,), (0,))):
    return lax.dot_general(left, right, (dims, ((), ())), preferred_element_type=f32)


def swap_halves(block):
    return jnp.concatenate([block[:, HEAD_DIM:], block[:, :HEAD_DIM]], axis=1)


def gelu_and_slope(value):
    size = jnp.abs(value)
    density = jnp.exp(value * value * -0.5)
    t = 1.0 / (1.0 + (0.3275911 * 0.5**0.5) * size)
    series = t * (
        0.254829592
        + t * (-0.284496736 + t * (1.421413741 + t * (-1.453152027 + t * 1.061405429)))
    )
    tail = 0.5 * series * density
    phi = jnp.where(value >= 0, 1.0 - tail, tail)
    return (value * phi, phi + value * density * 0.3989422804014327)


def adamw_update(weight, gradient, first_old, second_old, rate_value, decay_value):
    first_new = beta_first * first_old + (1.0 - beta_first) * gradient
    second_new = beta_second * second_old + (1.0 - beta_second) * (gradient * gradient)
    first_hat = first_new / (1.0 - beta_first**STEP)
    second_hat = second_new / (1.0 - beta_second**STEP)
    moved = weight - rate_value * (
        first_hat / (jnp.sqrt(second_hat) + adam_epsilon) + decay_value * weight
    )
    return (moved, first_new, second_new)


def norm_rows(values):
    center = jnp.mean(values, axis=1, keepdims=True)
    spread = jnp.mean(values * values, axis=1, keepdims=True) - center * center
    scaled = lax.rsqrt(spread + norm_epsilon)
    return ((values - center) * scaled, scaled)


def norm_backward(grad_normed, normed, scaled, gain_row):
    local_grad = grad_normed * gain_row
    first = jnp.mean(local_grad, axis=1, keepdims=True)
    second = jnp.mean(local_grad * normed, axis=1, keepdims=True)
    return scaled * (local_grad - first - normed * second)


def in_order(col, first, second):
    return jnp.where(
        col == 0,
        jnp.concatenate([first, second], axis=-1),
        jnp.concatenate([second, first], axis=-1),
    )


def split_features(col, array):
    part = array.shape[-1] // 4
    quarters = [array[..., i * part : (i + 1) * part] for i in range(4)]
    own = [jnp.where(col == 0, quarters[2 * i], quarters[2 * i + 1]) for i in range(2)]
    other = [jnp.where(col == 0, quarters[2 * i + 1], quarters[2 * i]) for i in range(2)]
    return [own[0], other[0], own[1], other[1]]


def resident(array):
    zeros = (0,) * array.ndim
    return pl.BlockSpec(array.shape, lambda i, *_: zeros, pipeline_mode=pl.Buffered(1))


def column_block(rows, width):
    return pl.BlockSpec((rows, width), lambda i, *_: (0, i))


def side_blocks(rows, width, along, steps):
    def first(i, *_):
        at = jnp.minimum(i, steps // 2 - 1)
        return (0, at) if along == 1 else (at, 0)

    def second(i, *_):
        at = jnp.maximum(i - steps // 2, 0)
        return (0, at) if along == 1 else (at, 0)

    block = (rows, width)
    return [pl.BlockSpec(block, first)] * 2 + [pl.BlockSpec(block, second)] * 2


def side_weight(refs, steps, axis):
    own = jnp.concatenate([refs[0][...], refs[1][...]], axis=axis)
    other = jnp.concatenate([refs[2][...], refs[3][...]], axis=axis)
    return jnp.where(pl.program_id(0) < steps // 2, own, other)


def split_parts(col, array):
    part = array.shape[0] // 4
    quarters = [array[i * part : (i + 1) * part] for i in range(4)]
    own = [jnp.where(col == 0, quarters[2 * i], quarters[2 * i + 1]) for i in range(2)]
    other = [jnp.where(col == 0, quarters[2 * i + 1], quarters[2 * i]) for i in range(2)]
    return [own[0], other[0], own[1], other[1]]


def together_kernel(place, *refs):
    parts, out_ref = refs[:4], refs[4]
    part, tokens = parts[0].shape
    wide = [ref[...].astype(f32) for ref in parts]
    for half in range(2):
        first, second = wide[2 * half], wide[2 * half + 1]
        both = [jnp.where(place[0] == 0, first, second), jnp.where(place[0] == 0, second, first)]
        block = jnp.concatenate(both, axis=0)
        at = 2 * part * half
        out_ref[0:tokens, at : at + 2 * part] = block.T.astype(bf16)
    low = tokens - tokens % 16
    row = lax.broadcasted_iota(jnp.int32, (out_ref.shape[0] - low, 1), 0) + low
    out_ref[low:, :] = jnp.where(row < tokens, out_ref[low:, :].astype(f32), 0.0).astype(bf16)


def tokens_together(place, parts):
    part, tokens = parts[0].shape
    padded = -(-tokens // ROWS) * ROWS
    return pl.pallas_call(
        together_kernel,
        in_specs=[pl.BlockSpec(memory_space=pltpu.SMEM)]
        + [pl.BlockSpec(memory_space=pltpu.VMEM)] * 4,
        out_specs=pl.BlockSpec(memory_space=pltpu.VMEM),
        out_shape=jax.ShapeDtypeStruct((padded, 4 * part), bf16),
        compiler_params=pltpu.CompilerParams(vmem_limit_bytes=40 * 2**20),
        cost_estimate=pl.CostEstimate(
            flops=0, bytes_accessed=16 * tokens * part, transcendentals=0
        ),
        name="tokens_together",
    )(place, *parts)


def apart_kernel(place, *refs):
    parts, out_ref = refs[:4], refs[4]
    tokens = out_ref.shape[1] // 4
    for block in range(4):
        for distance in range(4):

            @pl.when((place[1] ^ block) == distance)
            def _():
                columns = slice(block * tokens, (block + 1) * tokens)
                out_ref[:, columns] = parts[distance][...].astype(f32)[:, :tokens]


def tokens_apart(place, tokens, parts):
    part = parts[0].shape[0]
    return pl.pallas_call(
        apart_kernel,
        in_specs=[pl.BlockSpec(memory_space=pltpu.SMEM)]
        + [pl.BlockSpec(memory_space=pltpu.VMEM)] * 4,
        out_specs=pl.BlockSpec(memory_space=pltpu.VMEM),
        out_shape=jax.ShapeDtypeStruct((part, 4 * tokens), f32),
        compiler_params=pltpu.CompilerParams(vmem_limit_bytes=40 * 2**20),
        cost_estimate=pl.CostEstimate(
            flops=0, bytes_accessed=4 * tokens * part * 6, transcendentals=0
        ),
        name="tokens_apart",
    )(place, *parts).T


def forward_kernel(*refs):
    resid_ref, params = refs[:2]
    weights = refs[2:6]
    h_ref, mixed_ref, out_ref, probs_ref, wide, gathered = refs[6:]
    rows = resid_ref.shape[0]
    images = rows // SEQ
    tokens = images * SEQ
    steps = pl.num_programs(0)

    @pl.when(pl.program_id(0) == 0)
    def _():
        for start in range(0, rows, BLOCK):
            block = slice(start, start + BLOCK)
            normed, _ = norm_rows(resid_ref[block, :].astype(f32))
            h_ref[block, :] = (normed * params[0:1, :] + params[1:2, :]).astype(bf16)

    weight = side_weight(weights, STEPS, 0)
    for start in range(0, rows, BLOCK):
        block = slice(start, start + BLOCK)
        mixed = dot(h_ref[block, :], weight).astype(bf16)
        mixed_ref[block, :] = mixed
        wide[block, :] = mixed.astype(f32)
    wide[rows:, :] = jnp.zeros((wide.shape[0] - rows, 384), f32)
    low_lane = lax.broadcasted_iota(jnp.int32, (1, 128), 1) < HEAD_DIM
    key_lane = lax.broadcasted_iota(jnp.int32, (1, KROWS), 1) < SEQ
    scale = HEAD_DIM ** (-0.5)
    for group in range(0, images, GROUPED):
        members = range(group, min(group + GROUPED, images))
        scores, values = [], []
        for image in members:
            start = image * SEQ
            block_a = wide[start : start + KROWS, 0:128]
            block_b = wide[start : start + KROWS, 128:256]
            block_c = wide[start : start + KROWS, 256:384]
            query_0 = jnp.where(low_lane, block_a[:QROWS] * scale, 0.0).astype(bf16)
            query_1 = jnp.where(low_lane, 0.0, block_b[:QROWS] * scale).astype(bf16)
            scores.append(dot(query_0, swap_halves(block_a).astype(bf16), ((1,), (1,))))
            scores.append(dot(query_1, swap_halves(block_c).astype(bf16), ((1,), (1,))))
            values += [block_b.astype(bf16), block_c.astype(bf16)]
        scores = [jnp.where(key_lane, score, -1e30) for score in scores]
        tops = [jnp.max(score, axis=1, keepdims=True) for score in scores]
        exponents = [jnp.exp(score - top) for score, top in zip(scores, tops)]
        totals = [jnp.sum(exponent, axis=1, keepdims=True) for exponent in exponents]
        probs = [(e * (1.0 / total)).astype(bf16) for e, total in zip(exponents, totals)]
        outs = [dot(prob, value) for prob, value in zip(probs, values)]
        for at, image in enumerate(members):
            start = image * SEQ
            probs_ref[0, image * 2] = probs[2 * at]
            probs_ref[0, image * 2 + 1] = probs[2 * at + 1]
            gathered[start : start + QROWS, :] = jnp.where(
                low_lane, outs[2 * at], outs[2 * at + 1]
            )
    gathered[tokens:, :] = jnp.zeros((gathered.shape[0] - tokens, 128), f32)
    out_ref[...] = gathered[0:rows, :].astype(bf16)


def attend_forward(resid, params, weights):
    rows, width = resid.shape
    images = rows // SEQ
    padded = -(-((images - 1) * SEQ + KROWS) // 16) * 16
    pair_probs = (STEPS, 2 * images, QROWS, KROWS)
    half_rows = weights[0].shape[0]
    return pl.pallas_call(
        forward_kernel,
        grid=(STEPS,),
        in_specs=[resident(resid), resident(params), *side_blocks(half_rows, 384, 1, STEPS)],
        out_specs=[
            pl.BlockSpec((rows, width), lambda i: (0, 0)),
            column_block(rows, 384),
            column_block(rows, 128),
            pl.BlockSpec((1, *pair_probs[1:]), lambda i: (i, 0, 0, 0)),
        ],
        out_shape=[
            jax.ShapeDtypeStruct((rows, width), bf16),
            jax.ShapeDtypeStruct((rows, STEPS * 384), bf16),
            jax.ShapeDtypeStruct((rows, STEPS * 128), bf16),
            jax.ShapeDtypeStruct(pair_probs, bf16),
        ],
        scratch_shapes=[pltpu.VMEM((padded, 384), f32), pltpu.VMEM((padded, 128), f32)],
        compiler_params=pltpu.CompilerParams(vmem_limit_bytes=54 * 2**20),
        cost_estimate=pl.CostEstimate(
            flops=20 * 10**9, bytes_accessed=rows * width * 20, transcendentals=10**6
        ),
        name="attend_forward",
    )(resid, params, *weights)


def backward_kernel(place, *refs):
    mixed_ref, probs_ref, grad_ref, middle_ref, resid_ref, params = refs[:6]
    weights = refs[6:10]
    out_ref, out_parts, sums_ref = refs[10], refs[11:15], refs[15]
    wide, grad_wide, gathered, total = refs[16:]
    rows = mixed_ref.shape[0]
    images = rows // SEQ
    tokens = images * SEQ
    wide[rows:, :] = jnp.zeros((wide.shape[0] - rows, 384), f32)
    wide[0:rows, :] = mixed_ref[...].astype(f32)
    grad_wide[0:rows, :] = grad_ref[...].astype(f32)
    low_lane = lax.broadcasted_iota(jnp.int32, (1, 128), 1) < HEAD_DIM
    query_row = lax.broadcasted_iota(jnp.int32, (QROWS, 128), 0) < SEQ
    scale = HEAD_DIM ** (-0.5)
    for group in range(0, images, GROUPED):
        members = range(group, min(group + GROUPED, images))
        grad_probs, grad_values, probs, swapped = [], [], [], []
        for image in members:
            start = image * SEQ
            block_a = wide[start : start + KROWS, 0:128]
            block_b = wide[start : start + KROWS, 128:256]
            block_c = wide[start : start + KROWS, 256:384]
            grad = jnp.where(query_row, grad_wide[start : start + QROWS, :], 0.0)
            grad_low = grad.astype(bf16)
            probs_0 = probs_ref[0, 2 * image]
            probs_1 = probs_ref[0, 2 * image + 1]
            probs += [probs_0, probs_1]
            part_0 = jnp.where(low_lane, grad, 0.0).astype(bf16)
            part_1 = jnp.where(low_lane, 0.0, grad).astype(bf16)
            grad_probs.append(dot(part_0, block_b.astype(bf16), ((1,), (1,))))
            grad_probs.append(dot(part_1, block_c.astype(bf16), ((1,), (1,))))
            grad_values.append(dot(probs_0, grad_low, ((0,), (0,))))
            grad_values.append(dot(probs_1, grad_low, ((0,), (0,))))
            swapped.append(
                [(swap_halves(block) * scale).astype(bf16) for block in (block_a, block_b, block_c)]
            )
        wide_probs = [prob.astype(f32) for prob in probs]
        inner = [
            jnp.sum(prob * grad, axis=1, keepdims=True)
            for prob, grad in zip(wide_probs, grad_probs)
        ]
        score_grads = [
            (prob * (grad - each)).astype(bf16)
            for prob, grad, each in zip(wide_probs, grad_probs, inner)
        ]
        for at, image in enumerate(members):
            start = image * SEQ
            swapped_a, swapped_b, swapped_c = swapped[at]
            score_0, score_1 = score_grads[2 * at : 2 * at + 2]
            grad_v0, grad_v1 = grad_values[2 * at : 2 * at + 2]
            grad_q0 = dot(score_0, swapped_a)
            grad_k0 = dot(score_0, swapped_a[:QROWS], ((0,), (0,)))
            grad_q1 = dot(score_1, swapped_c)
            grad_k1 = dot(score_1, swapped_b[:QROWS], ((0,), (0,)))
            block = slice(start, start + QROWS)
            gathered[block, 0:128] = jnp.where(low_lane, grad_q0, grad_k0[:QROWS])
            gathered[block, 128:256] = jnp.where(low_lane, grad_v0[:QROWS], grad_q1)
            gathered[block, 256:384] = jnp.where(low_lane, grad_k1[:QROWS], grad_v1[:QROWS])
    gathered[tokens:, :] = jnp.zeros((gathered.shape[0] - tokens, 384), f32)
    weight = side_weight(weights, STEPS, 0)
    step = pl.program_id(0)

    @pl.when(step == 0)
    def _():
        total[...] = jnp.zeros_like(total)

    for start in range(0, rows, BLOCK):
        block = slice(start, start + BLOCK)
        grad_mixed = gathered[block, :].astype(bf16)
        out_ref[block, :] = grad_mixed
        total[block, :] += dot(grad_mixed, weight, ((1,), (1,)))

    @pl.when(step == STEPS - 1)
    def _():
        gain = jnp.zeros((1, total.shape[1]), f32)
        shift = jnp.zeros((1, total.shape[1]), f32)
        for start in range(0, rows, BLOCK):
            block = slice(start, start + BLOCK)
            grad_one = total[block, :]
            normed, scaled = norm_rows(resid_ref[block, :].astype(f32))
            gain += jnp.sum(grad_one * normed, axis=0, keepdims=True)
            shift += jnp.sum(grad_one, axis=0, keepdims=True)
            total[block, :] = middle_ref[block, :] + norm_backward(
                grad_one, normed, scaled, params[0:1, :]
            )
        sums_ref[0:1, :] = gain
        sums_ref[1:2, :] = shift
        for part_ref, part in zip(out_parts, split_parts(place[0], total[...].T)):
            part_ref[...] = part.astype(bf16)


def attend_backward(place, mixed, probs, grad_attended, grad_middle, resid, params, weights):
    rows, width = resid.shape
    images = rows // SEQ
    padded = -(-((images - 1) * SEQ + KROWS) // 16) * 16
    part = jax.ShapeDtypeStruct((width // 4, rows), bf16)
    sums = jax.ShapeDtypeStruct((2, width), f32)
    whole = [pl.BlockSpec(each.shape, lambda i, *_: (0, 0)) for each in [part] * 4 + [sums]]
    return pl.pallas_call(
        backward_kernel,
        grid_spec=pltpu.PrefetchScalarGridSpec(
            num_scalar_prefetch=1,
            grid=(STEPS,),
            in_specs=[
                column_block(rows, 384),
                pl.BlockSpec((1, *probs.shape[1:]), lambda i, *_: (i, 0, 0, 0)),
                column_block(rows, 128),
                resident(grad_middle),
                resident(resid),
                resident(params),
                *side_blocks(weights[0].shape[0], 384, 1, STEPS),
            ],
            out_specs=[column_block(rows, 384), *whole],
            scratch_shapes=[
                pltpu.VMEM((padded, 384), f32),
                pltpu.VMEM((padded, 128), f32),
                pltpu.VMEM((padded, 384), f32),
                pltpu.VMEM((rows, width), f32),
            ],
        ),
        out_shape=[jax.ShapeDtypeStruct(mixed.shape, bf16), *[part] * 4, sums],
        compiler_params=pltpu.CompilerParams(vmem_limit_bytes=54 * 2**20),
        cost_estimate=pl.CostEstimate(
            flops=30 * 10**9, bytes_accessed=rows * width * 24, transcendentals=0
        ),
        name="attend_backward",
    )(place, mixed, probs, grad_attended, grad_middle, resid, params, *weights)


def block_kernel(place, *refs):
    resid_ref, attended_ref, grad_ref, params = refs[:4]
    proj, expand, contract = refs[4:8], refs[8:12], refs[12:16]
    out_parts = refs[16:20]
    h_ref, hidden_ref, pre_ref, middle_ref, attended_grad_ref, sums_ref = refs[20:26]
    middle, output, grad_two = refs[26:]
    rows = resid_ref.shape[0]
    step = pl.program_id(0)
    blocks = [slice(start, start + BLOCK) for start in range(0, rows, BLOCK)]

    def proj_low():
        own = jnp.concatenate([proj[0][...], proj[1][...]], axis=1)
        return jnp.concatenate([own, jnp.concatenate([proj[2][...], proj[3][...]], axis=1)], axis=0)

    @pl.when(step == 0)
    def _():
        weight = proj_low()
        for block in blocks:
            value = resid_ref[block, :].astype(f32) + dot(attended_ref[block, :], weight)
            middle[block, :] = value
            output[block, :] = value
            grad_two[block, :] = jnp.zeros_like(value)
            normed, _ = norm_rows(value)
            h_ref[block, :] = (normed * params[2:3, :] + params[3:4, :]).astype(bf16)

    expand_low = side_weight(expand, STEPS, 0)
    contract_low = side_weight(contract, STEPS, 1)

    def products(block):
        return (
            dot(h_ref[block, :], expand_low),
            dot(grad_ref[block, :], contract_low, ((1,), (1,))),
        )

    ahead = products(blocks[0])
    for at, block in enumerate(blocks):
        before, grad_hidden = ahead
        if at + 1 < len(blocks):
            ahead = products(blocks[at + 1])
        value, slope = gelu_and_slope(before)
        hidden = value.astype(bf16)
        grad_pre = (grad_hidden * slope).astype(bf16)
        hidden_ref[block, :] = hidden
        pre_ref[block, :] = grad_pre
        output[block, :] += dot(hidden, contract_low)
        grad_two[block, :] += dot(grad_pre, expand_low, ((1,), (1,)))

    @pl.when(step == STEPS - 1)
    def _():
        weight = proj_low()
        gain = jnp.zeros((1, middle.shape[1]), f32)
        shift = jnp.zeros((1, middle.shape[1]), f32)
        for block in blocks:
            grad = grad_two[block, :]
            normed, scaled = norm_rows(middle[block, :])
            gain += jnp.sum(grad * normed, axis=0, keepdims=True)
            shift += jnp.sum(grad, axis=0, keepdims=True)
            grad_middle = grad_ref[block, :].astype(f32) + norm_backward(
                grad, normed, scaled, params[2:3, :]
            )
            middle_ref[block, :] = grad_middle
            attended_grad_ref[block, :] = dot(
                grad_middle.astype(bf16), weight, ((1,), (1,))
            ).astype(bf16)
        sums_ref[0:1, :] = gain
        sums_ref[1:2, :] = shift
        for part_ref, part in zip(out_parts, split_parts(place[0], output[...].T)):
            part_ref[...] = part.astype(bf16)


def block_middle(place, resid, attended, grad, params, proj, expand, contract):
    rows, width = resid.shape
    ff = 2 * expand[0].shape[1]
    chunk = ff // STEPS
    part = jax.ShapeDtypeStruct((width // 4, rows), bf16)
    narrow = jax.ShapeDtypeStruct((rows, width), bf16)
    broad = jax.ShapeDtypeStruct((rows, ff), bf16)
    wide = jax.ShapeDtypeStruct((rows, width), f32)
    sums = jax.ShapeDtypeStruct((2, width), f32)

    def fixed(shape):
        return pl.BlockSpec(shape.shape, lambda i, *_: (0, 0))

    return pl.pallas_call(
        block_kernel,
        grid_spec=pltpu.PrefetchScalarGridSpec(
            num_scalar_prefetch=1,
            grid=(STEPS,),
            in_specs=[
                *[resident(each) for each in (resid, attended, grad, params, *proj)],
                *side_blocks(expand[0].shape[0], chunk, 1, STEPS),
                *side_blocks(chunk, contract[0].shape[1], 0, STEPS),
            ],
            out_specs=[
                *[fixed(part)] * 4,
                fixed(narrow),
                column_block(rows, chunk),
                column_block(rows, chunk),
                fixed(wide),
                fixed(narrow),
                fixed(sums),
            ],
            scratch_shapes=[pltpu.VMEM((rows, width), f32)] * 3,
        ),
        out_shape=[*[part] * 4, narrow, broad, broad, wide, narrow, sums],
        compiler_params=pltpu.CompilerParams(vmem_limit_bytes=58 * 2**20),
        cost_estimate=pl.CostEstimate(
            flops=2 * rows * width * (4 * ff + 2 * width),
            bytes_accessed=rows * ff * 8,
            transcendentals=2 * rows * ff,
        ),
        name="block_middle",
    )(place, resid, attended, grad, params, *proj, *expand, *contract)


def adamw_kernel(place, weight, first, second, here, there, weight_out, first_out, second_out):
    x = place[2]
    mine = jnp.where(pl.program_id(0) // 4 == x, here[0].astype(f32), there[0].astype(f32))
    results = adamw_update(
        weight[...], mine, first[...], second[...], rate_matrix, decay_matrix
    )
    weight_out[...], first_out[...], second_out[...] = results


def adamw_pieces(place, weight, first, second, here, there):
    rows, width = weight.shape
    piece = pl.BlockSpec((rows // 8, width), lambda i, place: (i, 0))
    part = pl.BlockSpec((1, rows // 8, width), lambda i, place: ((i % 4) ^ place[3], 0, 0))
    return pl.pallas_call(
        adamw_kernel,
        grid_spec=pltpu.PrefetchScalarGridSpec(
            num_scalar_prefetch=1,
            grid=(8,),
            in_specs=[piece, piece, piece, part, part],
            out_specs=[piece] * 3,
        ),
        out_shape=[jax.ShapeDtypeStruct((rows, width), f32)] * 3,
        compiler_params=pltpu.CompilerParams(vmem_limit_bytes=40 * 2**20),
        cost_estimate=pl.CostEstimate(
            flops=20 * rows * width, bytes_accessed=28 * rows * width, transcendentals=0
        ),
        name="adamw_pieces",
    )(place, weight, first, second, here, there)


def local(
    tokens_in,
    out_grad,
    qkv_weight,
    proj_weight,
    expand_weight,
    contract_weight,
    norm_params,
    qkv_first,
    qkv_second,
    proj_first,
    proj_second,
    expand_first,
    expand_second,
    contract_first,
    contract_second,
    norm_first,
    norm_second,
):
    row = lax.axis_index("row")
    col = lax.axis_index("col")
    dp = lax.axis_index("dp")
    n_dp = lax.axis_size("dp")
    me = 2 * row + col
    place = jnp.stack([col, me, dp % 2, dp // 2]).astype(jnp.int32)
    tokens = tokens_in.shape[0] // 4
    part = tokens_in.shape[1]

    def swap(array, distance):
        if distance == 0:
            return array
        return lax.ppermute(array, GROUP, [(i, i ^ distance) for i in range(4)])

    def swap_dp(array, distance):
        return lax.ppermute(array, "dp", [(i, i ^ distance) for i in range(n_dp)])

    def swap_row(array):
        return swap(array, 2)

    def swap_col(array):
        return swap(array, 1)

    def token_blocks(array):
        return [lax.dynamic_slice(array, ((me ^ d) * tokens, 0), (tokens, part)) for d in range(4)]

    def swap_all(blocks):
        return [swap(block, d) for d, block in enumerate(blocks)]

    def ordered(bit, mine, partner):
        return jnp.where(
            bit == 0,
            jnp.concatenate([mine, partner], axis=0),
            jnp.concatenate([partner, mine], axis=0),
        )

    def by_halves(mine):
        rows = mine.shape[0] // 2
        got = swap_row(lax.dynamic_slice_in_dim(mine, (dp % 2) * rows, rows))
        return ordered(dp % 2, got, swap_dp(got, 1))

    def by_quarters(mine):
        rows = mine.shape[0] // 4
        got = swap_row(lax.dynamic_slice_in_dim(mine, (dp % 4) * rows, rows))
        got = ordered(dp % 2, got, swap_dp(got, 1))
        return ordered(dp // 2 % 2, got, swap_dp(got, 2))

    def all_blocks(mine, partner):
        return [mine, partner, swap_col(mine), swap_col(partner)]

    def reduce_row_col(left, right):
        half = right.shape[1] // 2
        rows = left.shape[1] // 2
        away = dot(left, right[:, half:], ((0,), (0,))).astype(bf16)
        kept = dot(left, right[:, :half], ((0,), (0,)))
        total = kept + swap_col(away).astype(f32)
        return total[:rows], total[rows:].astype(bf16)

    def reduce_col_row(left, right):
        half = left.shape[1] // 2
        columns = right.shape[1] // 2
        away = dot(left[:, half:], right, ((0,), (0,))).astype(bf16)
        kept = dot(left[:, :half], right, ((0,), (0,)))
        total = kept + swap_col(away).astype(f32)
        return total[:, :columns], total[:, columns:].astype(bf16)

    resid_parts = swap_all(token_blocks(tokens_in))
    params = [swap(norm_params, d) for d in range(4)]
    params = jnp.concatenate(
        [in_order(col, params[0], params[1]), in_order(col, params[2], params[3])], axis=1
    )
    qkv_mine = qkv_weight.astype(bf16)
    qkv_low = all_blocks(qkv_mine, by_halves(qkv_mine))

    resid_parts, proj_mine, expand_mine, contract_mine, grad_blocks = lax.optimization_barrier(
        (
            resid_parts,
            proj_weight.astype(bf16),
            expand_weight.astype(bf16),
            contract_weight.astype(bf16),
            token_blocks(out_grad),
        )
    )
    proj_low = all_blocks(proj_mine, by_halves(proj_mine))
    expand_low = all_blocks(expand_mine, by_quarters(expand_mine))
    contract_low = all_blocks(contract_mine, by_quarters(contract_mine))
    grad_parts = swap_all(grad_blocks)
    resid = tokens_together(place, [each.T for each in resid_parts])
    h_one, mixed, attended, probs = attend_forward(resid, params, qkv_low)
    grad_low = tokens_together(place, [each.T for each in grad_parts])
    outs = block_middle(place, resid, attended, grad_low, params, proj_low, expand_low, contract_low)
    output_parts = outs[:4]
    h_two, hidden, grad_pre, grad_middle, grad_attended, sums_two = outs[4:]
    contract_grad = reduce_col_row(hidden, grad_low)
    expand_grad = reduce_row_col(h_two, grad_pre)
    proj_grad = reduce_col_row(attended, grad_middle.astype(bf16))
    contract_grad, expand_grad, proj_grad, grad_attended = lax.optimization_barrier(
        (contract_grad, expand_grad, proj_grad, grad_attended)
    )
    contract_grad, expand_grad, proj_grad = [
        (kept, swap_row(away)) for kept, away in (contract_grad, expand_grad, proj_grad)
    ]
    outs = attend_backward(
        place, mixed, probs, grad_attended, grad_middle, resid, params, qkv_low
    )
    grad_mixed, input_parts, sums_one = outs[0], outs[1:5], outs[5]
    kept, away = reduce_row_col(h_one, grad_mixed)
    qkv_grad = (kept, swap_row(away))

    qkv_grad, output_parts, input_parts = lax.optimization_barrier(
        (qkv_grad, output_parts, input_parts)
    )

    def over_dp(kept, received):
        gradient = (kept + received.astype(f32)).astype(bf16)
        if n_dp != 8:
            return lax.psum(gradient, "dp").astype(f32)
        rows = gradient.shape[0] // 2
        x, z = dp % 2, dp // 2
        away = lax.dynamic_slice_in_dim(gradient, (1 - x) * rows, rows)
        total = lax.dynamic_slice_in_dim(gradient, x * rows, rows).astype(f32)
        total = (total + swap_dp(away, 1).astype(f32)).astype(bf16)
        pieces = [lax.dynamic_slice_in_dim(total, (z ^ d) * (rows // 4), rows // 4) for d in range(4)]
        mine = pieces[0].astype(f32)
        for d in range(1, 4):
            mine = mine + swap_dp(pieces[d], 2 * d).astype(f32)
        mine = mine.astype(bf16)
        here = jnp.stack([mine] + [swap_dp(mine, 2 * d) for d in range(1, 4)])
        return here, swap_dp(here, 1)

    contract_sum = over_dp(*contract_grad)
    expand_sum = over_dp(*expand_grad)
    proj_sum = over_dp(*proj_grad)
    qkv_sum = over_dp(*qkv_grad)
    norm_parts = split_features(col, jnp.concatenate([sums_one, sums_two], axis=0))
    norm_sum = norm_parts[0] + sum(swap(norm_parts[d], d) for d in range(1, 4))
    if n_dp == 8:
        for d in (1, 2, 4):
            norm_sum = norm_sum + swap_dp(norm_sum, d)
    else:
        norm_sum = lax.psum(norm_sum, "dp")

    results = (
        tokens_apart(place, tokens, swap_all(output_parts)),
        tokens_apart(place, tokens, swap_all(input_parts)),
    )
    for weight, gradient, first, second in (
        (qkv_weight, qkv_sum, qkv_first, qkv_second),
        (proj_weight, proj_sum, proj_first, proj_second),
        (expand_weight, expand_sum, expand_first, expand_second),
        (contract_weight, contract_sum, contract_first, contract_second),
    ):
        if n_dp == 8:
            results += tuple(adamw_pieces(place, weight, first, second, *gradient))
        else:
            results += adamw_update(weight, gradient, first, second, rate_matrix, decay_matrix)
    return results + adamw_update(norm_params, norm_sum, norm_first, norm_second, rate_norm, 0.0)


def solution(mesh):
    tokens = P("dp", ("row", "col"))
    one = P("row", "col")
    two = P("col", "row")
    norm = P(None, ("row", "col"))
    in_specs = (tokens, tokens, one, two, one, two, norm)
    in_specs += (one, one, two, two, one, one, two, two, norm, norm)
    out_specs = (tokens, tokens) + (one,) * 3 + (two,) * 3 + (one,) * 3 + (two,) * 3 + (norm,) * 3
    return jax.shard_map(local, mesh=mesh, in_specs=in_specs, out_specs=out_specs, check_vma=False)
```

```python
import jax
import jax.numpy as jnp
from jax import lax
from jax.experimental import pallas as pl
from jax.experimental.pallas import tpu as pltpu
from jax.sharding import PartitionSpec as P

HEAD_DIM = 64
SEQ = 197
QROWS = 208
KROWS = 256
STEP = 10
ROWS = 1200
BLOCK = 240
STEPS = 6
GROUPED = 2

norm_epsilon = 1e-06
beta_first = 0.9
beta_second = 0.999
adam_epsilon = 1e-08
rate_matrix = 0.1
rate_norm = 0.5
decay_matrix = 0.05

GROUP = ("row", "col")
bf16 = jnp.bfloat16
f32 = jnp.float32


def dot(left, right, dims=((1,), (0,))):
    return lax.dot_general(left, right, (dims, ((), ())), preferred_element_type=f32)


def swap_halves(block):
    return jnp.concatenate([block[:, HEAD_DIM:], block[:, :HEAD_DIM]], axis=1)


def gelu_and_slope(value):
    size = jnp.abs(value)
    density = jnp.exp(value * value * -0.5)
    t = 1.0 / (1.0 + (0.3275911 * 0.5**0.5) * size)
    series = t * (
        0.254829592
        + t * (-0.284496736 + t * (1.421413741 + t * (-1.453152027 + t * 1.061405429)))
    )
    tail = 0.5 * series * density
    phi = jnp.where(value >= 0, 1.0 - tail, tail)
    return (value * phi, phi + value * density * 0.3989422804014327)


def adamw_update(weight, gradient, first_old, second_old, rate_value, decay_value):
    first_new = beta_first * first_old + (1.0 - beta_first) * gradient
    second_new = beta_second * second_old + (1.0 - beta_second) * (gradient * gradient)
    first_hat = first_new / (1.0 - beta_first**STEP)
    second_hat = second_new / (1.0 - beta_second**STEP)
    moved = weight - rate_value * (
        first_hat / (jnp.sqrt(second_hat) + adam_epsilon) + decay_value * weight
    )
    return (moved, first_new, second_new)


def norm_rows(values):
    center = jnp.mean(values, axis=1, keepdims=True)
    spread = jnp.mean(values * values, axis=1, keepdims=True) - center * center
    scaled = lax.rsqrt(spread + norm_epsilon)
    return ((values - center) * scaled, scaled)


def norm_backward(grad_normed, normed, scaled, gain_row):
    local_grad = grad_normed * gain_row
    first = jnp.mean(local_grad, axis=1, keepdims=True)
    second = jnp.mean(local_grad * normed, axis=1, keepdims=True)
    return scaled * (local_grad - first - normed * second)


def in_order(col, first, second):
    return jnp.where(
        col == 0,
        jnp.concatenate([first, second], axis=-1),
        jnp.concatenate([second, first], axis=-1),
    )


def split_features(col, array):
    part = array.shape[-1] // 4
    quarters = [array[..., i * part : (i + 1) * part] for i in range(4)]
    own = [jnp.where(col == 0, quarters[2 * i], quarters[2 * i + 1]) for i in range(2)]
    other = [jnp.where(col == 0, quarters[2 * i + 1], quarters[2 * i]) for i in range(2)]
    return [own[0], other[0], own[1], other[1]]


def resident(array):
    zeros = (0,) * array.ndim
    return pl.BlockSpec(array.shape, lambda i, *_: zeros, pipeline_mode=pl.Buffered(1))


def column_block(rows, width):
    return pl.BlockSpec((rows, width), lambda i, *_: (0, i))


def side_blocks(rows, width, along, steps):
    def first(i, *_):
        at = jnp.minimum(i, steps // 2 - 1)
        return (0, at) if along == 1 else (at, 0)

    def second(i, *_):
        at = jnp.maximum(i - steps // 2, 0)
        return (0, at) if along == 1 else (at, 0)

    block = (rows, width)
    return [pl.BlockSpec(block, first)] * 2 + [pl.BlockSpec(block, second)] * 2


def side_weight(refs, steps, axis):
    own = jnp.concatenate([refs[0][...], refs[1][...]], axis=axis)
    other = jnp.concatenate([refs[2][...], refs[3][...]], axis=axis)
    return jnp.where(pl.program_id(0) < steps // 2, own, other)


def split_parts(col, array):
    part = array.shape[0] // 4
    quarters = [array[i * part : (i + 1) * part] for i in range(4)]
    own = [jnp.where(col == 0, quarters[2 * i], quarters[2 * i + 1]) for i in range(2)]
    other = [jnp.where(col == 0, quarters[2 * i + 1], quarters[2 * i]) for i in range(2)]
    return [own[0], other[0], own[1], other[1]]


def together_kernel(place, *refs):
    parts, out_ref = refs[:4], refs[4]
    part, tokens = parts[0].shape
    wide = [ref[...].astype(f32) for ref in parts]
    for half in range(2):
        first, second = wide[2 * half], wide[2 * half + 1]
        both = [jnp.where(place[0] == 0, first, second), jnp.where(place[0] == 0, second, first)]
        block = jnp.concatenate(both, axis=0)
        at = 2 * part * half
        out_ref[0:tokens, at : at + 2 * part] = block.T.astype(bf16)
    low = tokens - tokens % 16
    row = lax.broadcasted_iota(jnp.int32, (out_ref.shape[0] - low, 1), 0) + low
    out_ref[low:, :] = jnp.where(row < tokens, out_ref[low:, :].astype(f32), 0.0).astype(bf16)


def tokens_together(place, parts):
    part, tokens = parts[0].shape
    padded = -(-tokens // ROWS) * ROWS
    return pl.pallas_call(
        together_kernel,
        in_specs=[pl.BlockSpec(memory_space=pltpu.SMEM)]
        + [pl.BlockSpec(memory_space=pltpu.VMEM)] * 4,
        out_specs=pl.BlockSpec(memory_space=pltpu.VMEM),
        out_shape=jax.ShapeDtypeStruct((padded, 4 * part), bf16),
        compiler_params=pltpu.CompilerParams(vmem_limit_bytes=40 * 2**20),
        cost_estimate=pl.CostEstimate(
            flops=0, bytes_accessed=16 * tokens * part, transcendentals=0
        ),
        name="tokens_together",
    )(place, *parts)


def apart_kernel(place, *refs):
    parts, out_ref = refs[:4], refs[4]
    tokens = out_ref.shape[1] // 4
    for block in range(4):
        for distance in range(4):

            @pl.when((place[1] ^ block) == distance)
            def _():
                columns = slice(block * tokens, (block + 1) * tokens)
                out_ref[:, columns] = parts[distance][...].astype(f32)[:, :tokens]


def tokens_apart(place, tokens, parts):
    part = parts[0].shape[0]
    return pl.pallas_call(
        apart_kernel,
        in_specs=[pl.BlockSpec(memory_space=pltpu.SMEM)]
        + [pl.BlockSpec(memory_space=pltpu.VMEM)] * 4,
        out_specs=pl.BlockSpec(memory_space=pltpu.VMEM),
        out_shape=jax.ShapeDtypeStruct((part, 4 * tokens), f32),
        compiler_params=pltpu.CompilerParams(vmem_limit_bytes=40 * 2**20),
        cost_estimate=pl.CostEstimate(
            flops=0, bytes_accessed=4 * tokens * part * 6, transcendentals=0
        ),
        name="tokens_apart",
    )(place, *parts).T


def forward_kernel(*refs):
    resid_ref, params = refs[:2]
    weights = refs[2:6]
    h_ref, mixed_ref, out_ref, probs_ref, wide, gathered = refs[6:]
    rows = resid_ref.shape[0]
    images = rows // SEQ
    tokens = images * SEQ
    steps = pl.num_programs(0)

    @pl.when(pl.program_id(0) == 0)
    def _():
        for start in range(0, rows, BLOCK):
            block = slice(start, start + BLOCK)
            normed, _ = norm_rows(resid_ref[block, :].astype(f32))
            h_ref[block, :] = (normed * params[0:1, :] + params[1:2, :]).astype(bf16)

    weight = side_weight(weights, STEPS, 0)
    for start in range(0, rows, BLOCK):
        block = slice(start, start + BLOCK)
        mixed = dot(h_ref[block, :], weight).astype(bf16)
        mixed_ref[block, :] = mixed
        wide[block, :] = mixed.astype(f32)
    wide[rows:, :] = jnp.zeros((wide.shape[0] - rows, 384), f32)
    low_lane = lax.broadcasted_iota(jnp.int32, (1, 128), 1) < HEAD_DIM
    key_lane = lax.broadcasted_iota(jnp.int32, (1, KROWS), 1) < SEQ
    scale = HEAD_DIM ** (-0.5)
    for group in range(0, images, GROUPED):
        members = range(group, min(group + GROUPED, images))
        scores, values = [], []
        for image in members:
            start = image * SEQ
            block_a = wide[start : start + KROWS, 0:128]
            block_b = wide[start : start + KROWS, 128:256]
            block_c = wide[start : start + KROWS, 256:384]
            query_0 = jnp.where(low_lane, block_a[:QROWS] * scale, 0.0).astype(bf16)
            query_1 = jnp.where(low_lane, 0.0, block_b[:QROWS] * scale).astype(bf16)
            scores.append(dot(query_0, swap_halves(block_a).astype(bf16), ((1,), (1,))))
            scores.append(dot(query_1, swap_halves(block_c).astype(bf16), ((1,), (1,))))
            values += [block_b.astype(bf16), block_c.astype(bf16)]
        scores = [jnp.where(key_lane, score, -1e30) for score in scores]
        tops = [jnp.max(score, axis=1, keepdims=True) for score in scores]
        exponents = [jnp.exp(score - top) for score, top in zip(scores, tops)]
        totals = [jnp.sum(exponent, axis=1, keepdims=True) for exponent in exponents]
        probs = [(e * (1.0 / total)).astype(bf16) for e, total in zip(exponents, totals)]
        outs = [dot(prob, value) for prob, value in zip(probs, values)]
        for at, image in enumerate(members):
            start = image * SEQ
            probs_ref[0, image * 2] = probs[2 * at]
            probs_ref[0, image * 2 + 1] = probs[2 * at + 1]
            gathered[start : start + QROWS, :] = jnp.where(
                low_lane, outs[2 * at], outs[2 * at + 1]
            )
    gathered[tokens:, :] = jnp.zeros((gathered.shape[0] - tokens, 128), f32)
    out_ref[...] = gathered[0:rows, :].astype(bf16)


def attend_forward(resid, params, weights):
    rows, width = resid.shape
    images = rows // SEQ
    padded = -(-((images - 1) * SEQ + KROWS) // 16) * 16
    pair_probs = (STEPS, 2 * images, QROWS, KROWS)
    half_rows = weights[0].shape[0]
    return pl.pallas_call(
        forward_kernel,
        grid=(STEPS,),
        in_specs=[resident(resid), resident(params), *side_blocks(half_rows, 384, 1, STEPS)],
        out_specs=[
            pl.BlockSpec((rows, width), lambda i: (0, 0)),
            column_block(rows, 384),
            column_block(rows, 128),
            pl.BlockSpec((1, *pair_probs[1:]), lambda i: (i, 0, 0, 0)),
        ],
        out_shape=[
            jax.ShapeDtypeStruct((rows, width), bf16),
            jax.ShapeDtypeStruct((rows, STEPS * 384), bf16),
            jax.ShapeDtypeStruct((rows, STEPS * 128), bf16),
            jax.ShapeDtypeStruct(pair_probs, bf16),
        ],
        scratch_shapes=[pltpu.VMEM((padded, 384), f32), pltpu.VMEM((padded, 128), f32)],
        compiler_params=pltpu.CompilerParams(vmem_limit_bytes=54 * 2**20),
        cost_estimate=pl.CostEstimate(
            flops=20 * 10**9, bytes_accessed=rows * width * 20, transcendentals=10**6
        ),
        name="attend_forward",
    )(resid, params, *weights)


def backward_kernel(last, place, *refs):
    mixed_ref, probs_ref, grad_ref = refs[:3]
    weights = refs[3:5]
    if last:
        before_ref, middle_ref, resid_ref, params = refs[5:9]
        out_ref, out_parts, sums_ref = refs[9], refs[10:14], refs[14]
        wide, grad_wide, gathered, total = refs[15:]
    else:
        out_ref, total = refs[5:7]
        wide, grad_wide, gathered = refs[7:]
    rows = mixed_ref.shape[0]
    images = rows // SEQ
    tokens = images * SEQ
    wide[rows:, :] = jnp.zeros((wide.shape[0] - rows, 384), f32)
    wide[0:rows, :] = mixed_ref[...].astype(f32)
    grad_wide[0:rows, :] = grad_ref[...].astype(f32)
    low_lane = lax.broadcasted_iota(jnp.int32, (1, 128), 1) < HEAD_DIM
    query_row = lax.broadcasted_iota(jnp.int32, (QROWS, 128), 0) < SEQ
    scale = HEAD_DIM ** (-0.5)
    for group in range(0, images, GROUPED):
        members = range(group, min(group + GROUPED, images))
        grad_probs, grad_values, probs, swapped = [], [], [], []
        for image in members:
            start = image * SEQ
            block_a = wide[start : start + KROWS, 0:128]
            block_b = wide[start : start + KROWS, 128:256]
            block_c = wide[start : start + KROWS, 256:384]
            grad = jnp.where(query_row, grad_wide[start : start + QROWS, :], 0.0)
            grad_low = grad.astype(bf16)
            probs_0 = probs_ref[0, 2 * image]
            probs_1 = probs_ref[0, 2 * image + 1]
            probs += [probs_0, probs_1]
            part_0 = jnp.where(low_lane, grad, 0.0).astype(bf16)
            part_1 = jnp.where(low_lane, 0.0, grad).astype(bf16)
            grad_probs.append(dot(part_0, block_b.astype(bf16), ((1,), (1,))))
            grad_probs.append(dot(part_1, block_c.astype(bf16), ((1,), (1,))))
            grad_values.append(dot(probs_0, grad_low, ((0,), (0,))))
            grad_values.append(dot(probs_1, grad_low, ((0,), (0,))))
            swapped.append(
                [(swap_halves(block) * scale).astype(bf16) for block in (block_a, block_b, block_c)]
            )
        wide_probs = [prob.astype(f32) for prob in probs]
        inner = [
            jnp.sum(prob * grad, axis=1, keepdims=True)
            for prob, grad in zip(wide_probs, grad_probs)
        ]
        score_grads = [
            (prob * (grad - each)).astype(bf16)
            for prob, grad, each in zip(wide_probs, grad_probs, inner)
        ]
        for at, image in enumerate(members):
            start = image * SEQ
            swapped_a, swapped_b, swapped_c = swapped[at]
            score_0, score_1 = score_grads[2 * at : 2 * at + 2]
            grad_v0, grad_v1 = grad_values[2 * at : 2 * at + 2]
            grad_q0 = dot(score_0, swapped_a)
            grad_k0 = dot(score_0, swapped_a[:QROWS], ((0,), (0,)))
            grad_q1 = dot(score_1, swapped_c)
            grad_k1 = dot(score_1, swapped_b[:QROWS], ((0,), (0,)))
            block = slice(start, start + QROWS)
            gathered[block, 0:128] = jnp.where(low_lane, grad_q0, grad_k0[:QROWS])
            gathered[block, 128:256] = jnp.where(low_lane, grad_v0[:QROWS], grad_q1)
            gathered[block, 256:384] = jnp.where(low_lane, grad_k1[:QROWS], grad_v1[:QROWS])
    gathered[tokens:, :] = jnp.zeros((gathered.shape[0] - tokens, 384), f32)
    weight = jnp.concatenate([weights[0][...], weights[1][...]], axis=0)
    step = pl.program_id(0)

    @pl.when(step == 0)
    def _():
        total[...] = before_ref[...] if last else jnp.zeros_like(total)

    for start in range(0, rows, BLOCK):
        block = slice(start, start + BLOCK)
        grad_mixed = gathered[block, :].astype(bf16)
        out_ref[block, :] = grad_mixed
        total[block, :] += dot(grad_mixed, weight, ((1,), (1,)))

    if not last:
        return

    @pl.when(step == pl.num_programs(0) - 1)
    def _():
        gain = jnp.zeros((1, total.shape[1]), f32)
        shift = jnp.zeros((1, total.shape[1]), f32)
        for start in range(0, rows, BLOCK):
            block = slice(start, start + BLOCK)
            grad_one = total[block, :]
            normed, scaled = norm_rows(resid_ref[block, :].astype(f32))
            gain += jnp.sum(grad_one * normed, axis=0, keepdims=True)
            shift += jnp.sum(grad_one, axis=0, keepdims=True)
            total[block, :] = middle_ref[block, :] + norm_backward(
                grad_one, normed, scaled, params[0:1, :]
            )
        sums_ref[0:1, :] = gain
        sums_ref[1:2, :] = shift
        for part_ref, part in zip(out_parts, split_parts(place[0], total[...].T)):
            part_ref[...] = part.astype(bf16)


def attend_backward(place, mixed, probs, grad_attended, weights, side, rest):
    rows, width = grad_attended.shape
    images = rows // SEQ
    steps = STEPS // 2
    first = side * steps
    padded = -(-((images - 1) * SEQ + KROWS) // 16) * 16
    part = jax.ShapeDtypeStruct((width // 4, rows), bf16)
    sums = jax.ShapeDtypeStruct((2, width), f32)
    whole = jax.ShapeDtypeStruct((rows, width), f32)
    extra = [part] * 4 + [sums] if rest else [whole]
    scratch = [
        pltpu.VMEM((padded, 384), f32),
        pltpu.VMEM((padded, 128), f32),
        pltpu.VMEM((padded, 384), f32),
    ]
    if rest:
        scratch.append(pltpu.VMEM((rows, width), f32))
    weight_rows = weights[0].shape[0]
    return pl.pallas_call(
        lambda *refs: backward_kernel(bool(rest), *refs),
        grid_spec=pltpu.PrefetchScalarGridSpec(
            num_scalar_prefetch=1,
            grid=(steps,),
            in_specs=[
                pl.BlockSpec((rows, 384), lambda i, *_: (0, i + first)),
                pl.BlockSpec((1, *probs.shape[1:]), lambda i, *_: (i + first, 0, 0, 0)),
                pl.BlockSpec((rows, 128), lambda i, *_: (0, i + first)),
                *[pl.BlockSpec((weight_rows, 384), lambda i, *_: (0, i))] * 2,
                *[resident(each) for each in rest],
            ],
            out_specs=[
                column_block(rows, 384),
                *[pl.BlockSpec(each.shape, lambda i, *_: (0, 0)) for each in extra],
            ],
            scratch_shapes=scratch,
        ),
        out_shape=[jax.ShapeDtypeStruct((rows, steps * 384), bf16), *extra],
        compiler_params=pltpu.CompilerParams(vmem_limit_bytes=54 * 2**20),
        cost_estimate=pl.CostEstimate(
            flops=15 * 10**9, bytes_accessed=rows * width * 12, transcendentals=0
        ),
        name="attend_backward",
    )(place, mixed, probs, grad_attended, *weights[2 * side : 2 * side + 2], *rest)


def block_kernel(place, *refs):
    resid_ref, attended_ref, grad_ref, params = refs[:4]
    proj, expand, contract = refs[4:8], refs[8:12], refs[12:16]
    out_parts = refs[16:20]
    h_ref, hidden_ref, pre_ref, middle_ref, attended_grad_ref, sums_ref = refs[20:26]
    middle, output, grad_two = refs[26:]
    rows = resid_ref.shape[0]
    step = pl.program_id(0)
    blocks = [slice(start, start + BLOCK) for start in range(0, rows, BLOCK)]

    def proj_low():
        own = jnp.concatenate([proj[0][...], proj[1][...]], axis=1)
        return jnp.concatenate([own, jnp.concatenate([proj[2][...], proj[3][...]], axis=1)], axis=0)

    @pl.when(step == 0)
    def _():
        weight = proj_low()
        for block in blocks:
            value = resid_ref[block, :].astype(f32) + dot(attended_ref[block, :], weight)
            middle[block, :] = value
            output[block, :] = value
            grad_two[block, :] = jnp.zeros_like(value)
            normed, _ = norm_rows(value)
            h_ref[block, :] = (normed * params[2:3, :] + params[3:4, :]).astype(bf16)

    expand_low = side_weight(expand, STEPS, 0)
    contract_low = side_weight(contract, STEPS, 1)

    def products(block):
        return (
            dot(h_ref[block, :], expand_low),
            dot(grad_ref[block, :], contract_low, ((1,), (1,))),
        )

    ahead = products(blocks[0])
    for at, block in enumerate(blocks):
        before, grad_hidden = ahead
        if at + 1 < len(blocks):
            ahead = products(blocks[at + 1])
        value, slope = gelu_and_slope(before)
        hidden = value.astype(bf16)
        grad_pre = (grad_hidden * slope).astype(bf16)
        hidden_ref[block, :] = hidden
        pre_ref[block, :] = grad_pre
        output[block, :] += dot(hidden, contract_low)
        grad_two[block, :] += dot(grad_pre, expand_low, ((1,), (1,)))

    @pl.when(step == STEPS - 1)
    def _():
        weight = proj_low()
        gain = jnp.zeros((1, middle.shape[1]), f32)
        shift = jnp.zeros((1, middle.shape[1]), f32)
        for block in blocks:
            grad = grad_two[block, :]
            normed, scaled = norm_rows(middle[block, :])
            gain += jnp.sum(grad * normed, axis=0, keepdims=True)
            shift += jnp.sum(grad, axis=0, keepdims=True)
            grad_middle = grad_ref[block, :].astype(f32) + norm_backward(
                grad, normed, scaled, params[2:3, :]
            )
            middle_ref[block, :] = grad_middle
            attended_grad_ref[block, :] = dot(
                grad_middle.astype(bf16), weight, ((1,), (1,))
            ).astype(bf16)
        sums_ref[0:1, :] = gain
        sums_ref[1:2, :] = shift
        for part_ref, part in zip(out_parts, split_parts(place[0], output[...].T)):
            part_ref[...] = part.astype(bf16)


def block_middle(place, resid, attended, grad, params, proj, expand, contract):
    rows, width = resid.shape
    ff = 2 * expand[0].shape[1]
    chunk = ff // STEPS
    part = jax.ShapeDtypeStruct((width // 4, rows), bf16)
    narrow = jax.ShapeDtypeStruct((rows, width), bf16)
    broad = jax.ShapeDtypeStruct((rows, ff), bf16)
    wide = jax.ShapeDtypeStruct((rows, width), f32)
    sums = jax.ShapeDtypeStruct((2, width), f32)

    def fixed(shape):
        return pl.BlockSpec(shape.shape, lambda i, *_: (0, 0))

    return pl.pallas_call(
        block_kernel,
        grid_spec=pltpu.PrefetchScalarGridSpec(
            num_scalar_prefetch=1,
            grid=(STEPS,),
            in_specs=[
                *[resident(each) for each in (resid, attended, grad, params, *proj)],
                *side_blocks(expand[0].shape[0], chunk, 1, STEPS),
                *side_blocks(chunk, contract[0].shape[1], 0, STEPS),
            ],
            out_specs=[
                *[fixed(part)] * 4,
                fixed(narrow),
                column_block(rows, chunk),
                column_block(rows, chunk),
                fixed(wide),
                fixed(narrow),
                fixed(sums),
            ],
            scratch_shapes=[pltpu.VMEM((rows, width), f32)] * 3,
        ),
        out_shape=[*[part] * 4, narrow, broad, broad, wide, narrow, sums],
        compiler_params=pltpu.CompilerParams(vmem_limit_bytes=58 * 2**20),
        cost_estimate=pl.CostEstimate(
            flops=2 * rows * width * (4 * ff + 2 * width),
            bytes_accessed=rows * ff * 8,
            transcendentals=2 * rows * ff,
        ),
        name="block_middle",
    )(place, resid, attended, grad, params, *proj, *expand, *contract)


def adamw_kernel(place, weight, first, second, here, there, weight_out, first_out, second_out):
    x = place[2]
    mine = jnp.where(pl.program_id(0) // 4 == x, here[0].astype(f32), there[0].astype(f32))
    results = adamw_update(
        weight[...], mine, first[...], second[...], rate_matrix, decay_matrix
    )
    weight_out[...], first_out[...], second_out[...] = results


def adamw_pieces(place, weight, first, second, here, there):
    rows, width = weight.shape
    piece = pl.BlockSpec((rows // 8, width), lambda i, place: (i, 0))
    part = pl.BlockSpec((1, rows // 8, width), lambda i, place: ((i % 4) ^ place[3], 0, 0))
    return pl.pallas_call(
        adamw_kernel,
        grid_spec=pltpu.PrefetchScalarGridSpec(
            num_scalar_prefetch=1,
            grid=(8,),
            in_specs=[piece, piece, piece, part, part],
            out_specs=[piece] * 3,
        ),
        out_shape=[jax.ShapeDtypeStruct((rows, width), f32)] * 3,
        compiler_params=pltpu.CompilerParams(vmem_limit_bytes=40 * 2**20),
        cost_estimate=pl.CostEstimate(
            flops=20 * rows * width, bytes_accessed=28 * rows * width, transcendentals=0
        ),
        name="adamw_pieces",
    )(place, weight, first, second, here, there)


def local(
    tokens_in,
    out_grad,
    qkv_weight,
    proj_weight,
    expand_weight,
    contract_weight,
    norm_params,
    qkv_first,
    qkv_second,
    proj_first,
    proj_second,
    expand_first,
    expand_second,
    contract_first,
    contract_second,
    norm_first,
    norm_second,
):
    row = lax.axis_index("row")
    col = lax.axis_index("col")
    dp = lax.axis_index("dp")
    n_dp = lax.axis_size("dp")
    me = 2 * row + col
    place = jnp.stack([col, me, dp % 2, dp // 2]).astype(jnp.int32)
    tokens = tokens_in.shape[0] // 4
    part = tokens_in.shape[1]

    def swap(array, distance):
        if distance == 0:
            return array
        return lax.ppermute(array, GROUP, [(i, i ^ distance) for i in range(4)])

    def swap_dp(array, distance):
        return lax.ppermute(array, "dp", [(i, i ^ distance) for i in range(n_dp)])

    def swap_row(array):
        return swap(array, 2)

    def swap_col(array):
        return swap(array, 1)

    def token_blocks(array):
        return [lax.dynamic_slice(array, ((me ^ d) * tokens, 0), (tokens, part)) for d in range(4)]

    def swap_all(blocks):
        return [swap(block, d) for d, block in enumerate(blocks)]

    def ordered(bit, mine, partner):
        return jnp.where(
            bit == 0,
            jnp.concatenate([mine, partner], axis=0),
            jnp.concatenate([partner, mine], axis=0),
        )

    def dp_part(mine, count):
        rows = mine.shape[0] // count
        return lax.dynamic_slice_in_dim(mine, (dp % count) * rows, rows)

    def all_blocks(mine, partner):
        return [mine, partner, swap_col(mine), swap_col(partner)]

    resid_parts = swap_all(token_blocks(tokens_in))
    params = [swap(norm_params, d) for d in range(4)]
    params = jnp.concatenate(
        [in_order(col, params[0], params[1]), in_order(col, params[2], params[3])], axis=1
    )
    x, z = dp % 2, dp // 2
    qkv_mine = qkv_weight.astype(bf16)
    qkv_got = swap_row(dp_part(qkv_mine, 2))
    expand_mine = expand_weight.astype(bf16)
    contract_mine = contract_weight.astype(bf16)
    proj_mine = proj_weight.astype(bf16)

    resid_parts, qkv_got, *sends = lax.optimization_barrier(
        (
            resid_parts,
            qkv_got,
            dp_part(expand_mine, 4),
            dp_part(contract_mine, 4),
            dp_part(proj_mine, 2),
        )
    )
    qkv_next = swap_dp(qkv_got, 1)
    expand_got, contract_got, proj_got = [swap_row(each) for each in sends]
    qkv_got, qkv_next, expand_got, contract_got, proj_got, grad_blocks = lax.optimization_barrier(
        (qkv_got, qkv_next, expand_got, contract_got, proj_got, token_blocks(out_grad))
    )
    qkv_low = all_blocks(qkv_mine, ordered(x, qkv_got, qkv_next))
    quarters = [[each, swap_dp(each, 1), swap_dp(each, 2)] for each in (expand_got, contract_got)]
    proj_next = swap_dp(proj_got, 1)
    grad_parts = swap_all(grad_blocks)
    resid = tokens_together(place, [each.T for each in resid_parts])
    h_one, mixed, attended, probs = attend_forward(resid, params, qkv_low)
    attended, quarters, proj_next, grad_parts = lax.optimization_barrier(
        (attended, quarters, proj_next, grad_parts)
    )
    expand_row, contract_row = [
        ordered(
            z % 2,
            ordered(x, each[0], each[1]),
            ordered(x, each[2], swap_dp(each[2], 1)),
        )
        for each in quarters
    ]
    proj_low = all_blocks(proj_mine, ordered(x, proj_got, proj_next))
    expand_low = all_blocks(expand_mine, expand_row)
    contract_low = all_blocks(contract_mine, contract_row)
    grad_low = tokens_together(place, [each.T for each in grad_parts])
    outs = block_middle(place, resid, attended, grad_low, params, proj_low, expand_low, contract_low)
    output_parts = outs[:4]
    h_two, hidden, grad_pre, grad_middle, grad_attended, sums_two = outs[4:]

    def halves(array, axis):
        size = array.shape[axis] // 2
        return (
            lax.slice_in_dim(array, 0, size, axis=axis),
            lax.slice_in_dim(array, size, 2 * size, axis=axis),
        )

    def over_col(left, right, received):
        total = dot(left, right, ((0,), (0,))) + received.astype(f32)
        return total.astype(bf16)

    def split_x(array, axis):
        size = array.shape[axis] // 2
        kept = lax.dynamic_slice_in_dim(array, x * size, size, axis)
        return kept, lax.dynamic_slice_in_dim(array, (1 - x) * size, size, axis)

    def add(kept, received):
        return (kept.astype(f32) + received.astype(f32)).astype(bf16)

    def over_z(total):
        rows = total.shape[0] // 4
        pieces = [lax.dynamic_slice_in_dim(total, (z ^ d) * rows, rows) for d in range(4)]
        return [pieces[0]] + [swap_dp(pieces[d], 2 * d) for d in range(1, 4)]

    def sum_z(pieces):
        return sum(piece.astype(f32) for piece in pieces).astype(bf16)

    def gather_z(mine):
        return [mine] + [swap_dp(mine, 2 * d) for d in range(1, 4)]

    def gather_x(pieces):
        here = jnp.stack(pieces)
        return here, swap_dp(here, 1)

    hidden_own, hidden_other = halves(hidden, 1)
    pre_own, pre_other = halves(grad_pre, 1)
    attended_own, attended_other = halves(attended, 1)
    branch = grad_middle.astype(bf16)
    contract_away = swap_col(dot(hidden_other, grad_low, ((0,), (0,))).astype(bf16))
    expand_away = swap_col(dot(h_two, pre_other, ((0,), (0,))).astype(bf16))
    proj_away = swap_col(dot(attended_other, branch, ((0,), (0,))).astype(bf16))
    contract_sum = over_col(hidden_own, grad_low, contract_away)
    expand_sum = over_col(h_two, pre_own, expand_away)
    proj_sum = over_col(attended_own, branch, proj_away)
    contract_sum, expand_sum, proj_sum, grad_attended = lax.optimization_barrier(
        (contract_sum, expand_sum, proj_sum, grad_attended)
    )
    contract_kept, contract_away = halves(contract_sum, 1)
    proj_kept, proj_away = halves(proj_sum, 1)
    expand_sum = expand_sum.reshape(2, expand_sum.shape[0] // 2, expand_sum.shape[1])
    expand_kept, expand_away = split_x(expand_sum, 1)
    contract_got, expand_got, proj_got = (
        swap_row(contract_away),
        swap_dp(expand_away, 1),
        swap_row(proj_away),
    )
    mixed_other, grad_other = attend_backward(
        place, mixed, probs, grad_attended, qkv_low, 1, []
    )
    contract_got, expand_got, proj_got, mixed_other, grad_other = lax.optimization_barrier(
        (contract_got, expand_got, proj_got, mixed_other, grad_other)
    )
    contract_kept, contract_away = split_x(add(contract_kept, contract_got), 0)
    proj_kept, proj_away = split_x(add(proj_kept, proj_got), 0)
    expand_kept, expand_away = add(expand_kept, expand_got)
    qkv_away = dot(h_one, mixed_other, ((0,), (0,))).astype(bf16)
    contract_away, proj_away, expand_away, qkv_away, grad_other = lax.optimization_barrier(
        (contract_away, proj_away, expand_away, qkv_away, grad_other)
    )
    contract_got, expand_got, proj_got, qkv_got = (
        swap_dp(contract_away, 1),
        swap_row(expand_away),
        swap_dp(proj_away, 1),
        swap_col(qkv_away),
    )
    outs = attend_backward(
        place, mixed, probs, grad_attended, qkv_low, 0, [grad_other, grad_middle, resid, params]
    )
    mixed_own, input_parts, sums_one = outs[0], outs[1:5], outs[5]
    contract_got, expand_got, proj_got, qkv_got, mixed_own = lax.optimization_barrier(
        (contract_got, expand_got, proj_got, qkv_got, mixed_own)
    )
    qkv_kept, qkv_away = halves(over_col(h_one, mixed_own, qkv_got), 0)
    contract_sum = add(contract_kept, contract_got)
    expand_sum = add(expand_kept, expand_got)
    proj_sum = add(proj_kept, proj_got)
    qkv_away, contract_sum, expand_sum, proj_sum = lax.optimization_barrier(
        (qkv_away, contract_sum, expand_sum, proj_sum)
    )
    qkv_got = swap_row(qkv_away)
    if n_dp == 8:
        first_pieces = [over_z(each) for each in (contract_sum, expand_sum, proj_sum)]
        first_pieces, qkv_got, output_parts, input_parts = lax.optimization_barrier(
            (first_pieces, qkv_got, output_parts, input_parts)
        )
        qkv_kept, qkv_away = split_x(add(qkv_kept, qkv_got), 0)
        qkv_got = swap_dp(qkv_away, 1)
        mine = [sum_z(each) for each in first_pieces]
        mine, qkv_away = lax.optimization_barrier((mine, qkv_away))
        gathered = [gather_z(each) for each in mine]
        qkv_pieces = over_z(add(qkv_kept, qkv_got))
        gathered, qkv_pieces = lax.optimization_barrier((gathered, qkv_pieces))
        contract_sum, expand_sum, proj_sum = [gather_x(each) for each in gathered]
        qkv_sum = gather_x(gather_z(sum_z(qkv_pieces)))
    else:
        def whole(total):
            total = lax.psum(total, tuple(["dp"]), axis_index_groups=same_x)
            other = swap_dp(total, 1)
            return ordered(x, total, other).astype(f32)

        same_x = [[i for i in range(n_dp) if i % 2 == bit] for bit in range(2)]
        contract_sum, expand_sum, proj_sum = [
            whole(each) for each in (contract_sum, expand_sum, proj_sum)
        ]
        qkv_kept, qkv_away = split_x(add(qkv_kept, qkv_got), 0)
        qkv_sum = whole(add(qkv_kept, swap_dp(qkv_away, 1)))

    norm_parts = split_features(col, jnp.concatenate([sums_one, sums_two], axis=0))
    norm_sum = norm_parts[0] + sum(swap(norm_parts[d], d) for d in range(1, 4))
    if n_dp == 8:
        for d in (1, 2, 4):
            norm_sum = norm_sum + swap_dp(norm_sum, d)
    else:
        norm_sum = lax.psum(norm_sum, "dp")

    results = (
        tokens_apart(place, tokens, swap_all(output_parts)),
        tokens_apart(place, tokens, swap_all(input_parts)),
    )
    for weight, gradient, first, second in (
        (qkv_weight, qkv_sum, qkv_first, qkv_second),
        (proj_weight, proj_sum, proj_first, proj_second),
        (expand_weight, expand_sum, expand_first, expand_second),
        (contract_weight, contract_sum, contract_first, contract_second),
    ):
        if n_dp == 8:
            results += tuple(adamw_pieces(place, weight, first, second, *gradient))
        else:
            results += adamw_update(weight, gradient, first, second, rate_matrix, decay_matrix)
    return results + adamw_update(norm_params, norm_sum, norm_first, norm_second, rate_norm, 0.0)


def solution(mesh):
    tokens = P("dp", ("row", "col"))
    one = P("row", "col")
    two = P("col", "row")
    norm = P(None, ("row", "col"))
    in_specs = (tokens, tokens, one, two, one, two, norm)
    in_specs += (one, one, two, two, one, one, two, two, norm, norm)
    out_specs = (tokens, tokens) + (one,) * 3 + (two,) * 3 + (one,) * 3 + (two,) * 3 + (norm,) * 3
    return jax.shard_map(local, mesh=mesh, in_specs=in_specs, out_specs=out_specs, check_vma=False)
```

```python
import jax
import jax.numpy as jnp
from jax import lax
from jax.experimental import pallas as pl
from jax.experimental.pallas import tpu as pltpu
from jax.sharding import PartitionSpec as P

HEAD_DIM = 64
SEQ = 197
QROWS = 208
KROWS = 256
STEP = 10
ROWS = 1200
BLOCK = 608
STEPS = 6
GROUPED = 2
WIDE = 384
CHUNK = 768
MLP_ROWS = 1536

norm_epsilon = 1e-06
beta_first = 0.9
beta_second = 0.999
adam_epsilon = 1e-08
rate_matrix = 0.1
rate_norm = 0.5
decay_matrix = 0.05

GROUP = ("row", "col")
bf16 = jnp.bfloat16
f32 = jnp.float32


def dot(left, right, dims=((1,), (0,))):
    return lax.dot_general(left, right, (dims, ((), ())), preferred_element_type=f32)


def swap_halves(block):
    return jnp.concatenate([block[:, HEAD_DIM:], block[:, :HEAD_DIM]], axis=1)


def gelu_and_slope(value):
    size = jnp.abs(value)
    density = jnp.exp(value * value * -0.5)
    base = 1.0 + (0.3275911 * 0.5**0.5) * size
    t = pl.reciprocal(base, approx=True)
    t = t * (2.0 - base * t)
    series = t * (
        0.254829592
        + t * (-0.284496736 + t * (1.421413741 + t * (-1.453152027 + t * 1.061405429)))
    )
    tail = 0.5 * series * density
    phi = jnp.where(value >= 0, 1.0 - tail, tail)
    return (value * phi, phi + value * density * 0.3989422804014327)


def adamw_update(weight, gradient, first_old, second_old, rate_value, decay_value):
    first_new = beta_first * first_old + (1.0 - beta_first) * gradient
    second_new = beta_second * second_old + (1.0 - beta_second) * (gradient * gradient)
    first_hat = first_new / (1.0 - beta_first**STEP)
    second_hat = second_new / (1.0 - beta_second**STEP)
    moved = weight - rate_value * (
        first_hat / (jnp.sqrt(second_hat) + adam_epsilon) + decay_value * weight
    )
    return (moved, first_new, second_new)


def row_blocks(rows, size=BLOCK):
    return [slice(start, min(start + size, rows)) for start in range(0, rows, size)]


def norm_rows(values):
    center = jnp.mean(values, axis=1, keepdims=True)
    spread = jnp.mean(values * values, axis=1, keepdims=True) - center * center
    scaled = lax.rsqrt(spread + norm_epsilon)
    return ((values - center) * scaled, scaled)


def norm_backward(grad_normed, normed, scaled, gain_row):
    local_grad = grad_normed * gain_row
    first = jnp.mean(local_grad, axis=1, keepdims=True)
    second = jnp.mean(local_grad * normed, axis=1, keepdims=True)
    return scaled * (local_grad - first - normed * second)


def in_order(col, first, second):
    return jnp.where(
        col == 0,
        jnp.concatenate([first, second], axis=-1),
        jnp.concatenate([second, first], axis=-1),
    )


def split_features(col, array):
    part = array.shape[-1] // 4
    quarters = [array[..., i * part : (i + 1) * part] for i in range(4)]
    own = [jnp.where(col == 0, quarters[2 * i], quarters[2 * i + 1]) for i in range(2)]
    other = [jnp.where(col == 0, quarters[2 * i + 1], quarters[2 * i]) for i in range(2)]
    return [own[0], other[0], own[1], other[1]]


def resident(array):
    zeros = (0,) * array.ndim
    return pl.BlockSpec(array.shape, lambda i, *_: zeros, pipeline_mode=pl.Buffered(1))


def column_block(rows, width):
    return pl.BlockSpec((rows, width), lambda i, *_: (0, i))


def side_blocks(rows, width, along, steps):
    def first(i, *_):
        at = jnp.minimum(i, steps // 2 - 1)
        return (0, at) if along == 1 else (at, 0)

    def second(i, *_):
        at = jnp.maximum(i - steps // 2, 0)
        return (0, at) if along == 1 else (at, 0)

    block = (rows, width)
    return [pl.BlockSpec(block, first)] * 2 + [pl.BlockSpec(block, second)] * 2


def side_weight(refs, steps, axis):
    own = jnp.concatenate([refs[0][...], refs[1][...]], axis=axis)
    other = jnp.concatenate([refs[2][...], refs[3][...]], axis=axis)
    return jnp.where(pl.program_id(0) < steps // 2, own, other)


def split_parts(col, array):
    part = array.shape[0] // 4
    quarters = [array[i * part : (i + 1) * part] for i in range(4)]
    own = [jnp.where(col == 0, quarters[2 * i], quarters[2 * i + 1]) for i in range(2)]
    other = [jnp.where(col == 0, quarters[2 * i + 1], quarters[2 * i]) for i in range(2)]
    return [own[0], other[0], own[1], other[1]]


def together_kernel(place, *refs):
    parts, out_ref = refs[:4], refs[4]
    part, tokens = parts[0].shape
    wide = [ref[...].astype(f32) for ref in parts]
    for half in range(2):
        first, second = wide[2 * half], wide[2 * half + 1]
        both = [jnp.where(place[0] == 0, first, second), jnp.where(place[0] == 0, second, first)]
        block = jnp.concatenate(both, axis=0)
        at = 2 * part * half
        out_ref[0:tokens, at : at + 2 * part] = block.T.astype(bf16)
    low = tokens - tokens % 16
    row = lax.broadcasted_iota(jnp.int32, (out_ref.shape[0] - low, 1), 0) + low
    out_ref[low:, :] = jnp.where(row < tokens, out_ref[low:, :].astype(f32), 0.0).astype(bf16)


def tokens_together(place, parts):
    part, tokens = parts[0].shape
    padded = -(-tokens // ROWS) * ROWS
    return pl.pallas_call(
        together_kernel,
        in_specs=[pl.BlockSpec(memory_space=pltpu.SMEM)]
        + [pl.BlockSpec(memory_space=pltpu.VMEM)] * 4,
        out_specs=pl.BlockSpec(memory_space=pltpu.VMEM),
        out_shape=jax.ShapeDtypeStruct((padded, 4 * part), bf16),
        compiler_params=pltpu.CompilerParams(vmem_limit_bytes=40 * 2**20),
        cost_estimate=pl.CostEstimate(
            flops=0, bytes_accessed=16 * tokens * part, transcendentals=0
        ),
        name="tokens_together",
    )(place, *parts)


def apart_kernel(place, *refs):
    parts, out_ref = refs[:4], refs[4]
    tokens = out_ref.shape[1] // 4
    for block in range(4):
        for distance in range(4):

            @pl.when((place[1] ^ block) == distance)
            def _():
                columns = slice(block * tokens, (block + 1) * tokens)
                out_ref[:, columns] = parts[distance][...].astype(f32)[:, :tokens]


def tokens_apart(place, tokens, parts):
    part = parts[0].shape[0]
    return pl.pallas_call(
        apart_kernel,
        in_specs=[pl.BlockSpec(memory_space=pltpu.SMEM)]
        + [pl.BlockSpec(memory_space=pltpu.VMEM)] * 4,
        out_specs=pl.BlockSpec(memory_space=pltpu.VMEM),
        out_shape=jax.ShapeDtypeStruct((part, 4 * tokens), f32),
        compiler_params=pltpu.CompilerParams(vmem_limit_bytes=40 * 2**20),
        cost_estimate=pl.CostEstimate(
            flops=0, bytes_accessed=4 * tokens * part * 6, transcendentals=0
        ),
        name="tokens_apart",
    )(place, *parts).T


def forward_kernel(*refs):
    resid_ref, params = refs[:2]
    weights = refs[2:6]
    h_ref, mixed_ref, out_ref, probs_ref, wide, gathered = refs[6:]
    rows = resid_ref.shape[0]
    images = rows // SEQ
    tokens = images * SEQ
    steps = pl.num_programs(0)

    @pl.when(pl.program_id(0) == 0)
    def _():
        for block in row_blocks(rows):
            normed, _ = norm_rows(resid_ref[block, :].astype(f32))
            h_ref[block, :] = (normed * params[0:1, :] + params[1:2, :]).astype(bf16)

    weight = side_weight(weights, STEPS, 0)
    for block in row_blocks(rows):
        mixed = dot(h_ref[block, :], weight).astype(bf16)
        mixed_ref[block, :] = mixed
        wide[block, :] = mixed.astype(f32)
    wide[rows:, :] = jnp.zeros((wide.shape[0] - rows, 384), f32)
    low_lane = lax.broadcasted_iota(jnp.int32, (1, 128), 1) < HEAD_DIM
    key_lane = lax.broadcasted_iota(jnp.int32, (1, KROWS), 1) < SEQ
    scale = HEAD_DIM ** (-0.5)
    for group in range(0, images, GROUPED):
        members = range(group, min(group + GROUPED, images))
        scores, values = [], []
        for image in members:
            start = image * SEQ
            block_a = wide[start : start + KROWS, 0:128]
            block_b = wide[start : start + KROWS, 128:256]
            block_c = wide[start : start + KROWS, 256:384]
            query_0 = jnp.where(low_lane, block_a[:QROWS] * scale, 0.0).astype(bf16)
            query_1 = jnp.where(low_lane, 0.0, block_b[:QROWS] * scale).astype(bf16)
            scores.append(dot(query_0, swap_halves(block_a).astype(bf16), ((1,), (1,))))
            scores.append(dot(query_1, swap_halves(block_c).astype(bf16), ((1,), (1,))))
            values += [block_b.astype(bf16), block_c.astype(bf16)]
        scores = [jnp.where(key_lane, score, -1e30) for score in scores]
        tops = [jnp.max(score, axis=1, keepdims=True) for score in scores]
        exponents = [jnp.exp(score - top) for score, top in zip(scores, tops)]
        totals = [jnp.sum(exponent, axis=1, keepdims=True) for exponent in exponents]
        probs = [(e * (1.0 / total)).astype(bf16) for e, total in zip(exponents, totals)]
        outs = [dot(prob, value) for prob, value in zip(probs, values)]
        for at, image in enumerate(members):
            start = image * SEQ
            probs_ref[0, image * 2] = probs[2 * at]
            probs_ref[0, image * 2 + 1] = probs[2 * at + 1]
            gathered[start : start + QROWS, :] = jnp.where(
                low_lane, outs[2 * at], outs[2 * at + 1]
            )
    gathered[tokens:, :] = jnp.zeros((gathered.shape[0] - tokens, 128), f32)
    out_ref[...] = gathered[0:rows, :].astype(bf16)


def attend_forward(resid, params, weights):
    rows, width = resid.shape
    images = rows // SEQ
    padded = -(-((images - 1) * SEQ + KROWS) // 16) * 16
    pair_probs = (STEPS, 2 * images, QROWS, KROWS)
    half_rows = weights[0].shape[0]
    return pl.pallas_call(
        forward_kernel,
        grid=(STEPS,),
        in_specs=[resident(resid), resident(params), *side_blocks(half_rows, 384, 1, STEPS)],
        out_specs=[
            pl.BlockSpec((rows, width), lambda i: (0, 0)),
            column_block(rows, 384),
            column_block(rows, 128),
            pl.BlockSpec((1, *pair_probs[1:]), lambda i: (i, 0, 0, 0)),
        ],
        out_shape=[
            jax.ShapeDtypeStruct((rows, width), bf16),
            jax.ShapeDtypeStruct((rows, STEPS * 384), bf16),
            jax.ShapeDtypeStruct((rows, STEPS * 128), bf16),
            jax.ShapeDtypeStruct(pair_probs, bf16),
        ],
        scratch_shapes=[pltpu.VMEM((padded, 384), f32), pltpu.VMEM((padded, 128), f32)],
        compiler_params=pltpu.CompilerParams(vmem_limit_bytes=48 * 2**20),
        cost_estimate=pl.CostEstimate(
            flops=20 * 10**9, bytes_accessed=rows * width * 20, transcendentals=10**6
        ),
        name="attend_forward",
    )(resid, params, *weights)


def backward_kernel(last, place, *refs):
    mixed_ref, probs_ref, grad_ref = refs[:3]
    weights = refs[3:5]
    if last:
        before_ref, middle_ref, resid_ref, params = refs[5:9]
        out_ref, out_parts, sums_ref = refs[9], refs[10:14], refs[14]
        wide, grad_wide, gathered, total = refs[15:]
    else:
        out_ref, total = refs[5:7]
        wide, grad_wide, gathered = refs[7:]
    rows = mixed_ref.shape[0]
    images = rows // SEQ
    tokens = images * SEQ
    wide[rows:, :] = jnp.zeros((wide.shape[0] - rows, 384), f32)
    wide[0:rows, :] = mixed_ref[...].astype(f32)
    grad_wide[0:rows, :] = grad_ref[...].astype(f32)
    low_lane = lax.broadcasted_iota(jnp.int32, (1, 128), 1) < HEAD_DIM
    query_row = lax.broadcasted_iota(jnp.int32, (QROWS, 128), 0) < SEQ
    scale = HEAD_DIM ** (-0.5)
    for group in range(0, images, GROUPED):
        members = range(group, min(group + GROUPED, images))
        grad_probs, grad_values, probs, swapped = [], [], [], []
        for image in members:
            start = image * SEQ
            block_a = wide[start : start + KROWS, 0:128]
            block_b = wide[start : start + KROWS, 128:256]
            block_c = wide[start : start + KROWS, 256:384]
            grad = jnp.where(query_row, grad_wide[start : start + QROWS, :], 0.0)
            grad_low = grad.astype(bf16)
            probs_0 = probs_ref[0, 2 * image]
            probs_1 = probs_ref[0, 2 * image + 1]
            probs += [probs_0, probs_1]
            part_0 = jnp.where(low_lane, grad, 0.0).astype(bf16)
            part_1 = jnp.where(low_lane, 0.0, grad).astype(bf16)
            grad_probs.append(dot(part_0, block_b.astype(bf16), ((1,), (1,))))
            grad_probs.append(dot(part_1, block_c.astype(bf16), ((1,), (1,))))
            grad_values.append(dot(probs_0, grad_low, ((0,), (0,))))
            grad_values.append(dot(probs_1, grad_low, ((0,), (0,))))
            swapped.append(
                [(swap_halves(block) * scale).astype(bf16) for block in (block_a, block_b, block_c)]
            )
        wide_probs = [prob.astype(f32) for prob in probs]
        inner = [
            jnp.sum(prob * grad, axis=1, keepdims=True)
            for prob, grad in zip(wide_probs, grad_probs)
        ]
        score_grads = [
            (prob * (grad - each)).astype(bf16)
            for prob, grad, each in zip(wide_probs, grad_probs, inner)
        ]
        for at, image in enumerate(members):
            start = image * SEQ
            swapped_a, swapped_b, swapped_c = swapped[at]
            score_0, score_1 = score_grads[2 * at : 2 * at + 2]
            grad_v0, grad_v1 = grad_values[2 * at : 2 * at + 2]
            grad_q0 = dot(score_0, swapped_a)
            grad_k0 = dot(score_0, swapped_a[:QROWS], ((0,), (0,)))
            grad_q1 = dot(score_1, swapped_c)
            grad_k1 = dot(score_1, swapped_b[:QROWS], ((0,), (0,)))
            block = slice(start, start + QROWS)
            gathered[block, 0:128] = jnp.where(low_lane, grad_q0, grad_k0[:QROWS])
            gathered[block, 128:256] = jnp.where(low_lane, grad_v0[:QROWS], grad_q1)
            gathered[block, 256:384] = jnp.where(low_lane, grad_k1[:QROWS], grad_v1[:QROWS])
    gathered[tokens:, :] = jnp.zeros((gathered.shape[0] - tokens, 384), f32)
    weight = jnp.concatenate([weights[0][...], weights[1][...]], axis=0)
    step = pl.program_id(0)

    @pl.when(step == 0)
    def _():
        total[...] = before_ref[...] if last else jnp.zeros_like(total)

    for block in row_blocks(rows):
        grad_mixed = gathered[block, :].astype(bf16)
        out_ref[block, :] = grad_mixed
        total[block, :] += dot(grad_mixed, weight, ((1,), (1,)))

    if not last:
        return

    @pl.when(step == pl.num_programs(0) - 1)
    def _():
        gain = jnp.zeros((1, total.shape[1]), f32)
        shift = jnp.zeros((1, total.shape[1]), f32)
        for block in row_blocks(rows):
            grad_one = total[block, :]
            normed, scaled = norm_rows(resid_ref[block, :].astype(f32))
            gain += jnp.sum(grad_one * normed, axis=0, keepdims=True)
            shift += jnp.sum(grad_one, axis=0, keepdims=True)
            total[block, :] = middle_ref[block, :] + norm_backward(
                grad_one, normed, scaled, params[0:1, :]
            )
        sums_ref[0:1, :] = gain
        sums_ref[1:2, :] = shift
        for part_ref, part in zip(out_parts, split_parts(place[0], total[...].T)):
            part_ref[...] = part.astype(bf16)


def attend_backward(place, mixed, probs, grad_attended, weights, side, rest):
    rows, width = grad_attended.shape
    images = rows // SEQ
    steps = STEPS // 2
    first = side * steps
    padded = -(-((images - 1) * SEQ + KROWS) // 16) * 16
    part = jax.ShapeDtypeStruct((width // 4, rows), bf16)
    sums = jax.ShapeDtypeStruct((2, width), f32)
    whole = jax.ShapeDtypeStruct((rows, width), f32)
    extra = [part] * 4 + [sums] if rest else [whole]
    scratch = [
        pltpu.VMEM((padded, 384), f32),
        pltpu.VMEM((padded, 128), f32),
        pltpu.VMEM((padded, 384), f32),
    ]
    if rest:
        scratch.append(pltpu.VMEM((rows, width), f32))
    weight_rows = weights[0].shape[0]
    return pl.pallas_call(
        lambda *refs: backward_kernel(bool(rest), *refs),
        grid_spec=pltpu.PrefetchScalarGridSpec(
            num_scalar_prefetch=1,
            grid=(steps,),
            in_specs=[
                pl.BlockSpec((rows, 384), lambda i, *_: (0, i + first)),
                pl.BlockSpec((1, *probs.shape[1:]), lambda i, *_: (i + first, 0, 0, 0)),
                pl.BlockSpec((rows, 128), lambda i, *_: (0, i + first)),
                *[pl.BlockSpec((weight_rows, 384), lambda i, *_: (0, i))] * 2,
                *[resident(each) for each in rest],
            ],
            out_specs=[
                column_block(rows, 384),
                *[pl.BlockSpec(each.shape, lambda i, *_: (0, 0)) for each in extra],
            ],
            scratch_shapes=scratch,
        ),
        out_shape=[jax.ShapeDtypeStruct((rows, steps * 384), bf16), *extra],
        compiler_params=pltpu.CompilerParams(vmem_limit_bytes=48 * 2**20),
        name="attend_backward",
    )(place, mixed, probs, grad_attended, *weights[2 * side : 2 * side + 2], *rest)


def block_kernel(place, *refs):
    resid_ref, attended_ref, grad_ref, params = refs[:4]
    expand, contract, proj = refs[4:8], refs[8:12], refs[12:16]
    out_parts = refs[16:20]
    h_ref, hidden_ref, pre_ref, middle_ref, attended_grad_ref, sums_ref = refs[20:26]
    output, grad_two = refs[26:]
    middle = middle_ref
    rows = resid_ref.shape[0]
    step = pl.program_id(0)
    blocks = row_blocks(rows, 400)

    def proj_low():
        own = jnp.concatenate([proj[0][...], proj[1][...]], axis=1)
        return jnp.concatenate([own, jnp.concatenate([proj[2][...], proj[3][...]], axis=1)], axis=0)

    @pl.when(step == 0)
    def _():
        weight = proj_low()
        for block in blocks:
            value = resid_ref[block, :].astype(f32) + dot(attended_ref[block, :], weight)
            middle[block, :] = value
            output[block, :] = value
            grad_two[block, :] = jnp.zeros_like(value)
            normed, _ = norm_rows(value)
            h_ref[block, :] = (normed * params[2:3, :] + params[3:4, :]).astype(bf16)

    own_side = step < pl.num_programs(0) // 2

    def expand_side(own, other):
        upper = jnp.concatenate([own[at : at + WIDE, :] for at in range(0, CHUNK, WIDE)], axis=1)
        lower = jnp.concatenate([other[at : at + WIDE, :] for at in range(0, CHUNK, WIDE)], axis=1)
        return jnp.concatenate([upper, lower], axis=0)

    expand_low = jnp.where(
        own_side, expand_side(expand[0], expand[1]), expand_side(expand[2], expand[3])
    )
    contract_low = jnp.where(
        own_side,
        jnp.concatenate([contract[0][...], contract[1][...]], axis=1),
        jnp.concatenate([contract[2][...], contract[3][...]], axis=1),
    )

    def products(block):
        return (
            dot(h_ref[block, :], expand_low),
            dot(grad_ref[block, :], contract_low, ((1,), (1,))),
        )

    ahead = products(blocks[0])
    for at, block in enumerate(blocks):
        before, grad_hidden = ahead
        if at + 1 < len(blocks):
            ahead = products(blocks[at + 1])
        value, slope = gelu_and_slope(before)
        hidden = value.astype(bf16)
        grad_pre = (grad_hidden * slope).astype(bf16)
        hidden_ref[block, :] = hidden
        pre_ref[block, :] = grad_pre
        output[block, :] += dot(hidden, contract_low)
        grad_two[block, :] += dot(grad_pre, expand_low, ((1,), (1,)))

    @pl.when(step == pl.num_programs(0) - 1)
    def _():
        weight = proj_low()
        gain = jnp.zeros((1, middle.shape[1]), f32)
        shift = jnp.zeros((1, middle.shape[1]), f32)
        for block in blocks:
            grad = grad_two[block, :]
            normed, scaled = norm_rows(middle[block, :])
            gain += jnp.sum(grad * normed, axis=0, keepdims=True)
            shift += jnp.sum(grad, axis=0, keepdims=True)
            grad_middle = grad_ref[block, :].astype(f32) + norm_backward(
                grad, normed, scaled, params[2:3, :]
            )
            middle_ref[block, :] = grad_middle
            attended_grad_ref[block, :] = dot(
                grad_middle.astype(bf16), weight, ((1,), (1,))
            ).astype(bf16)
        sums_ref[0:1, :] = gain
        sums_ref[1:2, :] = shift
        for part_ref, part in zip(out_parts, split_parts(place[0], output[...].T)):
            part_ref[...] = part.astype(bf16)


def chunk_blocks(first, steps):
    def own(i, *_):
        return (first + jnp.minimum(i, steps // 2 - 1), 0)

    def other(i, *_):
        return (first + jnp.maximum(i - steps // 2, 0), 0)

    return [pl.BlockSpec((CHUNK, WIDE), own)] * 2 + [pl.BlockSpec((CHUNK, WIDE), other)] * 2


def block_middle(place, resid, attended, grad, params, weights):
    rows, width = resid.shape
    ff = 2 * MLP_ROWS
    chunk = CHUNK
    steps = ff // CHUNK
    part = jax.ShapeDtypeStruct((width // 4, rows), bf16)
    narrow = jax.ShapeDtypeStruct((rows, width), bf16)
    broad = jax.ShapeDtypeStruct((rows, ff), bf16)
    wide = jax.ShapeDtypeStruct((rows, width), f32)
    sums = jax.ShapeDtypeStruct((2, width), f32)

    def fixed(shape):
        return pl.BlockSpec(shape.shape, lambda i, *_: (0, 0), pipeline_mode=pl.Buffered(1))

    return pl.pallas_call(
        block_kernel,
        grid_spec=pltpu.PrefetchScalarGridSpec(
            num_scalar_prefetch=1,
            grid=(steps,),
            in_specs=[
                *[resident(each) for each in (resid, attended, grad, params)],
                *chunk_blocks(0, steps),
                *chunk_blocks(steps // 2, steps),
                *[
                    pl.BlockSpec(
                        (WIDE, WIDE),
                        lambda i, *_: (2 * MLP_ROWS // WIDE, 0),
                        pipeline_mode=pl.Buffered(1),
                    )
                ]
                * 4,
            ],
            out_specs=[
                *[fixed(part)] * 4,
                fixed(narrow),
                column_block(rows, chunk),
                column_block(rows, chunk),
                fixed(wide),
                fixed(narrow),
                fixed(sums),
            ],
            scratch_shapes=[pltpu.VMEM((rows, width), f32)] * 2,
        ),
        out_shape=[*[part] * 4, narrow, broad, broad, wide, narrow, sums],
        compiler_params=pltpu.CompilerParams(vmem_limit_bytes=56 * 2**20),
        cost_estimate=pl.CostEstimate(
            flops=2 * rows * width * (4 * ff + 2 * width),
            bytes_accessed=rows * ff * 8,
            transcendentals=2 * rows * ff,
        ),
        name="block_middle",
    )(place, resid, attended, grad, params, *weights, *weights, *weights)


def adamw_kernel(first_block, place, weight, first, second, here, there, *outs):
    block = pl.program_id(0) + first_block
    mine = jnp.where(block // 2 == place[2], here[0].astype(f32), there[0].astype(f32))
    results = adamw_update(
        weight[...], mine, first[...], second[...], rate_matrix, decay_matrix
    )
    for out, result in zip(outs, results):
        out[...] = result


def adamw_blocks(place, weight, first, second, here, there, unit, first_block):
    rows, width = weight.shape
    if rows == WIDE:
        piece = pl.BlockSpec((WIDE, WIDE), lambda i, *_: (0, i))
    else:
        piece = pl.BlockSpec((WIDE, WIDE), lambda i, *_: (i, 0))
    part = pl.BlockSpec((1, WIDE, WIDE), lambda i, *_: (unit, (i + first_block) % 2, 0))
    return pl.pallas_call(
        lambda *refs: adamw_kernel(first_block, *refs),
        grid_spec=pltpu.PrefetchScalarGridSpec(
            num_scalar_prefetch=1,
            grid=(rows * width // WIDE**2,),
            in_specs=[piece, piece, piece, part, part],
            out_specs=[piece] * 3,
        ),
        out_shape=[jax.ShapeDtypeStruct((rows, width), f32)] * 3,
        compiler_params=pltpu.CompilerParams(vmem_limit_bytes=40 * 2**20),
        cost_estimate=pl.CostEstimate(
            flops=20 * rows * width, bytes_accessed=28 * rows * width, transcendentals=0
        ),
        name="adamw_blocks",
    )(place, weight, first, second, here, there)


def local(
    tokens_in,
    out_grad,
    qkv_weight,
    proj_weight,
    expand_weight,
    contract_weight,
    norm_params,
    qkv_first,
    qkv_second,
    proj_first,
    proj_second,
    expand_first,
    expand_second,
    contract_first,
    contract_second,
    norm_first,
    norm_second,
):
    row = lax.axis_index("row")
    col = lax.axis_index("col")
    dp = lax.axis_index("dp")
    n_dp = lax.axis_size("dp")
    me = 2 * row + col
    place = jnp.stack([col, me, dp % 2, dp // 2]).astype(jnp.int32)
    tokens = tokens_in.shape[0] // 4
    part = tokens_in.shape[1]

    def swap(array, distance):
        if distance == 0:
            return array
        return lax.ppermute(array, GROUP, [(i, i ^ distance) for i in range(4)])

    def swap_dp(array, distance):
        return lax.ppermute(array, "dp", [(i, i ^ distance) for i in range(n_dp)])

    def swap_row(array):
        return swap(array, 2)

    def swap_col(array):
        return swap(array, 1)

    def token_blocks(array):
        return [lax.dynamic_slice(array, ((me ^ d) * tokens, 0), (tokens, part)) for d in range(4)]

    def swap_all(blocks):
        return [swap(block, d) for d, block in enumerate(blocks)]

    def ordered(bit, mine, partner):
        return jnp.where(
            bit == 0,
            jnp.concatenate([mine, partner], axis=0),
            jnp.concatenate([partner, mine], axis=0),
        )

    def dp_part(mine, count):
        rows = mine.shape[0] // count
        return lax.dynamic_slice_in_dim(mine, (dp % count) * rows, rows)

    def all_blocks(mine, partner):
        return [mine, partner, swap_col(mine), swap_col(partner)]

    resid_parts = swap_all(token_blocks(tokens_in))
    params = [swap(norm_params, d) for d in range(4)]
    params = jnp.concatenate(
        [in_order(col, params[0], params[1]), in_order(col, params[2], params[3])], axis=1
    )
    x, z = dp % 2, dp // 2

    def stack(array):
        blocks = [array[..., at : at + WIDE] for at in range(0, array.shape[-1], WIDE)]
        return jnp.concatenate(blocks, axis=-2)

    qkv_mine = qkv_weight.astype(bf16)
    qkv_got = swap_row(dp_part(qkv_mine, 2))
    rest_mine = jnp.concatenate(
        [stack(expand_weight), contract_weight, proj_weight], axis=0
    ).astype(bf16)

    resid_parts, params, qkv_got, rest_got = lax.optimization_barrier(
        (resid_parts, params, qkv_got, dp_part(rest_mine, 4))
    )
    qkv_next = swap_dp(qkv_got, 1)
    rest_got = swap_row(rest_got)
    resid = tokens_together(place, [each.T for each in resid_parts])
    qkv_got, qkv_next, grad_blocks, resid = lax.optimization_barrier(
        (qkv_got, qkv_next, token_blocks(out_grad), resid)
    )
    qkv_low = all_blocks(qkv_mine, ordered(x, qkv_got, qkv_next))
    qkv_low, rest_got, grad_blocks = lax.optimization_barrier((qkv_low, rest_got, grad_blocks))
    rest_x, rest_z = swap_dp(rest_got, 1), swap_dp(rest_got, 2)
    grad_parts = swap_all(grad_blocks)
    h_one, mixed, attended, probs = attend_forward(resid, params, qkv_low)
    attended, rest_x, rest_z, grad_parts = lax.optimization_barrier(
        (attended, rest_x, rest_z, grad_parts)
    )
    rest_row = ordered(
        z % 2, ordered(x, rest_got, rest_x), ordered(x, rest_z, swap_dp(rest_z, 1))
    )
    rest_low = all_blocks(rest_mine, rest_row)
    grad_low = tokens_together(place, [each.T for each in grad_parts])
    outs = block_middle(place, resid, attended, grad_low, params, rest_low)
    output_parts = outs[:4]
    h_two, hidden, grad_pre, grad_middle, grad_attended, sums_two = outs[4:]

    def halves(array, axis):
        size = array.shape[axis] // 2
        return (
            lax.slice_in_dim(array, 0, size, axis=axis),
            lax.slice_in_dim(array, size, 2 * size, axis=axis),
        )

    def over_col(left, right, received):
        total = dot(left, right, ((0,), (0,))) + received.astype(f32)
        return total.astype(bf16)

    def split(array, bit):
        size = array.shape[1] // 2
        kept = lax.dynamic_slice_in_dim(array, bit * size, size, 1)
        return kept, lax.dynamic_slice_in_dim(array, (1 - bit) * size, size, 1)

    def add(kept, received):
        return (kept.astype(f32) + received.astype(f32)).astype(bf16)

    def join(bit, mine, partner):
        return jnp.where(
            bit == 0,
            jnp.concatenate([mine, partner], axis=1),
            jnp.concatenate([partner, mine], axis=1),
        )

    def over_z(total):
        if n_dp != 8:
            same_x = [[i for i in range(n_dp) if i % 2 == bit] for bit in range(2)]
            return lax.psum(total, "dp", axis_index_groups=same_x)
        for distance, bit in ((2, z % 2), (4, z // 2)):
            kept, away = split(total, bit)
            total = add(kept, swap_dp(away, distance))
        for distance, bit in ((4, z // 2), (2, z % 2)):
            total = join(bit, total, swap_dp(total, distance))
        return total

    hidden_own, hidden_other = halves(hidden, 1)
    pre_own, pre_other = halves(grad_pre, 1)
    attended_own, attended_other = halves(attended, 1)
    branch = grad_middle.astype(bf16)
    contract_got = swap_col(dot(hidden_other, grad_low, ((0,), (0,))).astype(bf16))
    expand_got = swap_col(dot(h_two, pre_other, ((0,), (0,))).astype(bf16))
    proj_got = swap_col(dot(attended_other, branch, ((0,), (0,))).astype(bf16))
    contract_sum = over_col(hidden_own, grad_low, contract_got)
    contract_kept, contract_away = halves(contract_sum, 1)
    expand_sum = over_col(h_two, pre_own, expand_got)
    expand_sum = stack(expand_sum.reshape(2, WIDE, expand_sum.shape[1]))
    expand_kept, expand_away = split(expand_sum, x)
    proj_kept, proj_away = halves(over_col(attended_own, branch, proj_got), 1)
    contract_away, expand_away, proj_away, grad_attended = lax.optimization_barrier(
        (contract_away, expand_away, proj_away, grad_attended)
    )
    contract_got, expand_got = swap_row(contract_away), swap_dp(expand_away, 1)
    mixed_other, grad_other = attend_backward(
        place, mixed, probs, grad_attended, qkv_low, 1, []
    )
    contract_got, expand_got, mixed_other, grad_other = lax.optimization_barrier(
        (contract_got, expand_got, mixed_other, grad_other)
    )
    contract_kept, contract_away = split(add(contract_kept, contract_got)[None], x)
    expand_kept, expand_away = add(expand_kept, expand_got)
    qkv_away = dot(h_one, mixed_other, ((0,), (0,))).astype(bf16)
    contract_away, proj_away, expand_away, qkv_away, grad_other = lax.optimization_barrier(
        (contract_away, proj_away, expand_away, qkv_away, grad_other)
    )
    contract_got, expand_got, proj_got, qkv_got = (
        swap_dp(contract_away, 1),
        swap_row(expand_away),
        swap_row(proj_away),
        swap_col(qkv_away),
    )
    outs = attend_backward(
        place, mixed, probs, grad_attended, qkv_low, 0, [grad_other, grad_middle, resid, params]
    )
    mixed_own, input_parts, sums_one = outs[0], outs[1:5], outs[5]
    contract_got, expand_got, proj_got, qkv_got, mixed_own = lax.optimization_barrier(
        (contract_got, expand_got, proj_got, qkv_got, mixed_own)
    )
    qkv_kept, qkv_away = halves(over_col(h_one, mixed_own, qkv_got), 0)
    mlp_sum = jnp.concatenate(
        [add(contract_kept, contract_got), add(expand_kept, expand_got)[None]], axis=0
    )
    qkv_away, mlp_sum = lax.optimization_barrier((qkv_away, mlp_sum))
    qkv_got = swap_row(qkv_away)
    mlp_sum = over_z(mlp_sum)
    qkv_got, output_parts, input_parts = lax.optimization_barrier(
        (qkv_got, output_parts, input_parts)
    )
    both = jnp.concatenate([stack(add(qkv_kept, qkv_got)), add(proj_kept, proj_got)], axis=0)
    both_kept, both_away = split(both[None], x)
    both_sum = over_z(add(both_kept, swap_dp(both_away, 1)))
    mlp_sum = (mlp_sum, swap_dp(mlp_sum, 1))
    both_sum = (both_sum, swap_dp(both_sum, 1))

    norm_parts = split_features(col, jnp.concatenate([sums_one, sums_two], axis=0))
    norm_sum = norm_parts[0] + sum(swap(norm_parts[d], d) for d in range(1, 4))
    if n_dp == 8:
        for d in (1, 2, 4):
            norm_sum = norm_sum + swap_dp(norm_sum, d)
    else:
        norm_sum = lax.psum(norm_sum, "dp")

    results = (
        tokens_apart(place, tokens, swap_all(output_parts)),
        tokens_apart(place, tokens, swap_all(input_parts)),
    )
    for weight, gradient, first, second, unit, block in (
        (qkv_weight, both_sum, qkv_first, qkv_second, 0, 0),
        (proj_weight, both_sum, proj_first, proj_second, 0, 3),
        (expand_weight, mlp_sum, expand_first, expand_second, 1, 0),
        (contract_weight, mlp_sum, contract_first, contract_second, 0, 0),
    ):
        results += tuple(adamw_blocks(place, weight, first, second, *gradient, unit, block))
    return results + adamw_update(norm_params, norm_sum, norm_first, norm_second, rate_norm, 0.0)


def solution(mesh):
    tokens = P("dp", ("row", "col"))
    one = P("row", "col")
    two = P("col", "row")
    norm = P(None, ("row", "col"))
    in_specs = (tokens, tokens, one, two, one, two, norm)
    in_specs += (one, one, two, two, one, one, two, two, norm, norm)
    out_specs = (tokens, tokens) + (one,) * 3 + (two,) * 3 + (one,) * 3 + (two,) * 3 + (norm,) * 3
    return jax.shard_map(local, mesh=mesh, in_specs=in_specs, out_specs=out_specs, check_vma=False)
```

```python
import jax
import jax.numpy as jnp
from jax import lax
from jax.experimental import pallas as pl
from jax.experimental.pallas import tpu as pltpu
from jax.sharding import PartitionSpec as P

HEAD_DIM = 64
SEQ = 197
QROWS = 208
KROWS = 256
STEP = 10
ROWS = 1200
BLOCK = 608
STEPS = 6
GROUPED = 2
WIDE = 384
CHUNK = 768
MLP_ROWS = 1536

norm_epsilon = 1e-06
beta_first = 0.9
beta_second = 0.999
adam_epsilon = 1e-08
rate_matrix = 0.1
rate_norm = 0.5
decay_matrix = 0.05

GROUP = ("row", "col")
bf16 = jnp.bfloat16
f32 = jnp.float32


def dot(left, right, dims=((1,), (0,))):
    return lax.dot_general(left, right, (dims, ((), ())), preferred_element_type=f32)


def swap_halves(block):
    return jnp.concatenate([block[:, HEAD_DIM:], block[:, :HEAD_DIM]], axis=1)


def gelu_and_slope(value):
    size = jnp.abs(value)
    density = jnp.exp(value * value * -0.5)
    base = 1.0 + (0.3275911 * 0.5**0.5) * size
    t = pl.reciprocal(base, approx=True)
    t = t * (2.0 - base * t)
    series = t * (
        0.254829592
        + t * (-0.284496736 + t * (1.421413741 + t * (-1.453152027 + t * 1.061405429)))
    )
    tail = 0.5 * series * density
    phi = jnp.where(value >= 0, 1.0 - tail, tail)
    return (value * phi, phi + value * density * 0.3989422804014327)


def adamw_update(weight, gradient, first_old, second_old, rate_value, decay_value):
    first_new = beta_first * first_old + (1.0 - beta_first) * gradient
    second_new = beta_second * second_old + (1.0 - beta_second) * (gradient * gradient)
    first_hat = first_new / (1.0 - beta_first**STEP)
    second_hat = second_new / (1.0 - beta_second**STEP)
    moved = weight - rate_value * (
        first_hat / (jnp.sqrt(second_hat) + adam_epsilon) + decay_value * weight
    )
    return (moved, first_new, second_new)


def row_blocks(rows, size=BLOCK):
    return [slice(start, min(start + size, rows)) for start in range(0, rows, size)]


def norm_rows(values):
    center = jnp.mean(values, axis=1, keepdims=True)
    spread = jnp.mean(values * values, axis=1, keepdims=True) - center * center
    scaled = lax.rsqrt(spread + norm_epsilon)
    return ((values - center) * scaled, scaled)


def norm_backward(grad_normed, normed, scaled, gain_row):
    local_grad = grad_normed * gain_row
    first = jnp.mean(local_grad, axis=1, keepdims=True)
    second = jnp.mean(local_grad * normed, axis=1, keepdims=True)
    return scaled * (local_grad - first - normed * second)


def in_order(col, first, second):
    return jnp.where(
        col == 0,
        jnp.concatenate([first, second], axis=-1),
        jnp.concatenate([second, first], axis=-1),
    )


def split_features(col, array):
    part = array.shape[-1] // 4
    quarters = [array[..., i * part : (i + 1) * part] for i in range(4)]
    own = [jnp.where(col == 0, quarters[2 * i], quarters[2 * i + 1]) for i in range(2)]
    other = [jnp.where(col == 0, quarters[2 * i + 1], quarters[2 * i]) for i in range(2)]
    return [own[0], other[0], own[1], other[1]]


def resident(array):
    zeros = (0,) * array.ndim
    return pl.BlockSpec(array.shape, lambda i, *_: zeros, pipeline_mode=pl.Buffered(1))


def column_block(rows, width):
    return pl.BlockSpec((rows, width), lambda i, *_: (0, i))


def side_blocks(rows, width, along, steps):
    def first(i, *_):
        at = jnp.minimum(i, steps // 2 - 1)
        return (0, at) if along == 1 else (at, 0)

    def second(i, *_):
        at = jnp.maximum(i - steps // 2, 0)
        return (0, at) if along == 1 else (at, 0)

    block = (rows, width)
    return [pl.BlockSpec(block, first)] * 2 + [pl.BlockSpec(block, second)] * 2


def side_weight(refs, steps, axis):
    own = jnp.concatenate([refs[0][...], refs[1][...]], axis=axis)
    other = jnp.concatenate([refs[2][...], refs[3][...]], axis=axis)
    return jnp.where(pl.program_id(0) < steps // 2, own, other)


def split_parts(col, array):
    part = array.shape[0] // 4
    quarters = [array[i * part : (i + 1) * part] for i in range(4)]
    own = [jnp.where(col == 0, quarters[2 * i], quarters[2 * i + 1]) for i in range(2)]
    other = [jnp.where(col == 0, quarters[2 * i + 1], quarters[2 * i]) for i in range(2)]
    return [own[0], other[0], own[1], other[1]]


def together_kernel(place, *refs):
    parts, out_ref = refs[:4], refs[4]
    part, tokens = parts[0].shape
    wide = [ref[...].astype(f32) for ref in parts]
    for half in range(2):
        first, second = wide[2 * half], wide[2 * half + 1]
        both = [jnp.where(place[0] == 0, first, second), jnp.where(place[0] == 0, second, first)]
        block = jnp.concatenate(both, axis=0)
        at = 2 * part * half
        out_ref[0:tokens, at : at + 2 * part] = block.T.astype(bf16)
    low = tokens - tokens % 16
    row = lax.broadcasted_iota(jnp.int32, (out_ref.shape[0] - low, 1), 0) + low
    out_ref[low:, :] = jnp.where(row < tokens, out_ref[low:, :].astype(f32), 0.0).astype(bf16)


def tokens_together(place, parts):
    part, tokens = parts[0].shape
    padded = -(-tokens // ROWS) * ROWS
    return pl.pallas_call(
        together_kernel,
        in_specs=[pl.BlockSpec(memory_space=pltpu.SMEM)]
        + [pl.BlockSpec(memory_space=pltpu.VMEM)] * 4,
        out_specs=pl.BlockSpec(memory_space=pltpu.VMEM),
        out_shape=jax.ShapeDtypeStruct((padded, 4 * part), bf16),
        compiler_params=pltpu.CompilerParams(vmem_limit_bytes=40 * 2**20),
        cost_estimate=pl.CostEstimate(
            flops=0, bytes_accessed=16 * tokens * part, transcendentals=0
        ),
        name="tokens_together",
    )(place, *parts)


def apart_kernel(place, *refs):
    parts, out_ref = refs[:4], refs[4]
    tokens = out_ref.shape[1] // 4
    for block in range(4):
        for distance in range(4):

            @pl.when((place[1] ^ block) == distance)
            def _():
                columns = slice(block * tokens, (block + 1) * tokens)
                out_ref[:, columns] = parts[distance][...].astype(f32)[:, :tokens]


def tokens_apart(place, tokens, parts):
    part = parts[0].shape[0]
    return pl.pallas_call(
        apart_kernel,
        in_specs=[pl.BlockSpec(memory_space=pltpu.SMEM)]
        + [pl.BlockSpec(memory_space=pltpu.VMEM)] * 4,
        out_specs=pl.BlockSpec(memory_space=pltpu.VMEM),
        out_shape=jax.ShapeDtypeStruct((part, 4 * tokens), f32),
        compiler_params=pltpu.CompilerParams(vmem_limit_bytes=40 * 2**20),
        cost_estimate=pl.CostEstimate(
            flops=0, bytes_accessed=4 * tokens * part * 6, transcendentals=0
        ),
        name="tokens_apart",
    )(place, *parts).T


def forward_kernel(*refs):
    resid_ref, params = refs[:2]
    weights = refs[2:6]
    h_ref, mixed_ref, out_ref, probs_ref, wide, gathered = refs[6:]
    rows = resid_ref.shape[0]
    images = rows // SEQ
    tokens = images * SEQ
    steps = pl.num_programs(0)

    @pl.when(pl.program_id(0) == 0)
    def _():
        for block in row_blocks(rows):
            normed, _ = norm_rows(resid_ref[block, :].astype(f32))
            h_ref[block, :] = (normed * params[0:1, :] + params[1:2, :]).astype(bf16)

    weight = side_weight(weights, STEPS, 0)
    for block in row_blocks(rows):
        mixed = dot(h_ref[block, :], weight).astype(bf16)
        mixed_ref[block, :] = mixed
        wide[block, :] = mixed.astype(f32)
    wide[rows:, :] = jnp.zeros((wide.shape[0] - rows, 384), f32)
    low_lane = lax.broadcasted_iota(jnp.int32, (1, 128), 1) < HEAD_DIM
    key_lane = lax.broadcasted_iota(jnp.int32, (1, KROWS), 1) < SEQ
    scale = HEAD_DIM ** (-0.5)
    for group in range(0, images, GROUPED):
        members = range(group, min(group + GROUPED, images))
        scores, values = [], []
        for image in members:
            start = image * SEQ
            block_a = wide[start : start + KROWS, 0:128]
            block_b = wide[start : start + KROWS, 128:256]
            block_c = wide[start : start + KROWS, 256:384]
            query_0 = jnp.where(low_lane, block_a[:QROWS] * scale, 0.0).astype(bf16)
            query_1 = jnp.where(low_lane, 0.0, block_b[:QROWS] * scale).astype(bf16)
            scores.append(dot(query_0, swap_halves(block_a).astype(bf16), ((1,), (1,))))
            scores.append(dot(query_1, swap_halves(block_c).astype(bf16), ((1,), (1,))))
            values += [block_b.astype(bf16), block_c.astype(bf16)]
        scores = [jnp.where(key_lane, score, -1e30) for score in scores]
        tops = [jnp.max(score, axis=1, keepdims=True) for score in scores]
        exponents = [jnp.exp(score - top) for score, top in zip(scores, tops)]
        totals = [jnp.sum(exponent, axis=1, keepdims=True) for exponent in exponents]
        probs = [(e * (1.0 / total)).astype(bf16) for e, total in zip(exponents, totals)]
        outs = [dot(prob, value) for prob, value in zip(probs, values)]
        for at, image in enumerate(members):
            start = image * SEQ
            probs_ref[0, image * 2] = probs[2 * at]
            probs_ref[0, image * 2 + 1] = probs[2 * at + 1]
            gathered[start : start + QROWS, :] = jnp.where(
                low_lane, outs[2 * at], outs[2 * at + 1]
            )
    gathered[tokens:, :] = jnp.zeros((gathered.shape[0] - tokens, 128), f32)
    out_ref[...] = gathered[0:rows, :].astype(bf16)


def attend_forward(resid, params, weights):
    rows, width = resid.shape
    images = rows // SEQ
    padded = -(-((images - 1) * SEQ + KROWS) // 16) * 16
    pair_probs = (STEPS, 2 * images, QROWS, KROWS)
    half_rows = weights[0].shape[0]
    return pl.pallas_call(
        forward_kernel,
        grid=(STEPS,),
        in_specs=[resident(resid), resident(params), *side_blocks(half_rows, 384, 1, STEPS)],
        out_specs=[
            pl.BlockSpec((rows, width), lambda i: (0, 0)),
            column_block(rows, 384),
            column_block(rows, 128),
            pl.BlockSpec((1, *pair_probs[1:]), lambda i: (i, 0, 0, 0)),
        ],
        out_shape=[
            jax.ShapeDtypeStruct((rows, width), bf16),
            jax.ShapeDtypeStruct((rows, STEPS * 384), bf16),
            jax.ShapeDtypeStruct((rows, STEPS * 128), bf16),
            jax.ShapeDtypeStruct(pair_probs, bf16),
        ],
        scratch_shapes=[pltpu.VMEM((padded, 384), f32), pltpu.VMEM((padded, 128), f32)],
        compiler_params=pltpu.CompilerParams(vmem_limit_bytes=48 * 2**20),
        cost_estimate=pl.CostEstimate(
            flops=20 * 10**9, bytes_accessed=rows * width * 20, transcendentals=10**6
        ),
        name="attend_forward",
    )(resid, params, *weights)


def backward_kernel(last, place, *refs):
    mixed_ref, probs_ref, grad_ref = refs[:3]
    weights = refs[3:5]
    if last:
        before_ref, middle_ref, resid_ref, params = refs[5:9]
        out_ref, out_parts, sums_ref = refs[9], refs[10:14], refs[14]
        wide, grad_wide, gathered, total = refs[15:]
    else:
        out_ref, total = refs[5:7]
        wide, grad_wide, gathered = refs[7:]
    rows = mixed_ref.shape[0]
    images = rows // SEQ
    tokens = images * SEQ
    wide[rows:, :] = jnp.zeros((wide.shape[0] - rows, 384), f32)
    wide[0:rows, :] = mixed_ref[...].astype(f32)
    grad_wide[0:rows, :] = grad_ref[...].astype(f32)
    low_lane = lax.broadcasted_iota(jnp.int32, (1, 128), 1) < HEAD_DIM
    query_row = lax.broadcasted_iota(jnp.int32, (QROWS, 128), 0) < SEQ
    scale = HEAD_DIM ** (-0.5)
    for group in range(0, images, GROUPED):
        members = range(group, min(group + GROUPED, images))
        grad_probs, grad_values, probs, swapped = [], [], [], []
        for image in members:
            start = image * SEQ
            block_a = wide[start : start + KROWS, 0:128]
            block_b = wide[start : start + KROWS, 128:256]
            block_c = wide[start : start + KROWS, 256:384]
            grad = jnp.where(query_row, grad_wide[start : start + QROWS, :], 0.0)
            grad_low = grad.astype(bf16)
            probs_0 = probs_ref[0, 2 * image]
            probs_1 = probs_ref[0, 2 * image + 1]
            probs += [probs_0, probs_1]
            part_0 = jnp.where(low_lane, grad, 0.0).astype(bf16)
            part_1 = jnp.where(low_lane, 0.0, grad).astype(bf16)
            grad_probs.append(dot(part_0, block_b.astype(bf16), ((1,), (1,))))
            grad_probs.append(dot(part_1, block_c.astype(bf16), ((1,), (1,))))
            grad_values.append(dot(probs_0, grad_low, ((0,), (0,))))
            grad_values.append(dot(probs_1, grad_low, ((0,), (0,))))
            swapped.append(
                [(swap_halves(block) * scale).astype(bf16) for block in (block_a, block_b, block_c)]
            )
        wide_probs = [prob.astype(f32) for prob in probs]
        inner = [
            jnp.sum(prob * grad, axis=1, keepdims=True)
            for prob, grad in zip(wide_probs, grad_probs)
        ]
        score_grads = [
            (prob * (grad - each)).astype(bf16)
            for prob, grad, each in zip(wide_probs, grad_probs, inner)
        ]
        for at, image in enumerate(members):
            start = image * SEQ
            swapped_a, swapped_b, swapped_c = swapped[at]
            score_0, score_1 = score_grads[2 * at : 2 * at + 2]
            grad_v0, grad_v1 = grad_values[2 * at : 2 * at + 2]
            grad_q0 = dot(score_0, swapped_a)
            grad_k0 = dot(score_0, swapped_a[:QROWS], ((0,), (0,)))
            grad_q1 = dot(score_1, swapped_c)
            grad_k1 = dot(score_1, swapped_b[:QROWS], ((0,), (0,)))
            block = slice(start, start + QROWS)
            gathered[block, 0:128] = jnp.where(low_lane, grad_q0, grad_k0[:QROWS])
            gathered[block, 128:256] = jnp.where(low_lane, grad_v0[:QROWS], grad_q1)
            gathered[block, 256:384] = jnp.where(low_lane, grad_k1[:QROWS], grad_v1[:QROWS])
    gathered[tokens:, :] = jnp.zeros((gathered.shape[0] - tokens, 384), f32)
    weight = jnp.concatenate([weights[0][...], weights[1][...]], axis=0)
    step = pl.program_id(0)

    @pl.when(step == 0)
    def _():
        total[...] = before_ref[...] if last else jnp.zeros_like(total)

    for block in row_blocks(rows):
        grad_mixed = gathered[block, :].astype(bf16)
        out_ref[block, :] = grad_mixed
        total[block, :] += dot(grad_mixed, weight, ((1,), (1,)))

    if not last:
        return

    @pl.when(step == pl.num_programs(0) - 1)
    def _():
        gain = jnp.zeros((1, total.shape[1]), f32)
        shift = jnp.zeros((1, total.shape[1]), f32)
        for block in row_blocks(rows):
            grad_one = total[block, :]
            normed, scaled = norm_rows(resid_ref[block, :].astype(f32))
            gain += jnp.sum(grad_one * normed, axis=0, keepdims=True)
            shift += jnp.sum(grad_one, axis=0, keepdims=True)
            total[block, :] = middle_ref[block, :] + norm_backward(
                grad_one, normed, scaled, params[0:1, :]
            )
        sums_ref[0:1, :] = gain
        sums_ref[1:2, :] = shift
        for part_ref, part in zip(out_parts, split_parts(place[0], total[...].T)):
            part_ref[...] = part.astype(bf16)


def attend_backward(place, mixed, probs, grad_attended, weights, side, rest):
    rows, width = grad_attended.shape
    images = rows // SEQ
    steps = STEPS // 2
    first = side * steps
    padded = -(-((images - 1) * SEQ + KROWS) // 16) * 16
    part = jax.ShapeDtypeStruct((width // 4, rows), bf16)
    sums = jax.ShapeDtypeStruct((2, width), f32)
    whole = jax.ShapeDtypeStruct((rows, width), f32)
    extra = [part] * 4 + [sums] if rest else [whole]
    scratch = [
        pltpu.VMEM((padded, 384), f32),
        pltpu.VMEM((padded, 128), f32),
        pltpu.VMEM((padded, 384), f32),
    ]
    if rest:
        scratch.append(pltpu.VMEM((rows, width), f32))
    weight_rows = weights[0].shape[0]
    return pl.pallas_call(
        lambda *refs: backward_kernel(bool(rest), *refs),
        grid_spec=pltpu.PrefetchScalarGridSpec(
            num_scalar_prefetch=1,
            grid=(steps,),
            in_specs=[
                pl.BlockSpec((rows, 384), lambda i, *_: (0, i + first)),
                pl.BlockSpec((1, *probs.shape[1:]), lambda i, *_: (i + first, 0, 0, 0)),
                pl.BlockSpec((rows, 128), lambda i, *_: (0, i + first)),
                *[pl.BlockSpec((weight_rows, 384), lambda i, *_: (0, i))] * 2,
                *[resident(each) for each in rest],
            ],
            out_specs=[
                column_block(rows, 384),
                *[pl.BlockSpec(each.shape, lambda i, *_: (0, 0)) for each in extra],
            ],
            scratch_shapes=scratch,
        ),
        out_shape=[jax.ShapeDtypeStruct((rows, steps * 384), bf16), *extra],
        compiler_params=pltpu.CompilerParams(vmem_limit_bytes=48 * 2**20),
        name="attend_backward",
    )(place, mixed, probs, grad_attended, *weights[2 * side : 2 * side + 2], *rest)


def block_kernel(place, *refs):
    resid_ref, attended_ref, grad_ref, params = refs[:4]
    expand, contract, proj = refs[4:8], refs[8:12], refs[12:16]
    out_parts = refs[16:20]
    h_ref, hidden_ref, pre_ref, middle_ref, attended_grad_ref, sums_ref = refs[20:26]
    output, grad_two = refs[26:]
    middle = middle_ref
    rows = resid_ref.shape[0]
    step = pl.program_id(0)
    blocks = row_blocks(rows, 400)

    def proj_low():
        own = jnp.concatenate([proj[0][...], proj[1][...]], axis=1)
        return jnp.concatenate([own, jnp.concatenate([proj[2][...], proj[3][...]], axis=1)], axis=0)

    @pl.when(step == 0)
    def _():
        weight = proj_low()
        for block in blocks:
            value = resid_ref[block, :].astype(f32) + dot(attended_ref[block, :], weight)
            middle[block, :] = value
            output[block, :] = value
            grad_two[block, :] = jnp.zeros_like(value)
            normed, _ = norm_rows(value)
            h_ref[block, :] = (normed * params[2:3, :] + params[3:4, :]).astype(bf16)

    own_side = step < pl.num_programs(0) // 2

    def expand_side(own, other):
        upper = jnp.concatenate([own[at : at + WIDE, :] for at in range(0, CHUNK, WIDE)], axis=1)
        lower = jnp.concatenate([other[at : at + WIDE, :] for at in range(0, CHUNK, WIDE)], axis=1)
        return jnp.concatenate([upper, lower], axis=0)

    expand_low = jnp.where(
        own_side, expand_side(expand[0], expand[1]), expand_side(expand[2], expand[3])
    )
    contract_low = jnp.where(
        own_side,
        jnp.concatenate([contract[0][...], contract[1][...]], axis=1),
        jnp.concatenate([contract[2][...], contract[3][...]], axis=1),
    )

    def products(block):
        return (
            dot(h_ref[block, :], expand_low),
            dot(grad_ref[block, :], contract_low, ((1,), (1,))),
        )

    ahead = products(blocks[0])
    for at, block in enumerate(blocks):
        before, grad_hidden = ahead
        if at + 1 < len(blocks):
            ahead = products(blocks[at + 1])
        value, slope = gelu_and_slope(before)
        hidden = value.astype(bf16)
        grad_pre = (grad_hidden * slope).astype(bf16)
        hidden_ref[block, :] = hidden
        pre_ref[block, :] = grad_pre
        output[block, :] += dot(hidden, contract_low)
        grad_two[block, :] += dot(grad_pre, expand_low, ((1,), (1,)))

    @pl.when(step == pl.num_programs(0) - 1)
    def _():
        weight = proj_low()
        gain = jnp.zeros((1, middle.shape[1]), f32)
        shift = jnp.zeros((1, middle.shape[1]), f32)
        for block in blocks:
            grad = grad_two[block, :]
            normed, scaled = norm_rows(middle[block, :])
            gain += jnp.sum(grad * normed, axis=0, keepdims=True)
            shift += jnp.sum(grad, axis=0, keepdims=True)
            grad_middle = grad_ref[block, :].astype(f32) + norm_backward(
                grad, normed, scaled, params[2:3, :]
            )
            middle_ref[block, :] = grad_middle
            attended_grad_ref[block, :] = dot(
                grad_middle.astype(bf16), weight, ((1,), (1,))
            ).astype(bf16)
        sums_ref[0:1, :] = gain
        sums_ref[1:2, :] = shift
        for part_ref, part in zip(out_parts, split_parts(place[0], output[...].T)):
            part_ref[...] = part.astype(bf16)


def chunk_blocks(first, steps):
    def own(i, *_):
        return (first + jnp.minimum(i, steps // 2 - 1), 0)

    def other(i, *_):
        return (first + jnp.maximum(i - steps // 2, 0), 0)

    return [pl.BlockSpec((CHUNK, WIDE), own)] * 2 + [pl.BlockSpec((CHUNK, WIDE), other)] * 2


def block_middle(place, resid, attended, grad, params, weights):
    rows, width = resid.shape
    ff = 2 * MLP_ROWS
    chunk = CHUNK
    steps = ff // CHUNK
    part = jax.ShapeDtypeStruct((width // 4, rows), bf16)
    narrow = jax.ShapeDtypeStruct((rows, width), bf16)
    broad = jax.ShapeDtypeStruct((rows, ff), bf16)
    wide = jax.ShapeDtypeStruct((rows, width), f32)
    sums = jax.ShapeDtypeStruct((2, width), f32)

    def fixed(shape):
        return pl.BlockSpec(shape.shape, lambda i, *_: (0, 0), pipeline_mode=pl.Buffered(1))

    return pl.pallas_call(
        block_kernel,
        grid_spec=pltpu.PrefetchScalarGridSpec(
            num_scalar_prefetch=1,
            grid=(steps,),
            in_specs=[
                *[resident(each) for each in (resid, attended, grad, params)],
                *chunk_blocks(0, steps),
                *chunk_blocks(steps // 2, steps),
                *[
                    pl.BlockSpec(
                        (WIDE, WIDE),
                        lambda i, *_: (2 * MLP_ROWS // WIDE, 0),
                        pipeline_mode=pl.Buffered(1),
                    )
                ]
                * 4,
            ],
            out_specs=[
                *[fixed(part)] * 4,
                fixed(narrow),
                column_block(rows, chunk),
                column_block(rows, chunk),
                fixed(wide),
                fixed(narrow),
                fixed(sums),
            ],
            scratch_shapes=[pltpu.VMEM((rows, width), f32)] * 2,
        ),
        out_shape=[*[part] * 4, narrow, broad, broad, wide, narrow, sums],
        compiler_params=pltpu.CompilerParams(vmem_limit_bytes=56 * 2**20),
        cost_estimate=pl.CostEstimate(
            flops=2 * rows * width * (4 * ff + 2 * width),
            bytes_accessed=rows * ff * 8,
            transcendentals=2 * rows * ff,
        ),
        name="block_middle",
    )(place, resid, attended, grad, params, *weights, *weights, *weights)


def adamw_kernel(first_block, place, weight, first, second, here, there, *outs):
    block = pl.program_id(0) + first_block
    mine = jnp.where(block // 2 == place[2], here[0].astype(f32), there[0].astype(f32))
    results = adamw_update(
        weight[...], mine, first[...], second[...], rate_matrix, decay_matrix
    )
    for out, result in zip(outs, results):
        out[...] = result


def adamw_blocks(place, weight, first, second, here, there, unit, first_block):
    rows, width = weight.shape
    if rows == WIDE:
        piece = pl.BlockSpec((WIDE, WIDE), lambda i, *_: (0, i))
    else:
        piece = pl.BlockSpec((WIDE, WIDE), lambda i, *_: (i, 0))
    part = pl.BlockSpec((1, WIDE, WIDE), lambda i, *_: (unit, (i + first_block) % 2, 0))
    return pl.pallas_call(
        lambda *refs: adamw_kernel(first_block, *refs),
        grid_spec=pltpu.PrefetchScalarGridSpec(
            num_scalar_prefetch=1,
            grid=(rows * width // WIDE**2,),
            in_specs=[piece, piece, piece, part, part],
            out_specs=[piece] * 3,
        ),
        out_shape=[jax.ShapeDtypeStruct((rows, width), f32)] * 3,
        compiler_params=pltpu.CompilerParams(vmem_limit_bytes=40 * 2**20),
        cost_estimate=pl.CostEstimate(
            flops=20 * rows * width, bytes_accessed=28 * rows * width, transcendentals=0
        ),
        name="adamw_blocks",
    )(place, weight, first, second, here, there)


def local(
    tokens_in,
    out_grad,
    qkv_weight,
    proj_weight,
    expand_weight,
    contract_weight,
    norm_params,
    qkv_first,
    qkv_second,
    proj_first,
    proj_second,
    expand_first,
    expand_second,
    contract_first,
    contract_second,
    norm_first,
    norm_second,
):
    row = lax.axis_index("row")
    col = lax.axis_index("col")
    dp = lax.axis_index("dp")
    n_dp = lax.axis_size("dp")
    me = 2 * row + col
    place = jnp.stack([col, me, dp % 2, dp // 2]).astype(jnp.int32)
    tokens = tokens_in.shape[0] // 4
    part = tokens_in.shape[1]

    def swap(array, distance):
        if distance == 0:
            return array
        return lax.ppermute(array, GROUP, [(i, i ^ distance) for i in range(4)])

    def swap_dp(array, distance):
        return lax.ppermute(array, "dp", [(i, i ^ distance) for i in range(n_dp)])

    def swap_row(array):
        return swap(array, 2)

    def swap_col(array):
        return swap(array, 1)

    def token_blocks(array):
        return [lax.dynamic_slice(array, ((me ^ d) * tokens, 0), (tokens, part)) for d in range(4)]

    def swap_all(blocks):
        return [swap(block, d) for d, block in enumerate(blocks)]

    def ordered(bit, mine, partner):
        return jnp.where(
            bit == 0,
            jnp.concatenate([mine, partner], axis=0),
            jnp.concatenate([partner, mine], axis=0),
        )

    def dp_part(mine, count):
        rows = mine.shape[0] // count
        return lax.dynamic_slice_in_dim(mine, (dp % count) * rows, rows)

    def all_blocks(mine, partner):
        return [mine, partner, swap_col(mine), swap_col(partner)]

    x, z = dp % 2, dp // 2
    z_low, z_high = z % 2, z // 2 % 2

    def stack(array):
        blocks = [array[..., at : at + WIDE] for at in range(0, array.shape[-1], WIDE)]
        return jnp.concatenate(blocks, axis=-2)

    rest_mine = jnp.concatenate(
        [stack(expand_weight), contract_weight, proj_weight], axis=0
    ).astype(bf16)
    rest_got = swap_row(dp_part(rest_mine, 4))
    qkv_mine = qkv_weight.astype(bf16)
    qkv_got = swap_row(dp_part(qkv_mine, 2))
    resid_parts = swap_all(token_blocks(tokens_in))
    params = [swap(norm_params, d) for d in range(4)]
    params = jnp.concatenate(
        [in_order(col, params[0], params[1]), in_order(col, params[2], params[3])], axis=1
    )
    rest_x, rest_z = swap_dp(rest_got, 1), swap_dp(rest_got, 2)
    resid_parts, params, qkv_got, rest_x, rest_z = lax.optimization_barrier(
        (resid_parts, params, qkv_got, rest_x, rest_z)
    )
    qkv_next, rest_last = swap_dp(qkv_got, 1), swap_dp(rest_z, 1)
    resid = tokens_together(place, [each.T for each in resid_parts])
    qkv_next, grad_blocks, resid = lax.optimization_barrier(
        (qkv_next, token_blocks(out_grad), resid)
    )
    qkv_low = all_blocks(qkv_mine, ordered(x, qkv_got, qkv_next))
    grad_parts = swap_all(grad_blocks)
    rest_away = swap_col(rest_mine)
    h_one, mixed, attended, probs = attend_forward(resid, params, qkv_low)
    attended, rest_last, grad_parts, rest_away = lax.optimization_barrier(
        (attended, rest_last, grad_parts, rest_away)
    )
    rest_row = ordered(z_low, ordered(x, rest_got, rest_x), ordered(x, rest_z, rest_last))
    rest_low = [rest_mine, rest_row, rest_away, swap_col(rest_row)]
    grad_low = tokens_together(place, [each.T for each in grad_parts])
    outs = block_middle(place, resid, attended, grad_low, params, rest_low)
    output_parts = swap_all(outs[:4])
    h_two, hidden, grad_pre, grad_middle, grad_attended, sums_two = outs[4:]

    def halves(array, axis):
        size = array.shape[axis] // 2
        return (
            lax.slice_in_dim(array, 0, size, axis=axis),
            lax.slice_in_dim(array, size, 2 * size, axis=axis),
        )

    def over_col(left, right, received):
        total = dot(left, right, ((0,), (0,))) + received.astype(f32)
        return total.astype(bf16)

    def split(array, bit):
        size = array.shape[1] // 2
        kept = lax.dynamic_slice_in_dim(array, bit * size, size, 1)
        return kept, lax.dynamic_slice_in_dim(array, (1 - bit) * size, size, 1)

    def add(kept, received):
        return (kept.astype(f32) + received.astype(f32)).astype(bf16)

    def join(bit, mine, partner):
        return jnp.where(
            bit == 0,
            jnp.concatenate([mine, partner], axis=1),
            jnp.concatenate([partner, mine], axis=1),
        )

    same_x = [[i for i in range(n_dp) if i % 2 == bit] for bit in range(2)]

    def over_z(total, after):
        if n_dp != 8:
            return lax.psum(total, "dp", axis_index_groups=same_x), after
        for at, (distance, bit) in enumerate(((2, z_low), (4, z_high))):
            kept, away = split(total, bit)
            if at == 0:
                away, after = lax.optimization_barrier((away, after))
            total = add(kept, swap_dp(away, distance))
        for distance, bit in ((4, z_high), (2, z_low)):
            total = join(bit, total, swap_dp(total, distance))
        return total, after

    def over_z_direct(total):
        if n_dp != 8:
            return lax.psum(total, "dp", axis_index_groups=same_x)
        size = total.shape[1] // 4
        parts = [lax.dynamic_slice_in_dim(total, (z ^ d) * size, size, 1) for d in range(4)]
        mine = parts[0].astype(f32)
        for d in range(1, 4):
            mine = mine + swap_dp(parts[d], 2 * d).astype(f32)
        mine = mine.astype(bf16)
        parts = [mine] + [swap_dp(mine, 2 * d) for d in range(1, 4)]
        return join(z_high, join(z_low, *parts[:2]), join(z_low, *parts[2:]))

    def norm_total(sums):
        parts = split_features(col, sums)
        return parts[0] + sum(swap(parts[d], d) for d in range(1, 4))

    def norm_over_dp(total):
        if n_dp != 8:
            return lax.psum(total, "dp")
        for d in (1, 2, 4):
            total = total + swap_dp(total, d)
        return total

    hidden_own, hidden_other = halves(hidden, 1)
    pre_own, pre_other = halves(grad_pre, 1)
    attended_own, attended_other = halves(attended, 1)
    branch = grad_middle.astype(bf16)
    contract_got = swap_col(dot(hidden_other, grad_low, ((0,), (0,))).astype(bf16))
    expand_got = swap_col(dot(h_two, pre_other, ((0,), (0,))).astype(bf16))
    contract_sum = over_col(hidden_own, grad_low, contract_got)
    contract_kept, contract_away = halves(contract_sum, 1)
    contract_away, pre_own, branch = lax.optimization_barrier((contract_away, pre_own, branch))
    contract_got = swap_row(contract_away)
    proj_got = swap_col(dot(attended_other, branch, ((0,), (0,))).astype(bf16))
    expand_sum = over_col(h_two, pre_own, expand_got)
    expand_sum = stack(expand_sum.reshape(2, WIDE, expand_sum.shape[1]))
    expand_kept, expand_away = split(expand_sum, x)
    proj_kept, proj_away = halves(over_col(attended_own, branch, proj_got), 1)
    norm_two = norm_total(sums_two)
    expand_away, proj_away, norm_two, output_parts, grad_attended = lax.optimization_barrier(
        (expand_away, proj_away, norm_two, output_parts, grad_attended)
    )
    expand_got = swap_dp(expand_away, 1)
    mixed_other, grad_other = attend_backward(
        place, mixed, probs, grad_attended, qkv_low, 1, []
    )
    contract_got, expand_got, mixed_other, grad_other = lax.optimization_barrier(
        (contract_got, expand_got, mixed_other, grad_other)
    )
    contract_kept, contract_away = split(add(contract_kept, contract_got)[None], x)
    expand_kept, expand_away = add(expand_kept, expand_got)
    qkv_away = dot(h_one, mixed_other, ((0,), (0,))).astype(bf16)
    contract_away, proj_away, expand_away, qkv_away, grad_other = lax.optimization_barrier(
        (contract_away, proj_away, expand_away, qkv_away, grad_other)
    )
    contract_got, expand_got, proj_got, qkv_got = (
        swap_dp(contract_away, 1),
        swap_row(expand_away),
        swap_row(proj_away),
        swap_col(qkv_away),
    )
    output_tokens = tokens_apart(place, tokens, output_parts)
    outs = attend_backward(
        place, mixed, probs, grad_attended, qkv_low, 0, [grad_other, grad_middle, resid, params]
    )
    mixed_own, input_parts, sums_one = outs[0], outs[1:5], outs[5]
    contract_got, expand_got, proj_got, qkv_got, mixed_own = lax.optimization_barrier(
        (contract_got, expand_got, proj_got, qkv_got, mixed_own)
    )
    mlp_sum = jnp.concatenate(
        [add(contract_kept, contract_got), add(expand_kept, expand_got)[None]], axis=0
    )
    mlp_sum, mixed_own = over_z(mlp_sum, mixed_own)
    qkv_kept, qkv_away = halves(over_col(h_one, mixed_own, qkv_got), 0)
    qkv_got = swap_row(qkv_away)
    norm_sum = norm_over_dp(jnp.concatenate([norm_total(sums_one), norm_two], axis=0))
    qkv_got, input_parts, norm_sum = lax.optimization_barrier((qkv_got, input_parts, norm_sum))
    both = jnp.concatenate([stack(add(qkv_kept, qkv_got)), add(proj_kept, proj_got)], axis=0)
    both_kept, both_away = split(both[None], x)
    both_sum = add(both_kept, swap_dp(both_away, 1))
    input_parts = swap_all(input_parts)
    mlp_sum, input_parts = lax.optimization_barrier((mlp_sum, input_parts))
    mlp_sum = (mlp_sum, swap_dp(mlp_sum, 1))
    input_grad = tokens_apart(place, tokens, input_parts)
    both_sum = over_z_direct(both_sum)
    both_next = swap_dp(both_sum, 1)

    def adamw(weight, first, second, gradient, unit, block):
        return tuple(adamw_blocks(place, weight, first, second, *gradient, unit, block))

    expand_new = adamw(expand_weight, expand_first, expand_second, mlp_sum, 1, 0)
    contract_new = adamw(contract_weight, contract_first, contract_second, mlp_sum, 0, 0)
    both_next, expand_new, contract_new = lax.optimization_barrier(
        (both_next, expand_new, contract_new)
    )
    both_sum = (both_sum, both_next)
    qkv_new = adamw(qkv_weight, qkv_first, qkv_second, both_sum, 0, 0)
    proj_new = adamw(proj_weight, proj_first, proj_second, both_sum, 0, 3)
    norm_new = adamw_update(norm_params, norm_sum, norm_first, norm_second, rate_norm, 0.0)
    results = (output_tokens, input_grad, *qkv_new, *proj_new, *expand_new, *contract_new)
    return results + norm_new


def solution(mesh):
    tokens = P("dp", ("row", "col"))
    one = P("row", "col")
    two = P("col", "row")
    norm = P(None, ("row", "col"))
    in_specs = (tokens, tokens, one, two, one, two, norm)
    in_specs += (one, one, two, two, one, one, two, two, norm, norm)
    out_specs = (tokens, tokens) + (one,) * 3 + (two,) * 3 + (one,) * 3 + (two,) * 3 + (norm,) * 3
    return jax.shard_map(local, mesh=mesh, in_specs=in_specs, out_specs=out_specs, check_vma=False)
```

```python
import jax
import jax.numpy as jnp
from jax import lax
from jax.experimental import pallas as pl
from jax.experimental.pallas import tpu as pltpu
from jax.sharding import PartitionSpec as P

HEAD_DIM = 64
SEQ = 197
QROWS = 208
KROWS = 256
STEP = 10
ROWS = 1200
BLOCK = 608
STEPS = 6
GROUPED = 2
WIDE = 384
CHUNK = 768
MLP_ROWS = 1536

norm_epsilon = 1e-06
beta_first = 0.9
beta_second = 0.999
adam_epsilon = 1e-08
rate_matrix = 0.1
rate_norm = 0.5
decay_matrix = 0.05

GROUP = ("row", "col")
bf16 = jnp.bfloat16
f32 = jnp.float32


def dot(left, right, dims=((1,), (0,))):
    return lax.dot_general(left, right, (dims, ((), ())), preferred_element_type=f32)


def swap_halves(block):
    return jnp.concatenate([block[:, HEAD_DIM:], block[:, :HEAD_DIM]], axis=1)


def gelu_and_slope(value):
    size = jnp.abs(value)
    density = jnp.exp(value * value * -0.5)
    base = 1.0 + (0.3275911 * 0.5**0.5) * size
    t = pl.reciprocal(base, approx=True)
    t = t * (2.0 - base * t)
    series = t * (
        0.254829592
        + t * (-0.284496736 + t * (1.421413741 + t * (-1.453152027 + t * 1.061405429)))
    )
    tail = 0.5 * series * density
    phi = jnp.where(value >= 0, 1.0 - tail, tail)
    return (value * phi, phi + value * density * 0.3989422804014327)


def adamw_update(weight, gradient, first_old, second_old, rate_value, decay_value):
    first_new = beta_first * first_old + (1.0 - beta_first) * gradient
    second_new = beta_second * second_old + (1.0 - beta_second) * (gradient * gradient)
    first_hat = first_new / (1.0 - beta_first**STEP)
    second_hat = second_new / (1.0 - beta_second**STEP)
    moved = weight - rate_value * (
        first_hat / (jnp.sqrt(second_hat) + adam_epsilon) + decay_value * weight
    )
    return (moved, first_new, second_new)


def row_blocks(rows, size=BLOCK):
    return [slice(start, min(start + size, rows)) for start in range(0, rows, size)]


def norm_rows(values):
    center = jnp.mean(values, axis=1, keepdims=True)
    spread = jnp.mean(values * values, axis=1, keepdims=True) - center * center
    scaled = lax.rsqrt(spread + norm_epsilon)
    return ((values - center) * scaled, scaled)


def norm_backward(grad_normed, normed, scaled, gain_row):
    local_grad = grad_normed * gain_row
    first = jnp.mean(local_grad, axis=1, keepdims=True)
    second = jnp.mean(local_grad * normed, axis=1, keepdims=True)
    return scaled * (local_grad - first - normed * second)


def in_order(col, first, second):
    return jnp.where(
        col == 0,
        jnp.concatenate([first, second], axis=-1),
        jnp.concatenate([second, first], axis=-1),
    )


def split_features(col, array):
    part = array.shape[-1] // 4
    quarters = [array[..., i * part : (i + 1) * part] for i in range(4)]
    own = [jnp.where(col == 0, quarters[2 * i], quarters[2 * i + 1]) for i in range(2)]
    other = [jnp.where(col == 0, quarters[2 * i + 1], quarters[2 * i]) for i in range(2)]
    return [own[0], other[0], own[1], other[1]]


def resident(array):
    zeros = (0,) * array.ndim
    return pl.BlockSpec(array.shape, lambda i, *_: zeros, pipeline_mode=pl.Buffered(1))


def column_block(rows, width):
    return pl.BlockSpec((rows, width), lambda i, *_: (0, i))


def side_blocks(rows, width, along, steps):
    def first(i, *_):
        at = jnp.minimum(i, steps // 2 - 1)
        return (0, at) if along == 1 else (at, 0)

    def second(i, *_):
        at = jnp.maximum(i - steps // 2, 0)
        return (0, at) if along == 1 else (at, 0)

    block = (rows, width)
    return [pl.BlockSpec(block, first)] * 2 + [pl.BlockSpec(block, second)] * 2


def side_weight(refs, steps, axis):
    own = jnp.concatenate([refs[0][...], refs[1][...]], axis=axis)
    other = jnp.concatenate([refs[2][...], refs[3][...]], axis=axis)
    return jnp.where(pl.program_id(0) < steps // 2, own, other)


def split_parts(col, array):
    part = array.shape[0] // 4
    quarters = [array[i * part : (i + 1) * part] for i in range(4)]
    own = [jnp.where(col == 0, quarters[2 * i], quarters[2 * i + 1]) for i in range(2)]
    other = [jnp.where(col == 0, quarters[2 * i + 1], quarters[2 * i]) for i in range(2)]
    return [own[0], other[0], own[1], other[1]]


def together_kernel(place, *refs):
    parts, out_ref = refs[:4], refs[4]
    part, tokens = parts[0].shape
    wide = [ref[...].astype(f32) for ref in parts]
    for half in range(2):
        first, second = wide[2 * half], wide[2 * half + 1]
        both = [jnp.where(place[0] == 0, first, second), jnp.where(place[0] == 0, second, first)]
        block = jnp.concatenate(both, axis=0)
        at = 2 * part * half
        out_ref[0:tokens, at : at + 2 * part] = block.T.astype(bf16)
    low = tokens - tokens % 16
    row = lax.broadcasted_iota(jnp.int32, (out_ref.shape[0] - low, 1), 0) + low
    out_ref[low:, :] = jnp.where(row < tokens, out_ref[low:, :].astype(f32), 0.0).astype(bf16)


def tokens_together(place, parts):
    part, tokens = parts[0].shape
    padded = -(-tokens // ROWS) * ROWS
    return pl.pallas_call(
        together_kernel,
        in_specs=[pl.BlockSpec(memory_space=pltpu.SMEM)]
        + [pl.BlockSpec(memory_space=pltpu.VMEM)] * 4,
        out_specs=pl.BlockSpec(memory_space=pltpu.VMEM),
        out_shape=jax.ShapeDtypeStruct((padded, 4 * part), bf16),
        compiler_params=pltpu.CompilerParams(vmem_limit_bytes=40 * 2**20),
        cost_estimate=pl.CostEstimate(
            flops=0, bytes_accessed=16 * tokens * part, transcendentals=0
        ),
        name="tokens_together",
    )(place, *parts)


def apart_kernel(place, *refs):
    parts, out_ref = refs[:4], refs[4]
    tokens = out_ref.shape[1] // 4
    for block in range(4):
        for distance in range(4):

            @pl.when((place[1] ^ block) == distance)
            def _():
                columns = slice(block * tokens, (block + 1) * tokens)
                out_ref[:, columns] = parts[distance][...].astype(f32)[:, :tokens]


def tokens_apart(place, tokens, parts):
    part = parts[0].shape[0]
    return pl.pallas_call(
        apart_kernel,
        in_specs=[pl.BlockSpec(memory_space=pltpu.SMEM)]
        + [pl.BlockSpec(memory_space=pltpu.VMEM)] * 4,
        out_specs=pl.BlockSpec(memory_space=pltpu.VMEM),
        out_shape=jax.ShapeDtypeStruct((part, 4 * tokens), f32),
        compiler_params=pltpu.CompilerParams(vmem_limit_bytes=40 * 2**20),
        cost_estimate=pl.CostEstimate(
            flops=0, bytes_accessed=4 * tokens * part * 6, transcendentals=0
        ),
        name="tokens_apart",
    )(place, *parts).T


def forward_kernel(*refs):
    resid_ref, params = refs[:2]
    weights = refs[2:6]
    h_ref, mixed_ref, out_ref, probs_ref, wide, gathered = refs[6:]
    rows = resid_ref.shape[0]
    images = rows // SEQ
    tokens = images * SEQ
    steps = pl.num_programs(0)

    @pl.when(pl.program_id(0) == 0)
    def _():
        for block in row_blocks(rows):
            normed, _ = norm_rows(resid_ref[block, :].astype(f32))
            h_ref[block, :] = (normed * params[0:1, :] + params[1:2, :]).astype(bf16)

    weight = side_weight(weights, STEPS, 0)
    for block in row_blocks(rows):
        mixed = dot(h_ref[block, :], weight).astype(bf16)
        mixed_ref[block, :] = mixed
        wide[block, :] = mixed.astype(f32)
    wide[rows:, :] = jnp.zeros((wide.shape[0] - rows, 384), f32)
    low_lane = lax.broadcasted_iota(jnp.int32, (1, 128), 1) < HEAD_DIM
    key_lane = lax.broadcasted_iota(jnp.int32, (1, KROWS), 1) < SEQ
    scale = HEAD_DIM ** (-0.5)
    for group in range(0, images, GROUPED):
        members = range(group, min(group + GROUPED, images))
        scores, values = [], []
        for image in members:
            start = image * SEQ
            block_a = wide[start : start + KROWS, 0:128]
            block_b = wide[start : start + KROWS, 128:256]
            block_c = wide[start : start + KROWS, 256:384]
            query_0 = jnp.where(low_lane, block_a[:QROWS] * scale, 0.0).astype(bf16)
            query_1 = jnp.where(low_lane, 0.0, block_b[:QROWS] * scale).astype(bf16)
            scores.append(dot(query_0, swap_halves(block_a).astype(bf16), ((1,), (1,))))
            scores.append(dot(query_1, swap_halves(block_c).astype(bf16), ((1,), (1,))))
            values += [block_b.astype(bf16), block_c.astype(bf16)]
        scores = [jnp.where(key_lane, score, -1e30) for score in scores]
        tops = [jnp.max(score, axis=1, keepdims=True) for score in scores]
        exponents = [jnp.exp(score - top) for score, top in zip(scores, tops)]
        totals = [jnp.sum(exponent, axis=1, keepdims=True) for exponent in exponents]
        probs = [(e * (1.0 / total)).astype(bf16) for e, total in zip(exponents, totals)]
        outs = [dot(prob, value) for prob, value in zip(probs, values)]
        for at, image in enumerate(members):
            start = image * SEQ
            probs_ref[0, image * 2] = probs[2 * at]
            probs_ref[0, image * 2 + 1] = probs[2 * at + 1]
            gathered[start : start + QROWS, :] = jnp.where(
                low_lane, outs[2 * at], outs[2 * at + 1]
            )
    gathered[tokens:, :] = jnp.zeros((gathered.shape[0] - tokens, 128), f32)
    out_ref[...] = gathered[0:rows, :].astype(bf16)


def attend_forward(resid, params, weights):
    rows, width = resid.shape
    images = rows // SEQ
    padded = -(-((images - 1) * SEQ + KROWS) // 16) * 16
    pair_probs = (STEPS, 2 * images, QROWS, KROWS)
    half_rows = weights[0].shape[0]
    return pl.pallas_call(
        forward_kernel,
        grid=(STEPS,),
        in_specs=[resident(resid), resident(params), *side_blocks(half_rows, 384, 1, STEPS)],
        out_specs=[
            pl.BlockSpec((rows, width), lambda i: (0, 0)),
            column_block(rows, 384),
            column_block(rows, 128),
            pl.BlockSpec((1, *pair_probs[1:]), lambda i: (i, 0, 0, 0)),
        ],
        out_shape=[
            jax.ShapeDtypeStruct((rows, width), bf16),
            jax.ShapeDtypeStruct((rows, STEPS * 384), bf16),
            jax.ShapeDtypeStruct((rows, STEPS * 128), bf16),
            jax.ShapeDtypeStruct(pair_probs, bf16),
        ],
        scratch_shapes=[pltpu.VMEM((padded, 384), f32), pltpu.VMEM((padded, 128), f32)],
        compiler_params=pltpu.CompilerParams(vmem_limit_bytes=48 * 2**20),
        cost_estimate=pl.CostEstimate(
            flops=20 * 10**9, bytes_accessed=rows * width * 20, transcendentals=10**6
        ),
        name="attend_forward",
    )(resid, params, *weights)


def backward_kernel(first, started, last, place, *refs):
    mixed_ref, probs_ref, grad_ref = refs[:3]
    weights, refs = refs[3:7], refs[7:]
    if started:
        before_ref, refs = refs[0], refs[1:]
    if last:
        middle_ref, resid_ref, params = refs[:3]
        out_ref, out_parts, sums_ref = refs[3], refs[4:8], refs[8]
        wide, grad_wide, gathered, total = refs[9:]
    else:
        out_ref, total = refs[:2]
        wide, grad_wide, gathered = refs[2:]
    rows = mixed_ref.shape[0]
    images = rows // SEQ
    tokens = images * SEQ
    wide[rows:, :] = jnp.zeros((wide.shape[0] - rows, 384), f32)
    wide[0:rows, :] = mixed_ref[...].astype(f32)
    grad_wide[0:rows, :] = grad_ref[...].astype(f32)
    low_lane = lax.broadcasted_iota(jnp.int32, (1, 128), 1) < HEAD_DIM
    query_row = lax.broadcasted_iota(jnp.int32, (QROWS, 128), 0) < SEQ
    scale = HEAD_DIM ** (-0.5)
    for group in range(0, images, GROUPED):
        members = range(group, min(group + GROUPED, images))
        grad_probs, grad_values, probs, swapped = [], [], [], []
        for image in members:
            start = image * SEQ
            block_a = wide[start : start + KROWS, 0:128]
            block_b = wide[start : start + KROWS, 128:256]
            block_c = wide[start : start + KROWS, 256:384]
            grad = jnp.where(query_row, grad_wide[start : start + QROWS, :], 0.0)
            grad_low = grad.astype(bf16)
            probs_0 = probs_ref[0, 2 * image]
            probs_1 = probs_ref[0, 2 * image + 1]
            probs += [probs_0, probs_1]
            part_0 = jnp.where(low_lane, grad, 0.0).astype(bf16)
            part_1 = jnp.where(low_lane, 0.0, grad).astype(bf16)
            grad_probs.append(dot(part_0, block_b.astype(bf16), ((1,), (1,))))
            grad_probs.append(dot(part_1, block_c.astype(bf16), ((1,), (1,))))
            grad_values.append(dot(probs_0, grad_low, ((0,), (0,))))
            grad_values.append(dot(probs_1, grad_low, ((0,), (0,))))
            swapped.append(
                [(swap_halves(block) * scale).astype(bf16) for block in (block_a, block_b, block_c)]
            )
        wide_probs = [prob.astype(f32) for prob in probs]
        inner = [
            jnp.sum(prob * grad, axis=1, keepdims=True)
            for prob, grad in zip(wide_probs, grad_probs)
        ]
        score_grads = [
            (prob * (grad - each)).astype(bf16)
            for prob, grad, each in zip(wide_probs, grad_probs, inner)
        ]
        for at, image in enumerate(members):
            start = image * SEQ
            swapped_a, swapped_b, swapped_c = swapped[at]
            score_0, score_1 = score_grads[2 * at : 2 * at + 2]
            grad_v0, grad_v1 = grad_values[2 * at : 2 * at + 2]
            grad_q0 = dot(score_0, swapped_a)
            grad_k0 = dot(score_0, swapped_a[:QROWS], ((0,), (0,)))
            grad_q1 = dot(score_1, swapped_c)
            grad_k1 = dot(score_1, swapped_b[:QROWS], ((0,), (0,)))
            block = slice(start, start + QROWS)
            gathered[block, 0:128] = jnp.where(low_lane, grad_q0, grad_k0[:QROWS])
            gathered[block, 128:256] = jnp.where(low_lane, grad_v0[:QROWS], grad_q1)
            gathered[block, 256:384] = jnp.where(low_lane, grad_k1[:QROWS], grad_v1[:QROWS])
    gathered[tokens:, :] = jnp.zeros((gathered.shape[0] - tokens, 384), f32)
    step = pl.program_id(0)
    weight = jnp.where(
        (first + step) % STEPS < STEPS // 2,
        jnp.concatenate([weights[0][...], weights[1][...]], axis=0),
        jnp.concatenate([weights[2][...], weights[3][...]], axis=0),
    )

    @pl.when(step == 0)
    def _():
        total[...] = before_ref[...] if started else jnp.zeros_like(total)

    for block in row_blocks(rows):
        grad_mixed = gathered[block, :].astype(bf16)
        out_ref[block, :] = grad_mixed
        total[block, :] += dot(grad_mixed, weight, ((1,), (1,)))

    if not last:
        return

    @pl.when(step == pl.num_programs(0) - 1)
    def _():
        gain = jnp.zeros((1, total.shape[1]), f32)
        shift = jnp.zeros((1, total.shape[1]), f32)
        for block in row_blocks(rows):
            grad_one = total[block, :]
            normed, scaled = norm_rows(resid_ref[block, :].astype(f32))
            gain += jnp.sum(grad_one * normed, axis=0, keepdims=True)
            shift += jnp.sum(grad_one, axis=0, keepdims=True)
            total[block, :] = middle_ref[block, :] + norm_backward(
                grad_one, normed, scaled, params[0:1, :]
            )
        sums_ref[0:1, :] = gain
        sums_ref[1:2, :] = shift
        for part_ref, part in zip(out_parts, split_parts(place[0], total[...].T)):
            part_ref[...] = part.astype(bf16)


def attend_backward(place, mixed, probs, grad_attended, weights, first, before, rest):
    rows, width = grad_attended.shape
    images = rows // SEQ
    steps = 2
    padded = -(-((images - 1) * SEQ + KROWS) // 16) * 16
    part = jax.ShapeDtypeStruct((width // 4, rows), bf16)
    sums = jax.ShapeDtypeStruct((2, width), f32)
    whole = jax.ShapeDtypeStruct((rows, width), f32)
    extra = [part] * 4 + [sums] if rest else [whole]
    scratch = [
        pltpu.VMEM((padded, 384), f32),
        pltpu.VMEM((padded, 128), f32),
        pltpu.VMEM((padded, 384), f32),
    ]
    if rest:
        scratch.append(pltpu.VMEM((rows, width), f32))
    weight_rows = weights[0].shape[0]
    side = STEPS // 2

    def pair(i):
        return (first + i) % STEPS

    return pl.pallas_call(
        lambda *refs: backward_kernel(first, bool(before), bool(rest), *refs),
        grid_spec=pltpu.PrefetchScalarGridSpec(
            num_scalar_prefetch=1,
            grid=(steps,),
            in_specs=[
                pl.BlockSpec((rows, 384), lambda i, *_: (0, pair(i))),
                pl.BlockSpec((1, *probs.shape[1:]), lambda i, *_: (pair(i), 0, 0, 0)),
                pl.BlockSpec((rows, 128), lambda i, *_: (0, pair(i))),
                *[pl.BlockSpec((weight_rows, 384), lambda i, *_: (0, pair(i) % side))] * 4,
                *[resident(each) for each in (*before, *rest)],
            ],
            out_specs=[
                column_block(rows, 384),
                *[pl.BlockSpec(each.shape, lambda i, *_: (0, 0)) for each in extra],
            ],
            scratch_shapes=scratch,
        ),
        out_shape=[jax.ShapeDtypeStruct((rows, steps * 384), bf16), *extra],
        compiler_params=pltpu.CompilerParams(vmem_limit_bytes=48 * 2**20),
        name="attend_backward",
    )(place, mixed, probs, grad_attended, *weights, *before, *rest)


def block_kernel(place, *refs):
    resid_ref, attended_ref, grad_ref, params = refs[:4]
    expand, contract, proj = refs[4:8], refs[8:12], refs[12:16]
    out_parts = refs[16:20]
    h_ref, hidden_ref, pre_ref, middle_ref, attended_grad_ref, sums_ref = refs[20:26]
    output, grad_two = refs[26:]
    middle = middle_ref
    rows = resid_ref.shape[0]
    step = pl.program_id(0)
    blocks = row_blocks(rows, 400)

    def proj_low():
        own = jnp.concatenate([proj[0][...], proj[1][...]], axis=1)
        return jnp.concatenate([own, jnp.concatenate([proj[2][...], proj[3][...]], axis=1)], axis=0)

    @pl.when(step == 0)
    def _():
        weight = proj_low()
        for block in blocks:
            value = resid_ref[block, :].astype(f32) + dot(attended_ref[block, :], weight)
            middle[block, :] = value
            output[block, :] = value
            grad_two[block, :] = jnp.zeros_like(value)
            normed, _ = norm_rows(value)
            h_ref[block, :] = (normed * params[2:3, :] + params[3:4, :]).astype(bf16)

    own_side = step < pl.num_programs(0) // 2

    def expand_side(own, other):
        upper = jnp.concatenate([own[at : at + WIDE, :] for at in range(0, CHUNK, WIDE)], axis=1)
        lower = jnp.concatenate([other[at : at + WIDE, :] for at in range(0, CHUNK, WIDE)], axis=1)
        return jnp.concatenate([upper, lower], axis=0)

    expand_low = jnp.where(
        own_side, expand_side(expand[0], expand[1]), expand_side(expand[2], expand[3])
    )
    contract_low = jnp.where(
        own_side,
        jnp.concatenate([contract[0][...], contract[1][...]], axis=1),
        jnp.concatenate([contract[2][...], contract[3][...]], axis=1),
    )

    def products(block):
        return (
            dot(h_ref[block, :], expand_low),
            dot(grad_ref[block, :], contract_low, ((1,), (1,))),
        )

    ahead = products(blocks[0])
    for at, block in enumerate(blocks):
        before, grad_hidden = ahead
        if at + 1 < len(blocks):
            ahead = products(blocks[at + 1])
        value, slope = gelu_and_slope(before)
        hidden = value.astype(bf16)
        grad_pre = (grad_hidden * slope).astype(bf16)
        hidden_ref[block, :] = hidden
        pre_ref[block, :] = grad_pre
        output[block, :] += dot(hidden, contract_low)
        grad_two[block, :] += dot(grad_pre, expand_low, ((1,), (1,)))

    @pl.when(step == pl.num_programs(0) - 1)
    def _():
        weight = proj_low()
        gain = jnp.zeros((1, middle.shape[1]), f32)
        shift = jnp.zeros((1, middle.shape[1]), f32)
        for block in blocks:
            grad = grad_two[block, :]
            normed, scaled = norm_rows(middle[block, :])
            gain += jnp.sum(grad * normed, axis=0, keepdims=True)
            shift += jnp.sum(grad, axis=0, keepdims=True)
            grad_middle = grad_ref[block, :].astype(f32) + norm_backward(
                grad, normed, scaled, params[2:3, :]
            )
            middle_ref[block, :] = grad_middle
            attended_grad_ref[block, :] = dot(
                grad_middle.astype(bf16), weight, ((1,), (1,))
            ).astype(bf16)
        sums_ref[0:1, :] = gain
        sums_ref[1:2, :] = shift
        for part_ref, part in zip(out_parts, split_parts(place[0], output[...].T)):
            part_ref[...] = part.astype(bf16)


def chunk_blocks(first, steps):
    def own(i, *_):
        return (first + jnp.minimum(i, steps // 2 - 1), 0)

    def other(i, *_):
        return (first + jnp.maximum(i - steps // 2, 0), 0)

    return [pl.BlockSpec((CHUNK, WIDE), own)] * 2 + [pl.BlockSpec((CHUNK, WIDE), other)] * 2


def block_middle(place, resid, attended, grad, params, weights):
    rows, width = resid.shape
    ff = 2 * MLP_ROWS
    chunk = CHUNK
    steps = ff // CHUNK
    part = jax.ShapeDtypeStruct((width // 4, rows), bf16)
    narrow = jax.ShapeDtypeStruct((rows, width), bf16)
    broad = jax.ShapeDtypeStruct((rows, ff), bf16)
    wide = jax.ShapeDtypeStruct((rows, width), f32)
    sums = jax.ShapeDtypeStruct((2, width), f32)

    def fixed(shape):
        return pl.BlockSpec(shape.shape, lambda i, *_: (0, 0), pipeline_mode=pl.Buffered(1))

    return pl.pallas_call(
        block_kernel,
        grid_spec=pltpu.PrefetchScalarGridSpec(
            num_scalar_prefetch=1,
            grid=(steps,),
            in_specs=[
                *[resident(each) for each in (resid, attended, grad, params)],
                *chunk_blocks(0, steps),
                *chunk_blocks(steps // 2, steps),
                *[
                    pl.BlockSpec(
                        (WIDE, WIDE),
                        lambda i, *_: (2 * MLP_ROWS // WIDE, 0),
                        pipeline_mode=pl.Buffered(1),
                    )
                ]
                * 4,
            ],
            out_specs=[
                *[fixed(part)] * 4,
                fixed(narrow),
                column_block(rows, chunk),
                column_block(rows, chunk),
                fixed(wide),
                fixed(narrow),
                fixed(sums),
            ],
            scratch_shapes=[pltpu.VMEM((rows, width), f32)] * 2,
        ),
        out_shape=[*[part] * 4, narrow, broad, broad, wide, narrow, sums],
        compiler_params=pltpu.CompilerParams(vmem_limit_bytes=56 * 2**20),
        cost_estimate=pl.CostEstimate(
            flops=2 * rows * width * (4 * ff + 2 * width),
            bytes_accessed=rows * ff * 8,
            transcendentals=2 * rows * ff,
        ),
        name="block_middle",
    )(place, resid, attended, grad, params, *weights, *weights, *weights)


def adamw_kernel(first_block, place, weight, first, second, here, there, *outs):
    block = pl.program_id(0) + first_block
    mine = jnp.where(block // 2 == place[2], here[0].astype(f32), there[0].astype(f32))
    results = adamw_update(
        weight[...], mine, first[...], second[...], rate_matrix, decay_matrix
    )
    for out, result in zip(outs, results):
        out[...] = result


def adamw_blocks(place, weight, first, second, here, there, unit, first_block):
    rows, width = weight.shape
    if rows == WIDE:
        piece = pl.BlockSpec((WIDE, WIDE), lambda i, *_: (0, i))
    else:
        piece = pl.BlockSpec((WIDE, WIDE), lambda i, *_: (i, 0))
    part = pl.BlockSpec((1, WIDE, WIDE), lambda i, *_: (unit, (i + first_block) % 2, 0))
    return pl.pallas_call(
        lambda *refs: adamw_kernel(first_block, *refs),
        grid_spec=pltpu.PrefetchScalarGridSpec(
            num_scalar_prefetch=1,
            grid=(rows * width // WIDE**2,),
            in_specs=[piece, piece, piece, part, part],
            out_specs=[piece] * 3,
        ),
        out_shape=[jax.ShapeDtypeStruct((rows, width), f32)] * 3,
        compiler_params=pltpu.CompilerParams(vmem_limit_bytes=40 * 2**20),
        cost_estimate=pl.CostEstimate(
            flops=20 * rows * width, bytes_accessed=28 * rows * width, transcendentals=0
        ),
        name="adamw_blocks",
    )(place, weight, first, second, here, there)


def local(
    tokens_in,
    out_grad,
    qkv_weight,
    proj_weight,
    expand_weight,
    contract_weight,
    norm_params,
    qkv_first,
    qkv_second,
    proj_first,
    proj_second,
    expand_first,
    expand_second,
    contract_first,
    contract_second,
    norm_first,
    norm_second,
):
    row = lax.axis_index("row")
    col = lax.axis_index("col")
    dp = lax.axis_index("dp")
    n_dp = lax.axis_size("dp")
    me = 2 * row + col
    place = jnp.stack([col, me, dp % 2, dp // 2]).astype(jnp.int32)
    tokens = tokens_in.shape[0] // 4
    part = tokens_in.shape[1]

    def swap(array, distance):
        if distance == 0:
            return array
        return lax.ppermute(array, GROUP, [(i, i ^ distance) for i in range(4)])

    def swap_dp(array, distance):
        return lax.ppermute(array, "dp", [(i, i ^ distance) for i in range(n_dp)])

    def swap_row(array):
        return swap(array, 2)

    def swap_col(array):
        return swap(array, 1)

    def token_blocks(array):
        return [lax.dynamic_slice(array, ((me ^ d) * tokens, 0), (tokens, part)) for d in range(4)]

    def swap_all(blocks):
        return [swap(block, d) for d, block in enumerate(blocks)]

    def ordered(bit, mine, partner):
        return jnp.where(
            bit == 0,
            jnp.concatenate([mine, partner], axis=0),
            jnp.concatenate([partner, mine], axis=0),
        )

    def dp_part(mine, count):
        rows = mine.shape[0] // count
        return lax.dynamic_slice_in_dim(mine, (dp % count) * rows, rows)

    def all_blocks(mine, partner):
        return [mine, partner, swap_col(mine), swap_col(partner)]

    x, z = dp % 2, dp // 2
    z_low, z_high = z % 2, z // 2 % 2

    def stack(array):
        blocks = [array[..., at : at + WIDE] for at in range(0, array.shape[-1], WIDE)]
        return jnp.concatenate(blocks, axis=-2)

    resid_parts = swap_all(token_blocks(tokens_in))
    qkv_mine = qkv_weight.astype(bf16)
    qkv_got = swap_row(dp_part(qkv_mine, 2))
    rest_mine = jnp.concatenate(
        [stack(expand_weight), contract_weight, proj_weight], axis=0
    ).astype(bf16)
    params = [swap(norm_params, d) for d in range(4)]
    resid_parts, params, qkv_got, rest_got = lax.optimization_barrier(
        (resid_parts, params, qkv_got, dp_part(rest_mine, 4))
    )
    params = jnp.concatenate(
        [in_order(col, params[0], params[1]), in_order(col, params[2], params[3])], axis=1
    )
    qkv_next, rest_got = swap_dp(qkv_got, 1), swap_row(rest_got)
    resid = tokens_together(place, [each.T for each in resid_parts])
    qkv_next, rest_got, grad_blocks, resid = lax.optimization_barrier(
        (qkv_next, rest_got, token_blocks(out_grad), resid)
    )
    qkv_low = all_blocks(qkv_mine, ordered(x, qkv_got, qkv_next))
    rest_x, rest_z = swap_dp(rest_got, 1), swap_dp(rest_got, 2)
    grad_parts = swap_all(grad_blocks)
    rest_away = swap_col(rest_mine)
    h_one, mixed, attended, probs = attend_forward(resid, params, qkv_low)
    attended, rest_x, rest_z, grad_parts, rest_away = lax.optimization_barrier(
        (attended, rest_x, rest_z, grad_parts, rest_away)
    )
    cut = rest_got.shape[0] // 2
    rest_last = jnp.concatenate([swap_dp(rest_z[:cut], 1), swap_dp(rest_x[cut:], 2)], axis=0)
    rest_row = ordered(z_low, ordered(x, rest_got, rest_x), ordered(x, rest_z, rest_last))
    rest_low = [rest_mine, rest_row, rest_away, swap_col(rest_row)]
    grad_low = tokens_together(place, [each.T for each in grad_parts])
    outs = block_middle(place, resid, attended, grad_low, params, rest_low)
    output_parts = swap_all(outs[:4])
    h_two, hidden, grad_pre, grad_middle, grad_attended, sums_two = outs[4:]

    def halves(array, axis):
        size = array.shape[axis] // 2
        return (
            lax.slice_in_dim(array, 0, size, axis=axis),
            lax.slice_in_dim(array, size, 2 * size, axis=axis),
        )

    def over_col(left, right, received):
        total = dot(left, right, ((0,), (0,))) + received.astype(f32)
        return total.astype(bf16)

    def split(array, bit):
        size = array.shape[1] // 2
        kept = lax.dynamic_slice_in_dim(array, bit * size, size, 1)
        return kept, lax.dynamic_slice_in_dim(array, (1 - bit) * size, size, 1)

    def add(kept, received):
        return (kept.astype(f32) + received.astype(f32)).astype(bf16)

    def join(bit, mine, partner):
        return jnp.where(
            bit == 0,
            jnp.concatenate([mine, partner], axis=1),
            jnp.concatenate([partner, mine], axis=1),
        )

    same_x = [[i for i in range(n_dp) if i % 2 == bit] for bit in range(2)]

    def norm_total(sums):
        parts = split_features(col, sums)
        return parts[0] + sum(swap(parts[d], d) for d in range(1, 4))


    hidden_own, hidden_other = halves(hidden, 1)
    pre_own, pre_other = halves(grad_pre, 1)
    attended_own, attended_other = halves(attended, 1)
    branch = grad_middle.astype(bf16)
    contract_got = swap_col(dot(hidden_other, grad_low, ((0,), (0,))).astype(bf16))
    expand_got = swap_col(dot(h_two, pre_other, ((0,), (0,))).astype(bf16))
    contract_sum = over_col(hidden_own, grad_low, contract_got)
    contract_kept, contract_away = halves(contract_sum, 1)
    contract_away, pre_own, branch = lax.optimization_barrier((contract_away, pre_own, branch))
    contract_got = swap_row(contract_away)
    proj_got = swap_col(dot(attended_other, branch, ((0,), (0,))).astype(bf16))
    expand_sum = over_col(h_two, pre_own, expand_got)
    expand_sum = stack(expand_sum.reshape(2, WIDE, expand_sum.shape[1]))
    expand_kept, expand_away = split(expand_sum, x)
    proj_kept, proj_away = halves(over_col(attended_own, branch, proj_got), 1)
    norm_two = norm_total(sums_two)
    expand_away, proj_away, norm_two, output_parts, grad_attended = lax.optimization_barrier(
        (expand_away, proj_away, norm_two, output_parts, grad_attended)
    )
    expand_got = swap_dp(expand_away, 1)
    mixed_a, total = attend_backward(place, mixed, probs, grad_attended, qkv_low, 3, [], [])
    contract_got, expand_got, mixed_a, total = lax.optimization_barrier(
        (contract_got, expand_got, mixed_a, total)
    )
    contract_kept, contract_away = split(add(contract_kept, contract_got)[None], x)
    expand_kept, expand_away = add(expand_kept, expand_got)
    expand_away = jnp.concatenate([expand_away, proj_away], axis=0)
    contract_away, expand_away, total = lax.optimization_barrier(
        (contract_away, expand_away, total)
    )
    contract_got, expand_got = swap_dp(contract_away, 1), swap_row(expand_away)
    output_tokens = tokens_apart(place, tokens, output_parts)
    mixed_b, total = attend_backward(
        place, mixed, probs, grad_attended, qkv_low, 5, [total], []
    )
    contract_got, expand_got, mixed_b, total = lax.optimization_barrier(
        (contract_got, expand_got, mixed_b, total)
    )
    expand_got, proj_got = expand_got[: expand_kept.shape[0]], expand_got[expand_kept.shape[0] :]
    mlp_sum = jnp.concatenate(
        [add(contract_kept, contract_got), add(expand_kept, expand_got)[None]], axis=0
    )
    mlp_kept, mlp_away = split(mlp_sum, z_low)
    qkv_away = jnp.concatenate(
        [
            dot(h_one, mixed_a, ((0,), (0,))).astype(bf16),
            dot(h_one, mixed_b[:, :WIDE], ((0,), (0,))).astype(bf16),
        ],
        axis=1,
    )
    mlp_away, qkv_away, total = lax.optimization_barrier((mlp_away, qkv_away, total))
    mlp_got, qkv_got = swap_dp(mlp_away, 2), swap_col(qkv_away)
    outs = attend_backward(
        place, mixed, probs, grad_attended, qkv_low, 1, [total], [grad_middle, resid, params]
    )
    mixed_c, input_parts, sums_one = outs[0], outs[1:5], outs[5]
    mlp_got, qkv_got, mixed_c = lax.optimization_barrier((mlp_got, qkv_got, mixed_c))
    if n_dp == 8:
        mlp_sum = add(mlp_kept, mlp_got)
        mlp_kept, mlp_away = split(mlp_sum, z_high)
        mlp_away, mixed_c = lax.optimization_barrier((mlp_away, mixed_c))
        mlp_sum = add(mlp_kept, swap_dp(mlp_away, 4))
        mlp_sum = join(z_high, mlp_sum, swap_dp(mlp_sum, 4))
        mlp_sum = join(z_low, mlp_sum, swap_dp(mlp_sum, 2))
    else:
        mlp_sum = lax.psum(mlp_sum, "dp", axis_index_groups=same_x)
    qkv_sum = jnp.concatenate(
        [dot(h_one, mixed_b[:, WIDE:], ((0,), (0,))), dot(h_one, mixed_c, ((0,), (0,)))], axis=1
    )
    qkv_kept, qkv_away = halves((qkv_sum + qkv_got.astype(f32)).astype(bf16), 0)
    qkv_got = swap_row(qkv_away)
    norm_sum = jnp.concatenate([norm_total(sums_one), norm_two], axis=0)
    qkv_got, input_parts, norm_sum = lax.optimization_barrier((qkv_got, input_parts, norm_sum))
    both = jnp.concatenate([stack(add(qkv_kept, qkv_got)), add(proj_kept, proj_got)], axis=0)
    both_kept, both_away = split(both[None], x)
    both_got = swap_dp(both_away, 1)
    input_parts = swap_all(input_parts)
    if n_dp == 8:
        norm_got = swap_dp(norm_sum, 1)
        both_got, norm_got = lax.optimization_barrier((both_got, norm_got))
        both_sum, norm_sum = add(both_kept, both_got), norm_sum + norm_got
        size = both_sum.shape[1] // 4
        parts = [lax.dynamic_slice_in_dim(both_sum, (z ^ d) * size, size, 1) for d in range(4)]
        parts = [parts[0]] + [swap_dp(parts[d], 2 * d) for d in range(1, 4)]
        norm_got = swap_dp(norm_sum, 2)
        parts, norm_got, input_parts = lax.optimization_barrier((parts, norm_got, input_parts))
        mine, norm_sum = sum(each.astype(f32) for each in parts).astype(bf16), norm_sum + norm_got
        parts = [mine] + [swap_dp(mine, 2 * d) for d in range(1, 4)]
        norm_got = swap_dp(norm_sum, 4)
        parts, norm_got = lax.optimization_barrier((parts, norm_got))
        norm_sum = norm_sum + norm_got
        both_sum = join(z_high, join(z_low, *parts[:2]), join(z_low, *parts[2:]))
    else:
        norm_sum = lax.psum(norm_sum, "dp")
        both_sum = lax.psum(add(both_kept, both_got), "dp", axis_index_groups=same_x)
    mlp_sum = (mlp_sum, swap_dp(mlp_sum, 1))
    both_next = swap_dp(both_sum, 1)
    input_grad = tokens_apart(place, tokens, input_parts)

    def adamw(weight, first, second, gradient, unit, block):
        return tuple(adamw_blocks(place, weight, first, second, *gradient, unit, block))

    expand_new = adamw(expand_weight, expand_first, expand_second, mlp_sum, 1, 0)
    contract_new = adamw(contract_weight, contract_first, contract_second, mlp_sum, 0, 0)
    both_next, expand_new, contract_new = lax.optimization_barrier(
        (both_next, expand_new, contract_new)
    )
    both_sum = (both_sum, both_next)
    qkv_new = adamw(qkv_weight, qkv_first, qkv_second, both_sum, 0, 0)
    proj_new = adamw(proj_weight, proj_first, proj_second, both_sum, 0, 3)
    norm_new = adamw_update(norm_params, norm_sum, norm_first, norm_second, rate_norm, 0.0)
    results = (output_tokens, input_grad, *qkv_new, *proj_new, *expand_new, *contract_new)
    return results + norm_new


def solution(mesh):
    tokens = P("dp", ("row", "col"))
    one = P("row", "col")
    two = P("col", "row")
    norm = P(None, ("row", "col"))
    in_specs = (tokens, tokens, one, two, one, two, norm)
    in_specs += (one, one, two, two, one, one, two, two, norm, norm)
    out_specs = (tokens, tokens) + (one,) * 3 + (two,) * 3 + (one,) * 3 + (two,) * 3 + (norm,) * 3
    return jax.shard_map(local, mesh=mesh, in_specs=in_specs, out_specs=out_specs, check_vma=False)
```

```python
import jax
import jax.numpy as jnp
from jax import lax
from jax.experimental import pallas as pl
from jax.experimental.pallas import tpu as pltpu
from jax.sharding import PartitionSpec as P

HEAD_DIM = 64
SEQ = 197
QROWS = 208
KROWS = 256
STEP = 10
ROWS = 1200
BLOCK = 608
STEPS = 6
GROUPED = 2
WIDE = 384
CHUNK = 768
MLP_ROWS = 1536

norm_epsilon = 1e-06
beta_first = 0.9
beta_second = 0.999
adam_epsilon = 1e-08
rate_matrix = 0.1
rate_norm = 0.5
decay_matrix = 0.05

GROUP = ("row", "col")
bf16 = jnp.bfloat16
f32 = jnp.float32


def dot(left, right, dims=((1,), (0,))):
    return lax.dot_general(left, right, (dims, ((), ())), preferred_element_type=f32)


def swap_halves(block):
    return jnp.concatenate([block[:, HEAD_DIM:], block[:, :HEAD_DIM]], axis=1)


def gelu_and_slope(value):
    size = jnp.abs(value)
    density = jnp.exp(value * value * -0.5)
    base = 1.0 + (0.3275911 * 0.5**0.5) * size
    t = pl.reciprocal(base, approx=True)
    t = t * (2.0 - base * t)
    series = t * (
        0.254829592
        + t * (-0.284496736 + t * (1.421413741 + t * (-1.453152027 + t * 1.061405429)))
    )
    tail = 0.5 * series * density
    phi = jnp.where(value >= 0, 1.0 - tail, tail)
    return (value * phi, phi + value * density * 0.3989422804014327)


def adamw_update(weight, gradient, first_old, second_old, rate_value, decay_value):
    first_new = beta_first * first_old + (1.0 - beta_first) * gradient
    second_new = beta_second * second_old + (1.0 - beta_second) * (gradient * gradient)
    first_hat = first_new / (1.0 - beta_first**STEP)
    second_hat = second_new / (1.0 - beta_second**STEP)
    moved = weight - rate_value * (
        first_hat / (jnp.sqrt(second_hat) + adam_epsilon) + decay_value * weight
    )
    return (moved, first_new, second_new)


def row_blocks(rows, size=BLOCK):
    return [slice(start, min(start + size, rows)) for start in range(0, rows, size)]


def norm_rows(values):
    center = jnp.mean(values, axis=1, keepdims=True)
    spread = jnp.mean(values * values, axis=1, keepdims=True) - center * center
    scaled = lax.rsqrt(spread + norm_epsilon)
    return ((values - center) * scaled, scaled)


def norm_backward(grad_normed, normed, scaled, gain_row):
    local_grad = grad_normed * gain_row
    first = jnp.mean(local_grad, axis=1, keepdims=True)
    second = jnp.mean(local_grad * normed, axis=1, keepdims=True)
    return scaled * (local_grad - first - normed * second)


def in_order(col, first, second):
    return jnp.where(
        col == 0,
        jnp.concatenate([first, second], axis=-1),
        jnp.concatenate([second, first], axis=-1),
    )


def split_features(col, array):
    part = array.shape[-1] // 4
    quarters = [array[..., i * part : (i + 1) * part] for i in range(4)]
    own = [jnp.where(col == 0, quarters[2 * i], quarters[2 * i + 1]) for i in range(2)]
    other = [jnp.where(col == 0, quarters[2 * i + 1], quarters[2 * i]) for i in range(2)]
    return [own[0], other[0], own[1], other[1]]


def resident(array):
    zeros = (0,) * array.ndim
    return pl.BlockSpec(array.shape, lambda i, *_: zeros, pipeline_mode=pl.Buffered(1))


def column_block(rows, width):
    return pl.BlockSpec((rows, width), lambda i, *_: (0, i))


def side_blocks(rows, width, along, steps):
    def first(i, *_):
        at = jnp.minimum(i, steps // 2 - 1)
        return (0, at) if along == 1 else (at, 0)

    def second(i, *_):
        at = jnp.maximum(i - steps // 2, 0)
        return (0, at) if along == 1 else (at, 0)

    block = (rows, width)
    return [pl.BlockSpec(block, first)] * 2 + [pl.BlockSpec(block, second)] * 2


def side_weight(refs, steps, axis):
    own = jnp.concatenate([refs[0][...], refs[1][...]], axis=axis)
    other = jnp.concatenate([refs[2][...], refs[3][...]], axis=axis)
    return jnp.where(pl.program_id(0) < steps // 2, own, other)


def split_parts(col, array):
    part = array.shape[0] // 4
    quarters = [array[i * part : (i + 1) * part] for i in range(4)]
    own = [jnp.where(col == 0, quarters[2 * i], quarters[2 * i + 1]) for i in range(2)]
    other = [jnp.where(col == 0, quarters[2 * i + 1], quarters[2 * i]) for i in range(2)]
    return [own[0], other[0], own[1], other[1]]


def together_kernel(place, *refs):
    parts, out_ref = refs[:4], refs[4]
    part, tokens = parts[0].shape
    wide = [ref[...].astype(f32) for ref in parts]
    for half in range(2):
        first, second = wide[2 * half], wide[2 * half + 1]
        both = [jnp.where(place[0] == 0, first, second), jnp.where(place[0] == 0, second, first)]
        block = jnp.concatenate(both, axis=0)
        at = 2 * part * half
        out_ref[0:tokens, at : at + 2 * part] = block.T.astype(bf16)
    low = tokens - tokens % 16
    row = lax.broadcasted_iota(jnp.int32, (out_ref.shape[0] - low, 1), 0) + low
    out_ref[low:, :] = jnp.where(row < tokens, out_ref[low:, :].astype(f32), 0.0).astype(bf16)


def tokens_together(place, parts):
    part, tokens = parts[0].shape
    padded = -(-tokens // ROWS) * ROWS
    return pl.pallas_call(
        together_kernel,
        in_specs=[pl.BlockSpec(memory_space=pltpu.SMEM)]
        + [pl.BlockSpec(memory_space=pltpu.VMEM)] * 4,
        out_specs=pl.BlockSpec(memory_space=pltpu.VMEM),
        out_shape=jax.ShapeDtypeStruct((padded, 4 * part), bf16),
        compiler_params=pltpu.CompilerParams(vmem_limit_bytes=40 * 2**20),
        cost_estimate=pl.CostEstimate(
            flops=0, bytes_accessed=16 * tokens * part, transcendentals=0
        ),
        name="tokens_together",
    )(place, *parts)


def apart_kernel(place, *refs):
    parts, out_ref = refs[:4], refs[4]
    tokens = out_ref.shape[1] // 4
    for block in range(4):
        for distance in range(4):

            @pl.when((place[1] ^ block) == distance)
            def _():
                columns = slice(block * tokens, (block + 1) * tokens)
                out_ref[:, columns] = parts[distance][...].astype(f32)[:, :tokens]


def tokens_apart(place, tokens, parts):
    part = parts[0].shape[0]
    return pl.pallas_call(
        apart_kernel,
        in_specs=[pl.BlockSpec(memory_space=pltpu.SMEM)]
        + [pl.BlockSpec(memory_space=pltpu.VMEM)] * 4,
        out_specs=pl.BlockSpec(memory_space=pltpu.VMEM),
        out_shape=jax.ShapeDtypeStruct((part, 4 * tokens), f32),
        compiler_params=pltpu.CompilerParams(vmem_limit_bytes=40 * 2**20),
        cost_estimate=pl.CostEstimate(
            flops=0, bytes_accessed=4 * tokens * part * 6, transcendentals=0
        ),
        name="tokens_apart",
    )(place, *parts).T


def forward_kernel(*refs):
    resid_ref, params = refs[:2]
    weights = refs[2:6]
    h_ref, mixed_ref, out_ref, probs_ref, wide, gathered = refs[6:]
    rows = resid_ref.shape[0]
    images = rows // SEQ
    tokens = images * SEQ
    steps = pl.num_programs(0)

    @pl.when(pl.program_id(0) == 0)
    def _():
        for block in row_blocks(rows):
            normed, _ = norm_rows(resid_ref[block, :].astype(f32))
            h_ref[block, :] = (normed * params[0:1, :] + params[1:2, :]).astype(bf16)

    weight = side_weight(weights, STEPS, 0)
    for block in row_blocks(rows):
        mixed = dot(h_ref[block, :], weight).astype(bf16)
        mixed_ref[block, :] = mixed
        wide[block, :] = mixed.astype(f32)
    wide[rows:, :] = jnp.zeros((wide.shape[0] - rows, 384), f32)
    low_lane = lax.broadcasted_iota(jnp.int32, (1, 128), 1) < HEAD_DIM
    key_lane = lax.broadcasted_iota(jnp.int32, (1, KROWS), 1) < SEQ
    scale = HEAD_DIM ** (-0.5)
    for group in range(0, images, GROUPED):
        members = range(group, min(group + GROUPED, images))
        scores, values = [], []
        for image in members:
            start = image * SEQ
            block_a = wide[start : start + KROWS, 0:128]
            block_b = wide[start : start + KROWS, 128:256]
            block_c = wide[start : start + KROWS, 256:384]
            query_0 = jnp.where(low_lane, block_a[:QROWS] * scale, 0.0).astype(bf16)
            query_1 = jnp.where(low_lane, 0.0, block_b[:QROWS] * scale).astype(bf16)
            scores.append(dot(query_0, swap_halves(block_a).astype(bf16), ((1,), (1,))))
            scores.append(dot(query_1, swap_halves(block_c).astype(bf16), ((1,), (1,))))
            values += [block_b.astype(bf16), block_c.astype(bf16)]
        scores = [jnp.where(key_lane, score, -1e30) for score in scores]
        tops = [jnp.max(score, axis=1, keepdims=True) for score in scores]
        exponents = [jnp.exp(score - top) for score, top in zip(scores, tops)]
        totals = [jnp.sum(exponent, axis=1, keepdims=True) for exponent in exponents]
        probs = [(e * (1.0 / total)).astype(bf16) for e, total in zip(exponents, totals)]
        outs = [dot(prob, value) for prob, value in zip(probs, values)]
        for at, image in enumerate(members):
            start = image * SEQ
            probs_ref[0, image * 2] = probs[2 * at]
            probs_ref[0, image * 2 + 1] = probs[2 * at + 1]
            gathered[start : start + QROWS, :] = jnp.where(
                low_lane, outs[2 * at], outs[2 * at + 1]
            )
    gathered[tokens:, :] = jnp.zeros((gathered.shape[0] - tokens, 128), f32)
    out_ref[...] = gathered[0:rows, :].astype(bf16)


def attend_forward(resid, params, weights):
    rows, width = resid.shape
    images = rows // SEQ
    padded = -(-((images - 1) * SEQ + KROWS) // 16) * 16
    pair_probs = (STEPS, 2 * images, QROWS, KROWS)
    half_rows = weights[0].shape[0]
    return pl.pallas_call(
        forward_kernel,
        grid=(STEPS,),
        in_specs=[resident(resid), resident(params), *side_blocks(half_rows, 384, 1, STEPS)],
        out_specs=[
            pl.BlockSpec((rows, width), lambda i: (0, 0)),
            column_block(rows, 384),
            column_block(rows, 128),
            pl.BlockSpec((1, *pair_probs[1:]), lambda i: (i, 0, 0, 0)),
        ],
        out_shape=[
            jax.ShapeDtypeStruct((rows, width), bf16),
            jax.ShapeDtypeStruct((rows, STEPS * 384), bf16),
            jax.ShapeDtypeStruct((rows, STEPS * 128), bf16),
            jax.ShapeDtypeStruct(pair_probs, bf16),
        ],
        scratch_shapes=[pltpu.VMEM((padded, 384), f32), pltpu.VMEM((padded, 128), f32)],
        compiler_params=pltpu.CompilerParams(vmem_limit_bytes=48 * 2**20),
        cost_estimate=pl.CostEstimate(
            flops=20 * 10**9, bytes_accessed=rows * width * 20, transcendentals=10**6
        ),
        name="attend_forward",
    )(resid, params, *weights)


def backward_kernel(first, started, last, place, *refs):
    mixed_ref, probs_ref, grad_ref = refs[:3]
    weights, refs = refs[3:7], refs[7:]
    if started:
        before_ref, refs = refs[0], refs[1:]
    if last:
        middle_ref, resid_ref, params = refs[:3]
        out_ref, out_parts, sums_ref = refs[3], refs[4:8], refs[8]
        wide, grad_wide, gathered, total = refs[9:]
    else:
        out_ref, total = refs[:2]
        wide, grad_wide, gathered = refs[2:]
    rows = mixed_ref.shape[0]
    images = rows // SEQ
    tokens = images * SEQ
    wide[rows:, :] = jnp.zeros((wide.shape[0] - rows, 384), f32)
    wide[0:rows, :] = mixed_ref[...].astype(f32)
    grad_wide[0:rows, :] = grad_ref[...].astype(f32)
    low_lane = lax.broadcasted_iota(jnp.int32, (1, 128), 1) < HEAD_DIM
    query_row = lax.broadcasted_iota(jnp.int32, (QROWS, 128), 0) < SEQ
    scale = HEAD_DIM ** (-0.5)
    for group in range(0, images, GROUPED):
        members = range(group, min(group + GROUPED, images))
        grad_probs, grad_values, probs, swapped = [], [], [], []
        for image in members:
            start = image * SEQ
            block_a = wide[start : start + KROWS, 0:128]
            block_b = wide[start : start + KROWS, 128:256]
            block_c = wide[start : start + KROWS, 256:384]
            grad = jnp.where(query_row, grad_wide[start : start + QROWS, :], 0.0)
            grad_low = grad.astype(bf16)
            probs_0 = probs_ref[0, 2 * image]
            probs_1 = probs_ref[0, 2 * image + 1]
            probs += [probs_0, probs_1]
            part_0 = jnp.where(low_lane, grad, 0.0).astype(bf16)
            part_1 = jnp.where(low_lane, 0.0, grad).astype(bf16)
            grad_probs.append(dot(part_0, block_b.astype(bf16), ((1,), (1,))))
            grad_probs.append(dot(part_1, block_c.astype(bf16), ((1,), (1,))))
            grad_values.append(dot(probs_0, grad_low, ((0,), (0,))))
            grad_values.append(dot(probs_1, grad_low, ((0,), (0,))))
            swapped.append(
                [(swap_halves(block) * scale).astype(bf16) for block in (block_a, block_b, block_c)]
            )
        wide_probs = [prob.astype(f32) for prob in probs]
        inner = [
            jnp.sum(prob * grad, axis=1, keepdims=True)
            for prob, grad in zip(wide_probs, grad_probs)
        ]
        score_grads = [
            (prob * (grad - each)).astype(bf16)
            for prob, grad, each in zip(wide_probs, grad_probs, inner)
        ]
        for at, image in enumerate(members):
            start = image * SEQ
            swapped_a, swapped_b, swapped_c = swapped[at]
            score_0, score_1 = score_grads[2 * at : 2 * at + 2]
            grad_v0, grad_v1 = grad_values[2 * at : 2 * at + 2]
            grad_q0 = dot(score_0, swapped_a)
            grad_k0 = dot(score_0, swapped_a[:QROWS], ((0,), (0,)))
            grad_q1 = dot(score_1, swapped_c)
            grad_k1 = dot(score_1, swapped_b[:QROWS], ((0,), (0,)))
            block = slice(start, start + QROWS)
            gathered[block, 0:128] = jnp.where(low_lane, grad_q0, grad_k0[:QROWS])
            gathered[block, 128:256] = jnp.where(low_lane, grad_v0[:QROWS], grad_q1)
            gathered[block, 256:384] = jnp.where(low_lane, grad_k1[:QROWS], grad_v1[:QROWS])
    gathered[tokens:, :] = jnp.zeros((gathered.shape[0] - tokens, 384), f32)
    step = pl.program_id(0)
    weight = jnp.where(
        (first + step) % STEPS < STEPS // 2,
        jnp.concatenate([weights[0][...], weights[1][...]], axis=0),
        jnp.concatenate([weights[2][...], weights[3][...]], axis=0),
    )

    @pl.when(step == 0)
    def _():
        total[...] = before_ref[...] if started else jnp.zeros_like(total)

    for block in row_blocks(rows):
        grad_mixed = gathered[block, :].astype(bf16)
        out_ref[block, :] = grad_mixed
        total[block, :] += dot(grad_mixed, weight, ((1,), (1,)))

    if not last:
        return

    @pl.when(step == pl.num_programs(0) - 1)
    def _():
        gain = jnp.zeros((1, total.shape[1]), f32)
        shift = jnp.zeros((1, total.shape[1]), f32)
        for block in row_blocks(rows):
            grad_one = total[block, :]
            normed, scaled = norm_rows(resid_ref[block, :].astype(f32))
            gain += jnp.sum(grad_one * normed, axis=0, keepdims=True)
            shift += jnp.sum(grad_one, axis=0, keepdims=True)
            total[block, :] = middle_ref[block, :] + norm_backward(
                grad_one, normed, scaled, params[0:1, :]
            )
        sums_ref[0:1, :] = gain
        sums_ref[1:2, :] = shift
        for part_ref, part in zip(out_parts, split_parts(place[0], total[...].T)):
            part_ref[...] = part.astype(bf16)


def attend_backward(place, mixed, probs, grad_attended, weights, first, before, rest):
    rows, width = grad_attended.shape
    images = rows // SEQ
    steps = 2
    padded = -(-((images - 1) * SEQ + KROWS) // 16) * 16
    part = jax.ShapeDtypeStruct((width // 4, rows), bf16)
    sums = jax.ShapeDtypeStruct((2, width), f32)
    whole = jax.ShapeDtypeStruct((rows, width), f32)
    extra = [part] * 4 + [sums] if rest else [whole]
    scratch = [
        pltpu.VMEM((padded, 384), f32),
        pltpu.VMEM((padded, 128), f32),
        pltpu.VMEM((padded, 384), f32),
    ]
    if rest:
        scratch.append(pltpu.VMEM((rows, width), f32))
    weight_rows = weights[0].shape[0]
    side = STEPS // 2

    def pair(i):
        return (first + i) % STEPS

    return pl.pallas_call(
        lambda *refs: backward_kernel(first, bool(before), bool(rest), *refs),
        grid_spec=pltpu.PrefetchScalarGridSpec(
            num_scalar_prefetch=1,
            grid=(steps,),
            in_specs=[
                pl.BlockSpec((rows, 384), lambda i, *_: (0, pair(i))),
                pl.BlockSpec((1, *probs.shape[1:]), lambda i, *_: (pair(i), 0, 0, 0)),
                pl.BlockSpec((rows, 128), lambda i, *_: (0, pair(i))),
                *[pl.BlockSpec((weight_rows, 384), lambda i, *_: (0, pair(i) % side))] * 4,
                *[resident(each) for each in (*before, *rest)],
            ],
            out_specs=[
                column_block(rows, 384),
                *[pl.BlockSpec(each.shape, lambda i, *_: (0, 0)) for each in extra],
            ],
            scratch_shapes=scratch,
        ),
        out_shape=[jax.ShapeDtypeStruct((rows, steps * 384), bf16), *extra],
        compiler_params=pltpu.CompilerParams(vmem_limit_bytes=48 * 2**20),
        cost_estimate=pl.CostEstimate(flops=10**6, bytes_accessed=10**5, transcendentals=0),
        name="attend_backward",
    )(place, mixed, probs, grad_attended, *weights, *before, *rest)


def block_kernel(place, *refs):
    resid_ref, attended_ref, grad_ref, params = refs[:4]
    expand, contract, proj = refs[4:8], refs[8:12], refs[12:16]
    out_parts = refs[16:20]
    h_ref, hidden_ref, pre_ref, middle_ref, attended_grad_ref, sums_ref = refs[20:26]
    output, grad_two = refs[26:]
    middle = middle_ref
    rows = resid_ref.shape[0]
    step = pl.program_id(0)
    blocks = row_blocks(rows, 400)

    def proj_low():
        own = jnp.concatenate([proj[0][...], proj[1][...]], axis=1)
        return jnp.concatenate([own, jnp.concatenate([proj[2][...], proj[3][...]], axis=1)], axis=0)

    @pl.when(step == 0)
    def _():
        weight = proj_low()
        for block in blocks:
            value = resid_ref[block, :].astype(f32) + dot(attended_ref[block, :], weight)
            middle[block, :] = value
            output[block, :] = value
            grad_two[block, :] = jnp.zeros_like(value)
            normed, _ = norm_rows(value)
            h_ref[block, :] = (normed * params[2:3, :] + params[3:4, :]).astype(bf16)

    own_side = step < pl.num_programs(0) // 2

    def expand_side(own, other):
        upper = jnp.concatenate([own[at : at + WIDE, :] for at in range(0, CHUNK, WIDE)], axis=1)
        lower = jnp.concatenate([other[at : at + WIDE, :] for at in range(0, CHUNK, WIDE)], axis=1)
        return jnp.concatenate([upper, lower], axis=0)

    expand_low = jnp.where(
        own_side, expand_side(expand[0], expand[1]), expand_side(expand[2], expand[3])
    )
    contract_low = jnp.where(
        own_side,
        jnp.concatenate([contract[0][...], contract[1][...]], axis=1),
        jnp.concatenate([contract[2][...], contract[3][...]], axis=1),
    )

    def products(block):
        return (
            dot(h_ref[block, :], expand_low),
            dot(grad_ref[block, :], contract_low, ((1,), (1,))),
        )

    ahead = products(blocks[0])
    for at, block in enumerate(blocks):
        before, grad_hidden = ahead
        if at + 1 < len(blocks):
            ahead = products(blocks[at + 1])
        value, slope = gelu_and_slope(before)
        hidden = value.astype(bf16)
        grad_pre = (grad_hidden * slope).astype(bf16)
        hidden_ref[block, :] = hidden
        pre_ref[block, :] = grad_pre
        output[block, :] += dot(hidden, contract_low)
        grad_two[block, :] += dot(grad_pre, expand_low, ((1,), (1,)))

    @pl.when(step == pl.num_programs(0) - 1)
    def _():
        weight = proj_low()
        gain = jnp.zeros((1, middle.shape[1]), f32)
        shift = jnp.zeros((1, middle.shape[1]), f32)
        for block in blocks:
            grad = grad_two[block, :]
            normed, scaled = norm_rows(middle[block, :])
            gain += jnp.sum(grad * normed, axis=0, keepdims=True)
            shift += jnp.sum(grad, axis=0, keepdims=True)
            grad_middle = grad_ref[block, :].astype(f32) + norm_backward(
                grad, normed, scaled, params[2:3, :]
            )
            middle_ref[block, :] = grad_middle
            attended_grad_ref[block, :] = dot(
                grad_middle.astype(bf16), weight, ((1,), (1,))
            ).astype(bf16)
        sums_ref[0:1, :] = gain
        sums_ref[1:2, :] = shift
        for part_ref, part in zip(out_parts, split_parts(place[0], output[...].T)):
            part_ref[...] = part.astype(bf16)


def chunk_blocks(first, steps):
    def own(i, *_):
        return (first + jnp.minimum(i, steps // 2 - 1), 0)

    def other(i, *_):
        return (first + jnp.maximum(i - steps // 2, 0), 0)

    return [pl.BlockSpec((CHUNK, WIDE), own)] * 2 + [pl.BlockSpec((CHUNK, WIDE), other)] * 2


def block_middle(place, resid, attended, grad, params, weights):
    rows, width = resid.shape
    ff = 2 * MLP_ROWS
    chunk = CHUNK
    steps = ff // CHUNK
    part = jax.ShapeDtypeStruct((width // 4, rows), bf16)
    narrow = jax.ShapeDtypeStruct((rows, width), bf16)
    broad = jax.ShapeDtypeStruct((rows, ff), bf16)
    wide = jax.ShapeDtypeStruct((rows, width), f32)
    sums = jax.ShapeDtypeStruct((2, width), f32)

    def fixed(shape):
        return pl.BlockSpec(shape.shape, lambda i, *_: (0, 0), pipeline_mode=pl.Buffered(1))

    return pl.pallas_call(
        block_kernel,
        grid_spec=pltpu.PrefetchScalarGridSpec(
            num_scalar_prefetch=1,
            grid=(steps,),
            in_specs=[
                *[resident(each) for each in (resid, attended, grad, params)],
                *chunk_blocks(0, steps),
                *chunk_blocks(steps // 2, steps),
                *[
                    pl.BlockSpec(
                        (WIDE, WIDE),
                        lambda i, *_: (2 * MLP_ROWS // WIDE, 0),
                        pipeline_mode=pl.Buffered(1),
                    )
                ]
                * 4,
            ],
            out_specs=[
                *[fixed(part)] * 4,
                fixed(narrow),
                column_block(rows, chunk),
                column_block(rows, chunk),
                fixed(wide),
                fixed(narrow),
                fixed(sums),
            ],
            scratch_shapes=[pltpu.VMEM((rows, width), f32)] * 2,
        ),
        out_shape=[*[part] * 4, narrow, broad, broad, wide, narrow, sums],
        compiler_params=pltpu.CompilerParams(vmem_limit_bytes=56 * 2**20),
        cost_estimate=pl.CostEstimate(
            flops=2 * rows * width * (4 * ff + 2 * width),
            bytes_accessed=rows * ff * 8,
            transcendentals=2 * rows * ff,
        ),
        name="block_middle",
    )(place, resid, attended, grad, params, *weights, *weights, *weights)


def adamw_kernel(first_block, place, weight, first, second, here, there, *outs):
    block = pl.program_id(0) + first_block
    mine = jnp.where(block // 2 == place[2], here[0].astype(f32), there[0].astype(f32))
    results = adamw_update(
        weight[...], mine, first[...], second[...], rate_matrix, decay_matrix
    )
    for out, result in zip(outs, results):
        out[...] = result


def adamw_blocks(place, weight, first, second, here, there, unit, first_block):
    rows, width = weight.shape
    if rows == WIDE:
        piece = pl.BlockSpec((WIDE, WIDE), lambda i, *_: (0, i))
    else:
        piece = pl.BlockSpec((WIDE, WIDE), lambda i, *_: (i, 0))
    part = pl.BlockSpec((1, WIDE, WIDE), lambda i, *_: (unit, (i + first_block) % 2, 0))
    return pl.pallas_call(
        lambda *refs: adamw_kernel(first_block, *refs),
        grid_spec=pltpu.PrefetchScalarGridSpec(
            num_scalar_prefetch=1,
            grid=(rows * width // WIDE**2,),
            in_specs=[piece, piece, piece, part, part],
            out_specs=[piece] * 3,
        ),
        out_shape=[jax.ShapeDtypeStruct((rows, width), f32)] * 3,
        compiler_params=pltpu.CompilerParams(vmem_limit_bytes=40 * 2**20),
        cost_estimate=pl.CostEstimate(
            flops=20 * rows * width, bytes_accessed=28 * rows * width, transcendentals=0
        ),
        name="adamw_blocks",
    )(place, weight, first, second, here, there)


def local(
    tokens_in,
    out_grad,
    qkv_weight,
    proj_weight,
    expand_weight,
    contract_weight,
    norm_params,
    qkv_first,
    qkv_second,
    proj_first,
    proj_second,
    expand_first,
    expand_second,
    contract_first,
    contract_second,
    norm_first,
    norm_second,
):
    row = lax.axis_index("row")
    col = lax.axis_index("col")
    dp = lax.axis_index("dp")
    n_dp = lax.axis_size("dp")
    me = 2 * row + col
    place = jnp.stack([col, me, dp % 2, dp // 2]).astype(jnp.int32)
    tokens = tokens_in.shape[0] // 4
    part = tokens_in.shape[1]

    def swap(array, distance):
        if distance == 0:
            return array
        return lax.ppermute(array, GROUP, [(i, i ^ distance) for i in range(4)])

    def swap_dp(array, distance):
        return lax.ppermute(array, "dp", [(i, i ^ distance) for i in range(n_dp)])

    def swap_row(array):
        return swap(array, 2)

    def swap_col(array):
        return swap(array, 1)

    def token_blocks(array):
        return [lax.dynamic_slice(array, ((me ^ d) * tokens, 0), (tokens, part)) for d in range(4)]

    def swap_all(blocks):
        return [swap(block, d) for d, block in enumerate(blocks)]

    def ordered(bit, mine, partner):
        return jnp.where(
            bit == 0,
            jnp.concatenate([mine, partner], axis=0),
            jnp.concatenate([partner, mine], axis=0),
        )

    def dp_part(mine, count):
        rows = mine.shape[0] // count
        return lax.dynamic_slice_in_dim(mine, (dp % count) * rows, rows)

    def all_blocks(mine, partner):
        return [mine, partner, swap_col(mine), swap_col(partner)]

    x, z = dp % 2, dp // 2
    z_low, z_high = z % 2, z // 2 % 2

    def stack(array):
        blocks = [array[..., at : at + WIDE] for at in range(0, array.shape[-1], WIDE)]
        return jnp.concatenate(blocks, axis=-2)

    resid_parts = swap_all(token_blocks(tokens_in))
    qkv_mine = qkv_weight.astype(bf16)
    qkv_got = swap_row(dp_part(qkv_mine, 2))
    rest_mine = jnp.concatenate(
        [stack(expand_weight), contract_weight, proj_weight], axis=0
    ).astype(bf16)
    params = [swap(norm_params, d) for d in range(4)]
    resid_parts, params, qkv_got, rest_got = lax.optimization_barrier(
        (resid_parts, params, qkv_got, dp_part(rest_mine, 4))
    )
    params = jnp.concatenate(
        [in_order(col, params[0], params[1]), in_order(col, params[2], params[3])], axis=1
    )
    qkv_next, rest_got = swap_dp(qkv_got, 1), swap_row(rest_got)
    resid = tokens_together(place, [each.T for each in resid_parts])
    qkv_next, rest_got, grad_blocks, resid = lax.optimization_barrier(
        (qkv_next, rest_got, token_blocks(out_grad), resid)
    )
    qkv_low = all_blocks(qkv_mine, ordered(x, qkv_got, qkv_next))
    rest_x, rest_z = swap_dp(rest_got, 1), swap_dp(rest_got, 2)
    grad_parts = swap_all(grad_blocks)
    rest_away = swap_col(rest_mine)
    h_one, mixed, attended, probs = attend_forward(resid, params, qkv_low)
    attended, rest_x, rest_z, grad_parts, rest_away = lax.optimization_barrier(
        (attended, rest_x, rest_z, grad_parts, rest_away)
    )
    cut = rest_got.shape[0] // 2
    rest_last = jnp.concatenate([swap_dp(rest_z[:cut], 1), swap_dp(rest_x[cut:], 2)], axis=0)
    rest_row = ordered(z_low, ordered(x, rest_got, rest_x), ordered(x, rest_z, rest_last))
    rest_low = [rest_mine, rest_row, rest_away, swap_col(rest_row)]
    grad_low = tokens_together(place, [each.T for each in grad_parts])
    outs = block_middle(place, resid, attended, grad_low, params, rest_low)
    output_parts = outs[:4]
    h_two, hidden, grad_pre, grad_middle, grad_attended, sums_two = outs[4:]

    def halves(array, axis):
        size = array.shape[axis] // 2
        return (
            lax.slice_in_dim(array, 0, size, axis=axis),
            lax.slice_in_dim(array, size, 2 * size, axis=axis),
        )

    def over_col(left, right, received):
        total = dot(left, right, ((0,), (0,))) + received.astype(f32)
        return total.astype(bf16)

    def split(array, bit):
        size = array.shape[1] // 2
        kept = lax.dynamic_slice_in_dim(array, bit * size, size, 1)
        return kept, lax.dynamic_slice_in_dim(array, (1 - bit) * size, size, 1)

    def add(kept, received):
        return (kept.astype(f32) + received.astype(f32)).astype(bf16)

    def join(bit, mine, partner):
        return jnp.where(
            bit == 0,
            jnp.concatenate([mine, partner], axis=1),
            jnp.concatenate([partner, mine], axis=1),
        )

    same_x = [[i for i in range(n_dp) if i % 2 == bit] for bit in range(2)]

    def norm_total(sums):
        parts = split_features(col, sums)
        return parts[0] + sum(swap(parts[d], d) for d in range(1, 4))


    hidden_own, hidden_other = halves(hidden, 1)
    pre_own, pre_other = halves(grad_pre, 1)
    attended_own, attended_other = halves(attended, 1)
    branch = grad_middle.astype(bf16)
    contract_got = swap_col(dot(hidden_other, grad_low, ((0,), (0,))).astype(bf16))
    expand_got = swap_col(dot(h_two, pre_other, ((0,), (0,))).astype(bf16))
    contract_sum = over_col(hidden_own, grad_low, contract_got)
    contract_kept, contract_away = halves(contract_sum, 1)
    contract_away, pre_own, branch = lax.optimization_barrier((contract_away, pre_own, branch))
    contract_got = swap_row(contract_away)
    proj_got = swap_col(dot(attended_other, branch, ((0,), (0,))).astype(bf16))
    expand_sum = over_col(h_two, pre_own, expand_got)
    expand_sum = stack(expand_sum.reshape(2, WIDE, expand_sum.shape[1]))
    expand_kept, expand_away = split(expand_sum, x)
    proj_kept, proj_away = halves(over_col(attended_own, branch, proj_got), 1)
    expand_away, proj_away, grad_attended = lax.optimization_barrier(
        (expand_away, proj_away, grad_attended)
    )
    expand_got = swap_dp(expand_away, 1)
    mixed_a, total = attend_backward(place, mixed, probs, grad_attended, qkv_low, 3, [], [])
    contract_got, expand_got, mixed_a, total = lax.optimization_barrier(
        (contract_got, expand_got, mixed_a, total)
    )
    contract_kept, contract_away = split(add(contract_kept, contract_got)[None], x)
    expand_kept, expand_away = add(expand_kept, expand_got)
    expand_away = jnp.concatenate([expand_away, proj_away], axis=0)
    contract_away, expand_away, total = lax.optimization_barrier(
        (contract_away, expand_away, total)
    )
    contract_got, expand_got = swap_dp(contract_away, 1), swap_row(expand_away)
    mixed_b, total = attend_backward(
        place, mixed, probs, grad_attended, qkv_low, 5, [total], []
    )
    contract_got, expand_got, mixed_b, total = lax.optimization_barrier(
        (contract_got, expand_got, mixed_b, total)
    )
    expand_got, proj_got = expand_got[: expand_kept.shape[0]], expand_got[expand_kept.shape[0] :]
    mlp_sum = jnp.concatenate(
        [add(contract_kept, contract_got), add(expand_kept, expand_got)[None]], axis=0
    )
    mlp_kept, mlp_away = split(mlp_sum, z_low)
    qkv_away = jnp.concatenate(
        [
            dot(h_one, mixed_a, ((0,), (0,))).astype(bf16),
            dot(h_one, mixed_b[:, :WIDE], ((0,), (0,))).astype(bf16),
        ],
        axis=1,
    )
    mlp_away, qkv_away, total, output_parts = lax.optimization_barrier(
        (mlp_away, qkv_away, total, output_parts)
    )
    mlp_got, qkv_got = swap_dp(mlp_away, 2), swap_col(qkv_away)
    output_parts = swap_all(output_parts)
    outs = attend_backward(
        place, mixed, probs, grad_attended, qkv_low, 1, [total], [grad_middle, resid, params]
    )
    mixed_c, input_parts, sums_one = outs[0], outs[1:5], outs[5]
    mlp_got, qkv_got, mixed_c, output_parts = lax.optimization_barrier(
        (mlp_got, qkv_got, mixed_c, output_parts)
    )
    output_tokens = tokens_apart(place, tokens, output_parts)
    if n_dp == 8:
        mlp_sum = add(mlp_kept, mlp_got)
        mlp_kept, mlp_away = split(mlp_sum, z_high)
        mlp_away, mixed_c = lax.optimization_barrier((mlp_away, mixed_c))
        mlp_sum = add(mlp_kept, swap_dp(mlp_away, 4))
        mlp_sum = join(z_high, mlp_sum, swap_dp(mlp_sum, 4))
        mlp_sum = join(z_low, mlp_sum, swap_dp(mlp_sum, 2))
    else:
        mlp_sum = lax.psum(mlp_sum, "dp", axis_index_groups=same_x)
    qkv_sum = jnp.concatenate(
        [dot(h_one, mixed_b[:, WIDE:], ((0,), (0,))), dot(h_one, mixed_c, ((0,), (0,)))], axis=1
    )
    qkv_kept, qkv_away = halves((qkv_sum + qkv_got.astype(f32)).astype(bf16), 0)
    norm_sum = norm_total(jnp.concatenate([sums_one, sums_two], axis=0))
    qkv_away, norm_sum = lax.optimization_barrier((qkv_away, norm_sum))
    qkv_got = swap_row(qkv_away)
    qkv_got, input_parts = lax.optimization_barrier((qkv_got, input_parts))
    both = jnp.concatenate([stack(add(qkv_kept, qkv_got)), add(proj_kept, proj_got)], axis=0)
    both_kept, both_away = split(both[None], x)
    both_got = swap_dp(both_away, 1)
    input_parts = swap_all(input_parts)
    if n_dp == 8:
        norm_got = swap_dp(norm_sum, 1)
        both_got, norm_got = lax.optimization_barrier((both_got, norm_got))
        both_sum, norm_sum = add(both_kept, both_got), norm_sum + norm_got
        size = both_sum.shape[1] // 4
        parts = [lax.dynamic_slice_in_dim(both_sum, (z ^ d) * size, size, 1) for d in range(4)]
        parts = [parts[0]] + [swap_dp(parts[d], 2 * d) for d in range(1, 4)]
        norm_got = swap_dp(norm_sum, 2)
        parts, norm_got, input_parts = lax.optimization_barrier((parts, norm_got, input_parts))
        mine, norm_sum = sum(each.astype(f32) for each in parts).astype(bf16), norm_sum + norm_got
        parts = [mine] + [swap_dp(mine, 2 * d) for d in range(1, 4)]
        norm_got = swap_dp(norm_sum, 4)
        parts, norm_got = lax.optimization_barrier((parts, norm_got))
        norm_sum = norm_sum + norm_got
        both_sum = join(z_high, join(z_low, *parts[:2]), join(z_low, *parts[2:]))
    else:
        norm_sum = lax.psum(norm_sum, "dp")
        both_sum = lax.psum(add(both_kept, both_got), "dp", axis_index_groups=same_x)
    mlp_sum = (mlp_sum, swap_dp(mlp_sum, 1))
    both_next = swap_dp(both_sum, 1)
    input_grad = tokens_apart(place, tokens, input_parts)

    def adamw(weight, first, second, gradient, unit, block):
        return tuple(adamw_blocks(place, weight, first, second, *gradient, unit, block))

    expand_new = adamw(expand_weight, expand_first, expand_second, mlp_sum, 1, 0)
    contract_new = adamw(contract_weight, contract_first, contract_second, mlp_sum, 0, 0)
    both_next, expand_new, contract_new = lax.optimization_barrier(
        (both_next, expand_new, contract_new)
    )
    both_sum = (both_sum, both_next)
    qkv_new = adamw(qkv_weight, qkv_first, qkv_second, both_sum, 0, 0)
    proj_new = adamw(proj_weight, proj_first, proj_second, both_sum, 0, 3)
    norm_new = adamw_update(norm_params, norm_sum, norm_first, norm_second, rate_norm, 0.0)
    results = (output_tokens, input_grad, *qkv_new, *proj_new, *expand_new, *contract_new)
    return results + norm_new


def solution(mesh):
    tokens = P("dp", ("row", "col"))
    one = P("row", "col")
    two = P("col", "row")
    norm = P(None, ("row", "col"))
    in_specs = (tokens, tokens, one, two, one, two, norm)
    in_specs += (one, one, two, two, one, one, two, two, norm, norm)
    out_specs = (tokens, tokens) + (one,) * 3 + (two,) * 3 + (one,) * 3 + (two,) * 3 + (norm,) * 3
    return jax.shard_map(local, mesh=mesh, in_specs=in_specs, out_specs=out_specs, check_vma=False)
```
